128 devices in a mesh: section: 2 (over x_hi), dp: 64 (over y, x_lo, z, core).
Axes of the slice: x: 4 (x_hi: 2, x_lo: 2; x = x_hi * 2 + x_lo), y: 4, z: 4, core: 2. Of those that a mesh axis runs over, the one named last changes fastest.
Arguments:
- inputs: bfloat16 [2, 8192, 960], P(None, 'dp'), may hold values from -40 to 40
- segment_ids: int32 [2, 8192], P(None, 'dp'), may hold values from 0 to 127, never falling along the last dimension, each value on 1 to 128 neighbouring positions
- qkv_weight: bfloat16 [2, 960, 1600], P('section', 'dp'), may hold values from -0.1875 to 0.1875
- out_weight: bfloat16 [2, 960, 960], P('section', 'dp'), may hold values from -0.75 to 0.75
- gate_up_weight: bfloat16 [2, 960, 5120], P('section', 'dp'), may hold values from -0.1875 to 0.1875
- down_weight: bfloat16 [2, 2560, 960], P('section', 'dp'), may hold values from -0.125 to 0.125
- norm_gains: bfloat16 [2, 960, 2], P('section', 'dp'), may hold values from 0.099609375 to 1.8984375
- cotangent: bfloat16 [2, 8192, 960], P(None, 'dp'), may hold values from -6 to 6
Outputs:
- section_outputs: bfloat16 [2, 2, 8192, 960], P('section', None, 'dp')
- section_input_grads: bfloat16 [2, 2, 8192, 960], P('section', None, 'dp')
- qkv_grad: float32 [2, 960, 1600], P('section', 'dp')
- out_grad: float32 [2, 960, 960], P('section', 'dp')
- gate_up_grad: float32 [2, 960, 5120], P('section', 'dp')
- down_grad: float32 [2, 2560, 960], P('section', 'dp')
- gains_grad: float32 [2, 960, 2], P('section', 'dp')
The draws below stay inside these ranges and needn't reach their ends.
Inputs may be any that keep to these rules, and one draw needn't show every extreme that they name: `segment_ids`: within each micro-batch the document numbers never fall along the tokens, and each number names 1 to 128 tokens in a row.
All inputs are finite; a program needn't handle non-finite values.
Results may differ from the reference program's by a relative error of at most 0.02.
Values may be sent and summed in bfloat16 or wider, within the bound.
No kernel may reach another device: no remote copies, remote signals or barrier semaphores. Data moves between devices by JAX's collectives and lax.ppermute only.
A program may use at most 256 MiB of HBM per device.

```python
import math
import jax
import jax.numpy as jnp
import numpy as np
from jax import lax

D = 960
H = 15
KV = 5
HD = 64
FF = 2560
SEQ = 128
MB = 2
TOKENS = 8192
DOCS = 128
N_DP = 64


def draw_inputs(key, part):
    key = jax.random.fold_in(key, 7)
    values_key, row_key, column_key = jax.random.split(key, 3)
    values_base = jax.random.truncated_normal(values_key, -4.0, 4.0, (MB, TOKENS, D), jnp.float32)
    row_scale = jnp.exp(jax.random.uniform(row_key, (MB, TOKENS, 1), jnp.float32, -1.15, 1.15))
    column_scale = jnp.exp(jax.random.uniform(column_key, (1, 1, D), jnp.float32, -1.15, 1.15))
    return (values_base * row_scale * column_scale).astype(jnp.bfloat16)


def levels(own_key, extent, shards, smallest, largest):
    def one(dim, parts):
        heights = jax.random.uniform(jax.random.fold_in(jax.random.fold_in(own_key, 6), dim), (parts,), jnp.float32, smallest / len(shards), largest / len(shards))
        return jnp.repeat(jnp.exp(heights), extent[dim] // parts).reshape((-1,) + (1,) * (len(extent) - dim - 1))

    level = one(*shards[0])
    for cut in shards[1:]:
        level = level * one(*cut)
    return level


def profile(count, total, most, lean):
    weights = [(1 << 20) // math.isqrt(standing ** lean) + 1 for standing in range(2, count + 1)]
    surplus, given = total - most - (count - 1), [1] * (count - 1)
    while surplus > 0:
        candidates = [i for i in range(count - 1) if given[i] < most]
        whole, remaining = sum([weights[i] for i in candidates]), surplus
        for i in candidates:
            extra = min(most - given[i], max(1, remaining * weights[i] // whole), surplus)
            given[i] = given[i] + extra
            surplus = surplus - extra
    return np.array([most] + given)


def uneven(own_key, number_of, total, reach, slope):
    if number_of == 2:
        one = jax.random.randint(own_key, (), max(1, total - reach), min(reach, total - 1) + 1)
        return jnp.stack([one, total - one])
    sizes = jnp.asarray(profile(number_of, total, reach, slope), jnp.int32)
    couples = (number_of - 1) // 2
    donor, receiver = sizes[1:1 + 2 * couples:2], sizes[2:2 + 2 * couples:2]
    room = jnp.minimum(donor - 1, reach - receiver)
    moved = jax.random.randint(jax.random.fold_in(own_key, 1), (couples,), 0, 1 << 20) % (room + 1)
    sizes = sizes.at[1:1 + 2 * couples:2].set(donor - moved).at[2:2 + 2 * couples:2].set(receiver + moved)
    return sizes[jax.random.permutation(jax.random.fold_in(own_key, 2), number_of)]


def normal_values(own_key, dims, deviation, most, shards=(), kind=jnp.bfloat16):
    loudness = levels(own_key, dims, shards, -0.22, 0.18) if shards else 1.0
    values = jax.random.normal(own_key, dims, jnp.float32) * deviation * loudness
    return jnp.minimum(jnp.maximum(values, -most), most).astype(kind)


def setup_inputs(seed: int = 0) -> dict:
    key_of = jax.random.split(jax.random.key(seed), 9)
    return {
        "inputs": draw_inputs(jax.random.fold_in(key_of[8], 71), 0),
        "segment_ids": jax.vmap(lambda own: jnp.searchsorted(jnp.cumsum(uneven(own, DOCS, TOKENS, SEQ, 1)), jnp.arange(TOKENS), side="right"))(jax.random.split(key_of[1], MB)).reshape((MB, TOKENS)).astype(jnp.int32),
        "qkv_weight": normal_values(key_of[2], (2, D, D + 2 * KV * HD), D ** -0.5, 0.1875, ((0, 2), (1, 64))),
        "out_weight": normal_values(key_of[3], (2, D, D), (D // 16) ** -0.5, 0.75, ((0, 2), (1, 64))),
        "gate_up_weight": normal_values(key_of[4], (2, D, 2 * FF), D ** -0.5, 0.1875, ((0, 2), (1, 64))),
        "down_weight": normal_values(key_of[5], (2, FF, D), FF ** -0.5, 0.125, ((0, 2), (1, 64))),
        "norm_gains": jnp.clip(1.0 + 0.18 * jax.random.normal(key_of[6], (2, D, 2), jnp.float32), 0.099609375, 1.8984375).astype(jnp.bfloat16),
        "cotangent": normal_values(key_of[7], (MB, TOKENS, D), 1.0, 6.0, ((1, 64),)),
    }


EPSILON = 1e-05
ROPE_BASE = 100000.0

@jax.custom_vjp
def low(v):
    return lax.optimization_barrier(v.astype(jnp.bfloat16)).astype(jnp.float32)

@jax.custom_vjp
def low_back(v):
    return v

def low_keep(v):
    return (low(v), None)

def low_pass(kept, grad):
    return (grad,)

def back_keep(v):
    return (v, None)

def back_low(kept, grad):
    return (low(grad),)
low.defvjp(low_keep, low_pass)
low_back.defvjp(back_keep, back_low)

def rope_tables(length):
    position = jnp.arange(length, dtype=jnp.float32)[:, None]
    frequency = ROPE_BASE ** (-jnp.arange(0, HD, 2, dtype=jnp.float32) / HD)
    angle = position * frequency[None, :]
    return (jnp.cos(angle), jnp.sin(angle))

def rotate(vector, cosine_table, sine_table):
    halfway = vector.shape[-1] // 2
    first_half = vector[..., :halfway]
    second_half = vector[..., halfway:]
    cosine = cosine_table[:, None, :]
    sine_part = sine_table[:, None, :]
    return jnp.concatenate([first_half * cosine - second_half * sine_part, second_half * cosine + first_half * sine_part], -1)

def normalize(vector, gain):
    return vector * lax.rsqrt(lax.optimization_barrier(jnp.mean(vector * vector, axis=-1, keepdims=True)) + EPSILON) * gain

def layer(stream, seg_row, qkv_mat, out_mat, gate_up_mat, down_mat, gain_pair):
    highest = lax.Precision.HIGHEST
    length = stream.shape[0]
    cosine_table, sine_table = rope_tables(length)
    normed = low(normalize(stream, gain_pair[:, 0]))
    projected = jnp.dot(normed, qkv_mat, precision=highest)
    queries = low_back(projected[:, :D].reshape(length, H, HD))
    queries = low(low_back(rotate(queries, cosine_table, sine_table))).reshape(length, KV, H // KV, HD)
    keys_rot = low_back(projected[:, D:D + KV * HD].reshape(length, KV, HD))
    keys_rot = low(low_back(rotate(keys_rot, cosine_table, sine_table)))
    values = low(low_back(projected[:, D + KV * HD:].reshape(length, KV, HD)))
    scores = low_back(jnp.einsum('qkgd,tkd->kgqt', queries, keys_rot, precision=highest) * HD ** (-0.5))
    positions = jnp.arange(length)
    allowed = (seg_row[:, None] == seg_row[None, :]) & (positions[:, None] >= positions[None, :])
    scores = jnp.where(allowed, scores, -1000000000.0)
    row_max = lax.optimization_barrier(jnp.max(scores, axis=-1, keepdims=True))
    exp_scores = jnp.exp(scores - row_max)
    attn_probs = low(exp_scores / lax.optimization_barrier(jnp.sum(exp_scores, axis=-1, keepdims=True)))
    attended = jnp.einsum('kgqt,tkd->qkgd', attn_probs, values, precision=highest).reshape(length, D)
    attended = low(low_back(attended))
    middle = stream + low_back(jnp.dot(attended, out_mat, precision=highest))
    hidden_two = low(normalize(middle, gain_pair[:, 1]))
    gate_up = low_back(jnp.dot(hidden_two, gate_up_mat, precision=highest))
    activated = low(jax.nn.silu(gate_up[:, :FF]) * gate_up[:, FF:])
    return middle + low_back(jnp.dot(activated, down_mat, precision=highest))

def reference(inputs, segment_ids, qkv_weight, out_weight, gate_up_weight, down_weight, norm_gains, cotangent):
    count = MB * N_DP
    streams = inputs.astype(jnp.float32).reshape(count, SEQ, D)
    seg_rows = segment_ids.reshape(count, SEQ)
    shifts = jnp.zeros_like(streams)
    params = (qkv_weight.astype(jnp.float32), out_weight.astype(jnp.float32), gate_up_weight.astype(jnp.float32), down_weight.astype(jnp.float32), norm_gains.astype(jnp.float32))

    def forward(stream_all, shift_all, param_set):

        def single(item):
            stream, shift_in, seg_row = item
            first_set = [weight[0] for weight in param_set]
            second_set = [weight[1] for weight in param_set]
            hidden = low_back(low(layer(stream, seg_row, *first_set))) + shift_in
            final = low(layer(hidden, seg_row, *second_set))
            return (hidden, final)
        return lax.map(jax.checkpoint(single), (stream_all, shift_all, seg_rows))
    (hidden_all, final_all), backward = jax.vjp(forward, streams, shifts, params)
    grad_in, grad_mid, grad_params = backward((jnp.zeros_like(hidden_all), cotangent.astype(jnp.float32).reshape(count, SEQ, D)))
    section_outputs = jnp.stack([hidden_all, final_all]).reshape(2, MB, TOKENS, D).astype(jnp.bfloat16)
    section_input_grads = jnp.stack([grad_in, grad_mid]).reshape(2, MB, TOKENS, D).astype(jnp.bfloat16)
    return (section_outputs, section_input_grads, grad_params[0], grad_params[1], grad_params[2], grad_params[3], grad_params[4])
```

```python
import jax
import jax.numpy as jnp
from jax import lax
from jax.experimental import pallas as pl
from jax.experimental.pallas import tpu as pltpu
from jax.sharding import PartitionSpec as P

D = 960
H = 15
KV = 5
HD = 64
FF = 2560
QKV = D + 2 * KV * HD
N_DP = 64
ROWS = D // N_DP
PAD = 16
FROWS = FF // N_DP
LANES = 128
QKV_PAD = 1664
OUT_PAD = 1024

BF16 = jnp.bfloat16
F32 = jnp.float32


def place(y, x, z, core):
    return ((y % 4 * 2 + x % 2) * 4 + z % 4) * 2 + core % 2


def route(kind, step):
    pairs = []
    for source in range(N_DP):
        y, x, z, core = source // 16, source // 8 % 2, source // 2 % 4, source % 2
        if kind == "core":
            target = place(y, x, z, core + 1)
        elif kind == "x":
            target = place(y, x + 1, z, core)
        elif (kind == "wide") == (core == 0):
            target = place(y, x, z + step, core)
        else:
            target = place(y + step, x, z, core)
        pairs.append((source, target))
    return pairs


def send(block, kind, step=1):
    return lax.ppermute(block, "dp", route(kind, step))


def total(*terms):
    result = terms[0].astype(F32)
    for term in terms[1:]:
        result = result + term.astype(F32)
    return result


def ring_scatter(blocks, kind):
    half = blocks.shape[1] // 2
    from_left = send(blocks[2, :half], kind, 1)
    from_right = send(blocks[2, half:], kind, -1)
    onward = jnp.concatenate([total(blocks[1, :half], from_left).astype(BF16), blocks[1, half:]], 0)
    back = jnp.concatenate([blocks[3, :half], total(blocks[3, half:], from_right).astype(BF16)], 0)
    from_left = send(onward, kind, 1)
    from_right = send(back, kind, -1)
    return total(blocks[0], from_left, from_right).astype(BF16)


def scatter_sum(for_other, for_own):
    blocks = total(for_own, send(for_other, "core")).astype(BF16)
    blocks = ring_scatter(blocks.reshape((4, 8) + blocks.shape[1:]), "wide")
    blocks = ring_scatter(blocks.reshape((4, 2) + blocks.shape[1:]), "narrow")
    return total(blocks[0], send(blocks[1], "x"))


def ring_gather(block, kind):
    half = block.shape[0] // 2
    from_left = send(block, kind, 1)
    from_right = send(block, kind, -1)
    far_left = send(from_left[:half], kind, 1)
    far_right = send(from_right[half:], kind, -1)
    return [block, from_right, far_left, far_right, from_left]


def gather_rows(shard):
    block = jnp.stack([shard, send(shard, "x")], 0)
    block = jnp.concatenate(ring_gather(block, "narrow"), 0)
    pieces = ring_gather(block, "wide")
    others = [send(piece, "core") for piece in pieces]
    return jnp.concatenate(pieces + others, 0)


def block_order():
    index = lax.axis_index("dp")
    y, x, z, core = index // 16, index // 8 % 2, index // 2 % 4, index % 2
    position = jnp.arange(N_DP)
    core_step, wide, narrow, x_step = position // 32, position // 8 % 4, position // 2 % 4, position % 2
    core_there = (core + core_step) % 2
    z_step = jnp.where(core_there == 0, wide, narrow)
    y_step = jnp.where(core_there == 0, narrow, wide)
    return (((y + y_step) % 4 * 2 + (x + x_step) % 2) * 4 + (z + z_step) % 4) * 2 + core_there


def placement(order):
    column = jnp.arange(N_DP * PAD)
    inner = column % PAD
    row = jnp.where(inner < ROWS, jnp.repeat(order, PAD) * ROWS + inner, -1)
    return (jnp.arange(D)[:, None] == row[None, :]).astype(BF16)


def reorder_kernel(scatter, order_ref, blocks_ref, out_ref):
    def one(step, carry):
        there = order_ref[step]
        if scatter:
            out_ref[there] = blocks_ref[step]
        else:
            out_ref[step] = blocks_ref[there]
        return carry

    lax.fori_loop(0, N_DP, one, 0)


def reorder(blocks, order, scatter):
    return pl.pallas_call(
        lambda *refs: reorder_kernel(scatter, *refs),
        out_shape=jax.ShapeDtypeStruct(blocks.shape, blocks.dtype),
        in_specs=[
            pl.BlockSpec(memory_space=pltpu.SMEM),
            pl.BlockSpec(memory_space=pltpu.VMEM),
        ],
        out_specs=pl.BlockSpec(memory_space=pltpu.VMEM),
        compiler_params=pltpu.CompilerParams(vmem_limit_bytes=32 * 1024 * 1024),
    )(order, blocks)


def dot(left, right):
    return jnp.dot(left, right, preferred_element_type=F32)


def dot_t(left, right):
    return lax.dot_general(left, right, (((1,), (1,)), ((), ())), preferred_element_type=F32)


EPSILON = 1e-05
ROPE_BASE = 100000.0


def shifted(block, axis, distance):
    devices = range(lax.axis_size(axis))
    pairs = [(i - distance, i) for i in devices if i - distance in devices]
    return lax.ppermute(block, axis, pairs)


def rope_tables(length):
    position = jnp.arange(length, dtype=jnp.float32)[:, None]
    frequency = ROPE_BASE ** (-jnp.arange(0, HD, 2, dtype=jnp.float32) / HD)
    angle = position * frequency[None, :]
    return (jnp.cos(angle), jnp.sin(angle))


def rotate(vector, cosine_table, sine_table):
    halfway = vector.shape[-1] // 2
    first_half = vector[..., :halfway]
    second_half = vector[..., halfway:]
    cosine = cosine_table[:, None, :]
    sine_part = sine_table[:, None, :]
    return jnp.concatenate(
        [
            first_half * cosine - second_half * sine_part,
            second_half * cosine + first_half * sine_part,
        ],
        -1,
    )


def unrotate(vector, cosine_table, sine_table):
    halfway = vector.shape[-1] // 2
    first_half = vector[..., :halfway]
    second_half = vector[..., halfway:]
    cosine = cosine_table[:, None, :]
    sine_part = sine_table[:, None, :]
    return jnp.concatenate(
        [
            first_half * cosine + second_half * sine_part,
            second_half * cosine - first_half * sine_part,
        ],
        -1,
    )


def normalize(vector, gain):
    return vector * lax.rsqrt(jnp.mean(vector * vector, axis=-1, keepdims=True) + EPSILON) * gain


def swiglu(gate_part, up_part):
    return jax.nn.silu(gate_part) * up_part


def attention_scores(queries, keys_rot, allowed):
    scores = jnp.einsum(
        "qkgd,tkd->kgqt", queries, keys_rot, preferred_element_type=jnp.float32
    ) * HD ** (-0.5)
    return jnp.where(allowed, scores, -1000000000.0)


def layer_forward(layer_in, seg_row, weights):
    attn_mat, gate_up_mat, down_mat, gains_full, spread = weights
    length = layer_in.shape[0]
    cosine_table, sine_table = rope_tables(length)
    stream = layer_in.astype(F32)
    hidden_one = normalize(stream, gains_full[0]).astype(BF16)
    hidden_one = dot(hidden_one, spread).astype(BF16)
    projected = dot(hidden_one, attn_mat[:, :QKV_PAD])[:, :QKV]
    queries = rotate(projected[:, :D].reshape(length, H, HD), cosine_table, sine_table)
    queries = queries.astype(BF16).reshape(length, KV, H // KV, HD)
    keys_rot = rotate(
        projected[:, D : D + KV * HD].reshape(length, KV, HD), cosine_table, sine_table
    ).astype(BF16)
    values = projected[:, D + KV * HD :].reshape(length, KV, HD).astype(BF16)
    positions = jnp.arange(length)
    allowed = (seg_row[:, None] == seg_row[None, :]) & (positions[:, None] >= positions[None, :])
    scores = attention_scores(queries, keys_rot, allowed)
    row_max = jnp.max(scores, axis=-1, keepdims=True)
    exp_scores = jnp.exp(scores - row_max)
    row_total = jnp.sum(exp_scores, axis=-1, keepdims=True)
    attn_probs = exp_scores / row_total
    log_total = row_max + jnp.log(row_total)
    attended = jnp.einsum(
        "kgqt,tkd->qkgd",
        attn_probs.astype(BF16),
        values,
        preferred_element_type=F32,
    )
    attended = dot(attended.reshape(length, D).astype(BF16), spread).astype(BF16)
    middle = stream + dot(attended, attn_mat[:, QKV_PAD : QKV_PAD + D])
    hidden_two = normalize(middle, gains_full[1]).astype(BF16)
    hidden_two = dot(hidden_two, spread).astype(BF16)
    gate_up = dot(hidden_two, gate_up_mat)
    activated = swiglu(gate_up[:, :FF], gate_up[:, FF:]).astype(BF16)
    layer_out = middle + dot(activated, down_mat)
    kept = (
        stream,
        hidden_one,
        queries,
        keys_rot,
        values,
        allowed,
        log_total,
        attended,
        middle,
        hidden_two,
        gate_up,
        activated,
    )
    return (kept, layer_out)


def layer_backward(kept, grad_out, weights):
    attn_mat, gate_up_mat, down_mat, gains_full, spread = weights
    (
        stream,
        hidden_one,
        queries,
        keys_rot,
        values,
        allowed,
        log_total,
        attended,
        middle,
        hidden_two,
        gate_up,
        activated,
    ) = kept
    length = stream.shape[0]
    cosine_table, sine_table = rope_tables(length)
    grad_down = grad_out.astype(BF16)
    grad_act = dot_t(grad_down, down_mat)
    unused, swiglu_back = jax.vjp(swiglu, gate_up[:, :FF], gate_up[:, FF:])
    grad_gate, grad_upper = swiglu_back(grad_act)
    grad_gate_up = jnp.concatenate([grad_gate, grad_upper], -1).astype(BF16)
    grad_two = dot_t(dot_t(grad_gate_up, gate_up_mat).astype(BF16), spread)
    unused, norm_back_two = jax.vjp(normalize, middle, gains_full[1])
    grad_norm_two, gain_two = norm_back_two(grad_two)
    grad_middle = grad_out + grad_norm_two
    grad_attn = grad_middle.astype(BF16)
    grad_mixed = dot_t(grad_attn, attn_mat[:, QKV_PAD : QKV_PAD + D]).astype(BF16)
    grad_mixed = dot_t(grad_mixed, spread).astype(BF16)
    grad_mixed = grad_mixed.reshape(length, KV, H // KV, HD)
    scores = attention_scores(queries, keys_rot, allowed)
    attn_probs = jnp.exp(scores - log_total)
    grad_probs = jnp.einsum(
        "qkgd,tkd->kgqt", grad_mixed, values, preferred_element_type=F32
    )
    grad_scores = attn_probs * (
        grad_probs - jnp.sum(grad_probs * attn_probs, axis=-1, keepdims=True)
    )
    grad_scores = grad_scores.astype(BF16)
    grad_queries = jnp.einsum(
        "kgqt,tkd->qkgd", grad_scores, keys_rot, preferred_element_type=F32
    ) * HD ** (-0.5)
    grad_keys = jnp.einsum(
        "kgqt,qkgd->tkd", grad_scores, queries, preferred_element_type=F32
    ) * HD ** (-0.5)
    grad_values = jnp.einsum(
        "kgqt,qkgd->tkd",
        attn_probs.astype(BF16),
        grad_mixed,
        preferred_element_type=F32,
    )
    grad_queries = grad_queries.astype(BF16).reshape(length, H, HD).astype(F32)
    grad_keys = grad_keys.astype(BF16).astype(F32)
    grad_q_pre = unrotate(grad_queries, cosine_table, sine_table).astype(BF16).reshape(length, D)
    grad_k_pre = (
        unrotate(grad_keys, cosine_table, sine_table).astype(BF16).reshape(length, KV * HD)
    )
    grad_v_pre = grad_values.astype(BF16).reshape(length, KV * HD)
    grad_proj = jnp.concatenate([grad_q_pre, grad_k_pre, grad_v_pre], -1)
    grad_one = dot_t(dot_t(grad_proj, attn_mat[:, :QKV]).astype(BF16), spread)
    unused, norm_back_one = jax.vjp(normalize, stream, gains_full[0])
    grad_norm_one, gain_one = norm_back_one(grad_one)
    grad_in = grad_middle + grad_norm_one
    pieces = (
        grad_proj,
        grad_attn,
        grad_gate_up,
        grad_down,
        jnp.stack([gain_one, gain_two], 0),
    )
    return (grad_in, pieces)


def contract(left_rows, right_rows):
    return lax.dot_general(
        left_rows, right_rows, (((0,), (0,)), ((), ())), preferred_element_type=F32
    ).astype(BF16)


def halves(left_rows, right_rows):
    own = contract(left_rows[:, : N_DP * PAD // 2], right_rows)
    other = contract(left_rows[:, N_DP * PAD // 2 :], right_rows)
    return (other, own)


def as_blocks(rows):
    return rows.reshape(N_DP // 2, -1, rows.shape[-1])


def per_device(
    inputs, segment_ids, qkv_weight, out_weight, gate_up_weight, down_weight, norm_gains, cotangent
):
    batches = inputs.shape[0]
    is_first = lax.axis_index("section") == 0
    order = block_order()
    spread = placement(order)
    attn_shard = jnp.concatenate(
        [
            qkv_weight[0],
            norm_gains[0],
            jnp.zeros((ROWS, QKV_PAD - QKV - 2), BF16),
            out_weight[0],
            jnp.zeros((ROWS, OUT_PAD - D), BF16),
        ],
        1,
    )
    attn_mat = gather_rows(jnp.pad(attn_shard, ((0, 1), (0, 0)))).reshape(N_DP * PAD, -1)
    gate_up_mat = gather_rows(jnp.pad(gate_up_weight[0], ((0, 1), (0, 0)))).reshape(N_DP * PAD, -1)
    down_mat = reorder(gather_rows(down_weight[0]), order, True).reshape(FF, D)
    gains_full = lax.dot_general(
        attn_mat[:, QKV : QKV + 2], spread, (((0,), (1,)), ((), ())), preferred_element_type=F32
    )
    weights = (attn_mat, gate_up_mat, down_mat, gains_full, spread)
    received = jnp.zeros(inputs.shape[1:], BF16)
    saved = []
    produced = []
    for turn in range(batches + 1):
        own_input = inputs[min(turn, batches - 1)]
        layer_in = jnp.where(is_first, own_input, received)
        seg_row = jnp.where(
            is_first, segment_ids[min(turn, batches - 1)], segment_ids[max(turn - 1, 0)]
        )
        kept, layer_out = layer_forward(layer_in, seg_row, weights)
        layer_out = layer_out.astype(BF16)
        saved.append(kept)
        produced.append(layer_out)
        if turn < batches:
            received = shifted(layer_out, "section", 1)
    section_outputs = jnp.stack(
        [
            jnp.where(is_first, produced[position], produced[position + 1])
            for position in range(batches)
        ]
    )[None]
    received = jnp.zeros(inputs.shape[1:], BF16)
    returned = []
    collected = []
    for turn in range(batches + 1):
        if turn < batches:
            own_grad = cotangent[turn]
        else:
            own_grad = jnp.zeros(inputs.shape[1:], BF16)
        grad_out = jnp.where(is_first, received, own_grad).astype(F32)
        kept = jax.tree.map(
            lambda for_first, for_second: jnp.where(is_first, for_first, for_second),
            saved[max(turn - 1, 0)],
            saved[min(turn + 1, batches)],
        )
        grad_in, pieces = layer_backward(kept, grad_out, weights)
        grad_in = grad_in.astype(BF16)
        returned.append(grad_in)
        collected.append(pieces)
        if turn < batches:
            received = shifted(grad_in, "section", -1)
    section_input_grads = jnp.stack(
        [
            jnp.where(is_first, returned[position + 1], returned[position])
            for position in range(batches)
        ]
    )[None]

    def lefts(member):
        return jnp.concatenate(
            [jnp.where(is_first, saved[b][member], saved[b + 1][member]) for b in range(batches)], 0
        )

    def rights(member):
        return jnp.concatenate(
            [
                jnp.where(is_first, collected[b + 1][member], collected[b][member])
                for b in range(batches)
            ],
            0,
        )

    down_blocks = contract(lefts(11), rights(3)).reshape(N_DP, FROWS, D)
    down_blocks = reorder(down_blocks, order, False)
    down_grad = scatter_sum(down_blocks[N_DP // 2 :], down_blocks[: N_DP // 2])
    other, own = halves(lefts(9), rights(2))
    gate_up_grad = scatter_sum(as_blocks(other), as_blocks(own))
    gain_sum = collected[0][4]
    for pieces in collected[1:]:
        gain_sum = gain_sum + pieces[4]
    gain_high = gain_sum.astype(BF16)
    gain_low = (gain_sum - gain_high.astype(F32)).astype(BF16)
    gain_rows = lax.dot_general(
        spread, jnp.stack([gain_high, gain_low]), (((0,), (2,)), ((), ())), preferred_element_type=F32
    )
    gain_rows = (gain_rows[:, 0] + gain_rows[:, 1]).astype(BF16)
    qkv_terms = halves(lefts(1), rights(0))
    out_terms = halves(lefts(7), rights(1))
    attn_terms = []
    middle_row = N_DP * PAD // 2
    for term, start in ((0, middle_row), (1, 0)):
        attn_terms.append(
            jnp.concatenate(
                [
                    qkv_terms[term],
                    gain_rows[start : start + middle_row],
                    jnp.zeros((middle_row, QKV_PAD - QKV - 2), BF16),
                    out_terms[term],
                    jnp.zeros((middle_row, OUT_PAD - D), BF16),
                ],
                1,
            )
        )
    attn_grad = scatter_sum(as_blocks(attn_terms[0]), as_blocks(attn_terms[1]))
    return (
        section_outputs,
        section_input_grads,
        attn_grad[None, :ROWS, :QKV],
        attn_grad[None, :ROWS, QKV_PAD : QKV_PAD + D],
        gate_up_grad[None, :ROWS],
        down_grad[None],
        attn_grad[None, :ROWS, QKV : QKV + 2],
    )


def solution(mesh):
    in_specs = (
        P(None, "dp", None),
        P(None, "dp"),
        P("section", "dp", None),
        P("section", "dp", None),
        P("section", "dp", None),
        P("section", "dp", None),
        P("section", "dp", None),
        P(None, "dp", None),
    )
    out_specs = (
        P("section", None, "dp", None),
        P("section", None, "dp", None),
        P("section", "dp", None),
        P("section", "dp", None),
        P("section", "dp", None),
        P("section", "dp", None),
        P("section", "dp", None),
    )
    return jax.shard_map(
        per_device, mesh=mesh, in_specs=in_specs, out_specs=out_specs, check_vma=False
    )
```

```python
import jax
import jax.numpy as jnp
from jax import lax
from jax.experimental import pallas as pl
from jax.experimental.pallas import tpu as pltpu
from jax.sharding import PartitionSpec as P

D = 960
H = 15
KV = 5
HD = 64
FF = 2560
QKV = D + 2 * KV * HD
N_DP = 64
ROWS = D // N_DP
PAD = 16
FROWS = FF // N_DP
LANES = 128
QKV_PAD = 1664
OUT_PAD = 1024

EPSILON = 1e-05
ROPE_BASE = 100000.0
BF16 = jnp.bfloat16
F32 = jnp.float32


def place(y, x, z, core):
    return ((y % 4 * 2 + x % 2) * 4 + z % 4) * 2 + core % 2


def route(kind, step):
    pairs = []
    for source in range(N_DP):
        y, x, z, core = source // 16, source // 8 % 2, source // 2 % 4, source % 2
        if kind == "core":
            target = place(y, x, z, core + 1)
        elif kind == "x":
            target = place(y, x + 1, z, core)
        elif (kind == "wide") == (core == 0):
            target = place(y, x, z + step, core)
        else:
            target = place(y + step, x, z, core)
        pairs.append((source, target))
    return pairs


def send(block, kind, step=1):
    return lax.ppermute(block, "dp", route(kind, step))


def total(*terms):
    result = terms[0].astype(F32)
    for term in terms[1:]:
        result = result + term.astype(F32)
    return result


def near_scatter(blocks):
    blocks = yield from ring_scatter(blocks, "narrow")
    (got,) = yield (send(blocks[1], "x"),)
    return total(blocks[0], got)


def ring_scatter(blocks, kind):
    blocks = blocks.reshape((4, blocks.shape[0] // 4) + blocks.shape[1:])
    half = blocks.shape[1] // 2
    left, right = yield (send(blocks[3, :half], kind, 1), send(blocks[3, half:], kind, -1))
    onward = jnp.concatenate([total(blocks[1, :half], left).astype(BF16), blocks[1, half:]], 0)
    back = jnp.concatenate([blocks[2, :half], total(blocks[2, half:], right).astype(BF16)], 0)
    left, right = yield (send(onward, kind, 1), send(back, kind, -1))
    return total(blocks[0], left, right).astype(BF16)


def far_scatter(for_other, for_own):
    (got,) = yield (send(for_other, "core"),)
    blocks = total(for_own(), got).astype(BF16)
    return (yield from ring_scatter(blocks, "wide"))


def down_scatter(for_other, for_own):
    blocks = yield from far_scatter(for_other, for_own)
    return (yield from near_scatter(blocks))


class Flow:
    def __init__(self, stages):
        self.stages = stages
        self.result = None
        self.pending = next(stages)

    def advance(self, arrived):
        try:
            self.pending = self.stages.send(arrived)
        except StopIteration as end:
            self.pending = ()
            self.result = end.value


def step(flows, value):
    flows = [flow for flow in flows if flow.result is None]
    arrived, value = lax.optimization_barrier((tuple(flow.pending for flow in flows), value))
    for flow, got in zip(flows, arrived):
        flow.advance(got)
    return value


def ring_gather(block, kind):
    half = block.shape[0] // 2
    from_left = send(block, kind, 1)
    from_right = send(block, kind, -1)
    far_left = send(from_left[:half], kind, 1)
    far_right = send(from_right[half:], kind, -1)
    sides = jnp.concatenate([from_right, from_left], 0)
    return [block, sides, jnp.concatenate([far_left, far_right], 0)]


def gather_near(shard):
    block = jnp.stack([shard, send(shard, "x")], 0)
    return jnp.concatenate(ring_gather(block, "narrow"), 0)


def gather_far(block):
    pieces = ring_gather(block, "wide")
    others = [send(piece, "core") for piece in pieces]
    return (pieces[2], jnp.concatenate(pieces + others, 0))


def after(value, earlier):
    return lax.optimization_barrier((value, earlier))[0]


def block_order():
    index = lax.axis_index("dp")
    y, x, z, core = index // 16, index // 8 % 2, index // 2 % 4, index % 2
    position = jnp.arange(N_DP)
    core_step, wide, narrow, x_step = position // 32, position // 8 % 4, position // 2 % 4, position % 2
    wide, narrow = wide ^ (wide // 2), narrow ^ (narrow // 2)
    core_there = (core + core_step) % 2
    z_step = jnp.where(core_there == 0, wide, narrow)
    y_step = jnp.where(core_there == 0, narrow, wide)
    return (((y + y_step) % 4 * 2 + (x + x_step) % 2) * 4 + (z + z_step) % 4) * 2 + core_there


def placement(order):
    column = jnp.arange(N_DP * PAD)
    inner = column % PAD
    row = jnp.where(inner < ROWS, jnp.repeat(order, PAD) * ROWS + inner, -1)
    return (jnp.arange(D)[:, None] == row[None, :]).astype(BF16)


def reorder_kernel(scatter, order_ref, blocks_ref, out_ref):
    def one(step, carry):
        there = order_ref[step]
        if scatter:
            out_ref[there] = blocks_ref[step]
        else:
            out_ref[step] = blocks_ref[there]
        return carry

    lax.fori_loop(0, N_DP, one, 0)


def reorder(blocks, order, scatter):
    return pl.pallas_call(
        lambda *refs: reorder_kernel(scatter, *refs),
        out_shape=jax.ShapeDtypeStruct(blocks.shape, blocks.dtype),
        in_specs=[
            pl.BlockSpec(memory_space=pltpu.SMEM),
            pl.BlockSpec(memory_space=pltpu.VMEM),
        ],
        out_specs=pl.BlockSpec(memory_space=pltpu.VMEM),
        compiler_params=pltpu.CompilerParams(vmem_limit_bytes=32 * 1024 * 1024),
    )(order, blocks)


def across(left, right):
    return lax.dot_general(left, right, (((0,), (0,)), ((), ())), preferred_element_type=F32)


VMEM_BYTES = 48 * 1024 * 1024


def down_kernel(place_ref, left_ref, right_ref, out_ref):
    step = pl.program_id(0)
    rows = across(left_ref[...], right_ref[...]).astype(BF16)
    count = rows.shape[0] // FROWS
    for block in range(count):
        out_ref[place_ref[step * count + block]] = rows[block * FROWS : (block + 1) * FROWS]


def down_sums(left, right, places):
    tokens = left.shape[0]
    width = 640
    return pl.pallas_call(
        down_kernel,
        grid=(FF // width,),
        out_shape=jax.ShapeDtypeStruct((N_DP, FROWS, D), BF16),
        in_specs=[
            pl.BlockSpec(memory_space=pltpu.SMEM),
            pl.BlockSpec((tokens, width), lambda i: (0, i)),
            pl.BlockSpec((tokens, D), lambda i: (0, 0)),
        ],
        out_specs=pl.BlockSpec((N_DP, FROWS, D), lambda i: (0, 0, 0)),
        compiler_params=pltpu.CompilerParams(vmem_limit_bytes=VMEM_BYTES),
        cost_estimate=pl.CostEstimate(
            flops=2 * tokens * FF * D, bytes_accessed=2 * FF * D, transcendentals=0
        ),
    )(places, left, right)


def gate_up_kernel(left_ref, gate_ref, up_ref, out_ref):
    left = left_ref[...]
    out_ref[:, :FF] = across(left, gate_ref[...]).astype(BF16)
    out_ref[:, FF:] = across(left, up_ref[...]).astype(BF16)


def gate_up_sums(left, gate, up, first):
    tokens = left.shape[0]
    columns = 2 * FF
    width = 128
    count = N_DP * PAD // 2 // width
    return pl.pallas_call(
        gate_up_kernel,
        grid=(count,),
        out_shape=jax.ShapeDtypeStruct((N_DP * PAD // 2, columns), BF16),
        in_specs=[
            pl.BlockSpec((tokens, width), lambda i: (0, i + first * count)),
            pl.BlockSpec((tokens, FF), lambda i: (0, 0)),
            pl.BlockSpec((tokens, FF), lambda i: (0, 0)),
        ],
        out_specs=pl.BlockSpec((width, columns), lambda i: (i, 0)),
        compiler_params=pltpu.CompilerParams(vmem_limit_bytes=VMEM_BYTES),
        cost_estimate=pl.CostEstimate(
            flops=tokens * N_DP * PAD * columns, bytes_accessed=N_DP * PAD * columns, transcendentals=0
        ),
    )(left, gate, up)


def attn_kernel(left_ref, mixed_ref, proj_ref, attn_ref, gain_ref, out_ref):
    qkv = across(left_ref[...], proj_ref[...])
    edge = QKV_PAD - LANES
    out_ref[:, :edge] = qkv[:, :edge].astype(BF16)
    out_ref[:, edge:QKV_PAD] = (qkv[:, edge:] + gain_ref[...]).astype(BF16)
    out_ref[:, QKV_PAD:] = across(mixed_ref[...], attn_ref[...]).astype(BF16)


def attn_sums(left, mixed, proj, attn, gain, first):
    tokens = left.shape[0]
    width = 128
    count = N_DP * PAD // 2 // width
    columns = QKV_PAD + OUT_PAD
    return pl.pallas_call(
        attn_kernel,
        grid=(count,),
        out_shape=jax.ShapeDtypeStruct((N_DP * PAD // 2, columns), BF16),
        in_specs=[
            pl.BlockSpec((tokens, width), lambda i: (0, i + first * count)),
            pl.BlockSpec((tokens, width), lambda i: (0, i + first * count)),
            pl.BlockSpec((tokens, QKV_PAD), lambda i: (0, 0)),
            pl.BlockSpec((tokens, OUT_PAD), lambda i: (0, 0)),
            pl.BlockSpec((width, LANES), lambda i: (i + first * count, 0)),
        ],
        out_specs=pl.BlockSpec((width, columns), lambda i: (i, 0)),
        compiler_params=pltpu.CompilerParams(vmem_limit_bytes=VMEM_BYTES),
        cost_estimate=pl.CostEstimate(
            flops=tokens * N_DP * PAD * columns, bytes_accessed=N_DP * PAD * columns, transcendentals=0
        ),
    )(left, mixed, proj, attn, gain)


def dot(left, right):
    return jnp.dot(left, right, preferred_element_type=F32)


def dot_t(left, right):
    return lax.dot_general(left, right, (((1,), (1,)), ((), ())), preferred_element_type=F32)


def shifted(block, axis, distance):
    devices = range(lax.axis_size(axis))
    pairs = [(i - distance, i) for i in devices if i - distance in devices]
    return lax.ppermute(block, axis, pairs)


def rope_tables(length):
    position = jnp.arange(length, dtype=F32)[:, None]
    frequency = ROPE_BASE ** (-jnp.arange(0, HD, 2, dtype=F32) / HD)
    angle = position * frequency[None, :]
    cosine, sine = jnp.cos(angle), jnp.sin(angle)
    return (jnp.tile(cosine, (1, LANES // (HD // 2))), jnp.tile(jnp.concatenate([-sine, sine], 1), (1, LANES // HD)))


SCALE = HD**-0.5
TURNED = D + KV * HD
PARTS = 5
PART = FF // PARTS


def params():
    return pltpu.CompilerParams(vmem_limit_bytes=VMEM_BYTES)


def whole(*shape):
    return pl.BlockSpec(shape, lambda *_: (0,) * len(shape))


def scaled(value, gain):
    return value * lax.rsqrt(jnp.mean(value * value, axis=-1, keepdims=True) + EPSILON) * gain


def scaled_backward(value, gain, grad):
    inverse = lax.rsqrt(jnp.mean(value * value, axis=-1, keepdims=True) + EPSILON)
    normed = value * inverse
    inner = grad * gain
    gain_sum = jnp.sum(grad * normed, axis=0, keepdims=True)
    through = inverse * (inner - normed * jnp.mean(inner * normed, axis=-1, keepdims=True))
    return (through, gain_sum)


def turn_heads(value, cosine, sine):
    first = lax.broadcasted_iota(jnp.int32, cosine.shape, 1) % HD < HD // 2
    tiles = []
    for start in range(0, TURNED, LANES):
        tile = value[:, start : start + LANES]
        other = jnp.where(first, pltpu.roll(tile, LANES - HD // 2, 1), pltpu.roll(tile, HD // 2, 1))
        tiles.append(tile * cosine + other * sine)
    return tiles


def head_columns(value, index):
    return value[:, index * HD : index * HD + HD]


def group_rows(value, group):
    return jnp.concatenate(
        [head_columns(value, group * (H // KV) + j) for j in range(H // KV)], 0
    ).astype(BF16)


def probabilities(queries, keys, mask):
    scores = jnp.where(mask > 0, dot_t(queries, keys) * SCALE, -1000000000.0)
    terms = jnp.exp(scores - jnp.max(scores, axis=-1, keepdims=True))
    return terms / jnp.sum(terms, axis=-1, keepdims=True)


def attend_forward_kernel(
    flag_ref, own_ref, got_ref, mask_ref, spread_ref, mat_ref, gains_ref, cosine_ref, sine_ref,
    hidden_ref, heads_ref, mixed_ref, middle_ref, second_ref,
):
    first = flag_ref[0] == 1
    stream = jnp.where(first, own_ref[0].astype(F32), got_ref[...].astype(F32))
    spread = spread_ref[...]
    gains = gains_ref[...]
    hidden = dot(scaled(stream, gains[0:1]).astype(BF16), spread).astype(BF16)
    hidden_ref[...] = hidden
    projected = dot(hidden, mat_ref[:, :QKV_PAD])
    tiles = turn_heads(projected, cosine_ref[...], sine_ref[...])
    for index, tile in enumerate(tiles):
        heads_ref[:, index * LANES : index * LANES + LANES] = tile.astype(BF16)
    heads_ref[:, TURNED:] = projected[:, TURNED:].astype(BF16)
    turned = jnp.concatenate(tiles, 1)
    mask = jnp.concatenate([mask_ref[0]] * (H // KV), 0)
    length = stream.shape[0]
    outs = []
    for group in range(KV):
        queries = group_rows(turned, group)
        keys = head_columns(turned, H + group).astype(BF16)
        values = head_columns(projected, H + KV + group).astype(BF16)
        mixed = dot(probabilities(queries, keys, mask).astype(BF16), values)
        outs += [mixed[j * length : j * length + length] for j in range(H // KV)]
    mixed = dot(jnp.concatenate(outs, 1).astype(BF16), spread).astype(BF16)
    mixed_ref[...] = mixed
    middle = stream + dot(mixed, mat_ref[:, QKV_PAD:])[:, :D]
    middle_ref[...] = middle
    second_ref[...] = dot(scaled(middle, gains[1:2]).astype(BF16), spread).astype(BF16)


def attend_forward(flags, inputs, got, masks, spread, mat, gains, cosine, sine):
    length = got.shape[0]
    wide = N_DP * PAD
    return pl.pallas_call(
        attend_forward_kernel,
        grid_spec=pltpu.PrefetchScalarGridSpec(
            num_scalar_prefetch=1,
            grid=(1,),
            in_specs=[
                pl.BlockSpec((1, length, D), lambda i, flag: (flag[1], 0, 0)),
                whole(length, D),
                pl.BlockSpec((1, length, length), lambda i, flag: (flag[1], 0, 0)),
                whole(D, wide),
                whole(wide, QKV_PAD + OUT_PAD),
                whole(2, D),
                whole(length, LANES),
                whole(length, LANES),
            ],
            out_specs=[
                whole(length, wide),
                whole(length, QKV_PAD),
                whole(length, wide),
                whole(length, D),
                whole(length, wide),
            ],
        ),
        out_shape=[
            jax.ShapeDtypeStruct((length, wide), BF16),
            jax.ShapeDtypeStruct((length, QKV_PAD), BF16),
            jax.ShapeDtypeStruct((length, wide), BF16),
            jax.ShapeDtypeStruct((length, D), F32),
            jax.ShapeDtypeStruct((length, wide), BF16),
        ],
        compiler_params=params(),
        cost_estimate=pl.CostEstimate(
            flops=2 * length * wide * 5700, bytes_accessed=8000000, transcendentals=H * length * length
        ),
    )(flags, inputs, got, masks, spread, mat, gains, cosine, sine)


def mlp_forward_kernel(
    second_ref, middle_ref, gate_mat_ref, up_mat_ref, down_ref, gate_ref, up_ref, act_ref, out_ref, sum_ref
):
    part = pl.program_id(0)
    second = second_ref[...]
    gate = dot(second, gate_mat_ref[...])
    up = dot(second, up_mat_ref[...])
    gate_ref[...] = gate
    up_ref[...] = up
    act = (gate / (1.0 + jnp.exp(-gate)) * up).astype(BF16)
    act_ref[...] = act
    before = jnp.where(part == 0, middle_ref[...], sum_ref[...])
    after_part = before + dot(act, down_ref[...])
    sum_ref[...] = after_part
    out_ref[...] = after_part.astype(BF16)


def mlp_forward(second, middle, gate_up_mat, down_mat):
    length, wide = second.shape
    column = lambda i: (0, i)
    return pl.pallas_call(
        mlp_forward_kernel,
        grid=(PARTS,),
        in_specs=[
            whole(length, wide),
            whole(length, D),
            pl.BlockSpec((wide, PART), column),
            pl.BlockSpec((wide, PART), lambda i: (0, i + PARTS)),
            pl.BlockSpec((PART, D), lambda i: (i, 0)),
        ],
        out_specs=[
            pl.BlockSpec((length, PART), column),
            pl.BlockSpec((length, PART), column),
            pl.BlockSpec((length, PART), column),
            whole(length, D),
        ],
        out_shape=[
            jax.ShapeDtypeStruct((length, FF), F32),
            jax.ShapeDtypeStruct((length, FF), F32),
            jax.ShapeDtypeStruct((length, FF), BF16),
            jax.ShapeDtypeStruct((length, D), BF16),
        ],
        scratch_shapes=[pltpu.VMEM((length, D), F32)],
        compiler_params=params(),
        cost_estimate=pl.CostEstimate(
            flops=2 * length * wide * 7680, bytes_accessed=20000000, transcendentals=length * FF
        ),
    )(second, middle, gate_up_mat, gate_up_mat, down_mat)


def mlp_backward_kernel(
    flag_ref, grad_ref, middle_a_ref, middle_b_ref, gate_a_ref, gate_b_ref, up_a_ref, up_b_ref,
    gate_mat_ref, up_mat_ref, down_ref, spread_ref, gains_ref,
    grad_gate_ref, grad_up_ref, grad_middle_ref, gain_ref, sum_ref,
):
    part = pl.program_id(0)
    first = flag_ref[0] == 1
    gate = jnp.where(first, gate_a_ref[...], gate_b_ref[...])
    up = jnp.where(first, up_a_ref[...], up_b_ref[...])
    grad_act = dot_t(grad_ref[...], down_ref[...])
    sig = 1.0 / (1.0 + jnp.exp(-gate))
    grad_gate = (grad_act * up * sig * (1.0 + gate * (1.0 - sig))).astype(BF16)
    grad_up = (grad_act * gate * sig).astype(BF16)
    grad_gate_ref[...] = grad_gate
    grad_up_ref[...] = grad_up
    more = dot_t(grad_gate, gate_mat_ref[...]) + dot_t(grad_up, up_mat_ref[...])

    @pl.when(part == 0)
    def begin():
        sum_ref[...] = more

    @pl.when(part > 0)
    def go_on():
        sum_ref[...] += more

    @pl.when(part == PARTS - 1)
    def end():
        grad_two = dot_t(sum_ref[...].astype(BF16), spread_ref[...])
        middle = jnp.where(first, middle_a_ref[...], middle_b_ref[...])
        through, gain = scaled_backward(middle, gains_ref[1:2], grad_two)
        grad_middle_ref[...] = grad_ref[...].astype(F32) + through
        gain_ref[...] = gain


def mlp_backward(flags, grad, middles, gates, ups, gate_up_mat, down_mat, spread, gains):
    length = grad.shape[0]
    wide = N_DP * PAD
    column = lambda i, flag: (0, i)
    chosen = pl.BlockSpec((length, PART), lambda i, flag: (0, i * flag[0]))
    other = pl.BlockSpec((length, PART), lambda i, flag: (0, i * (1 - flag[0])))
    return pl.pallas_call(
        mlp_backward_kernel,
        grid_spec=pltpu.PrefetchScalarGridSpec(
            num_scalar_prefetch=1,
            grid=(PARTS,),
            in_specs=[
                whole(length, D),
                whole(length, D),
                whole(length, D),
                chosen,
                other,
                chosen,
                other,
                pl.BlockSpec((wide, PART), column),
                pl.BlockSpec((wide, PART), lambda i, flag: (0, i + PARTS)),
                pl.BlockSpec((PART, D), lambda i, flag: (i, 0)),
                whole(D, wide),
                whole(2, D),
            ],
            out_specs=[
                pl.BlockSpec((length, PART), column),
                pl.BlockSpec((length, PART), column),
                whole(length, D),
                whole(1, D),
            ],
            scratch_shapes=[pltpu.VMEM((length, wide), F32)],
        ),
        out_shape=[
            jax.ShapeDtypeStruct((length, FF), BF16),
            jax.ShapeDtypeStruct((length, FF), BF16),
            jax.ShapeDtypeStruct((length, D), F32),
            jax.ShapeDtypeStruct((1, D), F32),
        ],
        compiler_params=params(),
        cost_estimate=pl.CostEstimate(
            flops=2 * length * wide * 7680, bytes_accessed=22000000, transcendentals=length * FF
        ),
    )(flags, grad, *middles, *gates, *ups, gate_up_mat, gate_up_mat, down_mat, spread, gains)


def attend_backward_kernel(
    flag_ref, grad_ref, own_ref, got_ref, heads_a_ref, heads_b_ref, mask_ref, spread_ref, mat_ref,
    gains_ref, cosine_ref, sine_ref, grad_proj_ref, grad_attn_ref, grad_in_ref, gain_ref,
):
    first = flag_ref[0] == 1
    spread = spread_ref[...]
    grad_middle = grad_ref[...]
    grad_attn = grad_middle.astype(BF16)
    length = grad_middle.shape[0]
    grad_attn_ref[:, :D] = grad_attn
    grad_attn_ref[:, D:] = jnp.zeros((length, OUT_PAD - D), BF16)
    grad_mixed = dot_t(grad_attn, mat_ref[:, QKV_PAD : QKV_PAD + D]).astype(BF16)
    grad_mixed = dot_t(grad_mixed, spread)
    heads = jnp.where(first, heads_a_ref[...].astype(F32), heads_b_ref[...].astype(F32))
    mask = jnp.concatenate([mask_ref[0]] * (H // KV), 0)
    grad_queries, grad_keys, grad_values = [], [], []
    for group in range(KV):
        queries = group_rows(heads, group)
        keys = head_columns(heads, H + group).astype(BF16)
        values = head_columns(heads, H + KV + group).astype(BF16)
        mixed = group_rows(grad_mixed, group)
        probs = probabilities(queries, keys, mask)
        grad_probs = dot_t(mixed, values)
        grad_scores = probs * (grad_probs - jnp.sum(grad_probs * probs, axis=-1, keepdims=True))
        grad_scores = grad_scores.astype(BF16)
        queries_part = dot(grad_scores, keys) * SCALE
        grad_queries += [queries_part[j * length : j * length + length] for j in range(H // KV)]
        grad_keys.append(across(grad_scores, queries) * SCALE)
        grad_values.append(across(probs.astype(BF16), mixed))
    turned = jnp.concatenate(grad_queries + grad_keys, 1).astype(BF16).astype(F32)
    tiles = turn_heads(turned, cosine_ref[...], -sine_ref[...])
    blank = jnp.zeros((length, QKV_PAD - QKV), F32)
    grad_proj = jnp.concatenate(tiles + grad_values + [blank], 1).astype(BF16)
    grad_proj_ref[...] = grad_proj
    grad_one = dot_t(grad_proj, mat_ref[:, :QKV_PAD]).astype(BF16)
    grad_one = dot_t(grad_one, spread)
    stream = jnp.where(first, own_ref[0].astype(F32), got_ref[...].astype(F32))
    through, gain = scaled_backward(stream, gains_ref[0:1], grad_one)
    grad_in_ref[...] = (grad_middle + through).astype(BF16)
    gain_ref[...] = gain


def attend_backward(flags, grad, inputs, got, heads, masks, spread, mat, gains, cosine, sine):
    length = grad.shape[0]
    wide = N_DP * PAD
    return pl.pallas_call(
        attend_backward_kernel,
        grid_spec=pltpu.PrefetchScalarGridSpec(
            num_scalar_prefetch=1,
            grid=(1,),
            in_specs=[
                whole(length, D),
                pl.BlockSpec((1, length, D), lambda i, flag: (flag[1], 0, 0)),
                whole(length, D),
                whole(length, QKV_PAD),
                whole(length, QKV_PAD),
                pl.BlockSpec((1, length, length), lambda i, flag: (flag[1], 0, 0)),
                whole(D, wide),
                whole(wide, QKV_PAD + OUT_PAD),
                whole(2, D),
                whole(length, LANES),
                whole(length, LANES),
            ],
            out_specs=[
                whole(length, QKV_PAD),
                whole(length, OUT_PAD),
                whole(length, D),
                whole(1, D),
            ],
        ),
        out_shape=[
            jax.ShapeDtypeStruct((length, QKV_PAD), BF16),
            jax.ShapeDtypeStruct((length, OUT_PAD), BF16),
            jax.ShapeDtypeStruct((length, D), BF16),
            jax.ShapeDtypeStruct((1, D), F32),
        ],
        compiler_params=params(),
        cost_estimate=pl.CostEstimate(
            flops=2 * length * wide * 6700, bytes_accessed=9000000, transcendentals=H * length * length
        ),
    )(flags, grad, inputs, got, *heads, masks, spread, mat, gains, cosine, sine)


def as_blocks(rows):
    return rows.reshape(N_DP // 2, -1, rows.shape[-1])


def per_device(
    inputs, segment_ids, qkv_weight, out_weight, gate_up_weight, down_weight, norm_gains, cotangent
):
    batches = inputs.shape[0]
    is_first = lax.axis_index("section") == 0
    order = block_order()
    spread = placement(order)
    attn_shard = jnp.concatenate(
        [
            qkv_weight[0],
            norm_gains[0],
            jnp.zeros((ROWS, QKV_PAD - QKV - 2), BF16),
            out_weight[0],
            jnp.zeros((ROWS, OUT_PAD - D), BF16),
        ],
        1,
    )
    widths = (QKV_PAD + OUT_PAD, 2 * FF)
    down_shard = jnp.pad(down_weight[0], ((0, 0), (0, OUT_PAD - D))).reshape(PAD, -1)
    rows = jnp.concatenate(
        [
            jnp.pad(attn_shard, ((0, 1), (0, 0))),
            jnp.pad(gate_up_weight[0], ((0, 1), (0, 0))),
            down_shard,
        ],
        1,
    )
    near = gather_near(rows)
    near_attn = near[:, :, : widths[0]]
    near_gate_up = near[:, :, widths[0] : widths[0] + widths[1]]
    near_down = near[:, :, widths[0] + widths[1] :].reshape(8, FROWS, OUT_PAD)[:, :, :D]
    signal, attn_mat = gather_far(near_attn)
    signal, gate_up_mat = gather_far(after(near_gate_up, signal))
    signal, down_mat = gather_far(after(near_down, signal))
    attn_mat = attn_mat.reshape(N_DP * PAD, -1)
    gate_up_mat = gate_up_mat.reshape(N_DP * PAD, -1)
    down_mat = reorder(down_mat, order, True).reshape(FF, D)
    gains_full = lax.dot_general(
        attn_mat[:, QKV : QKV + 2], spread, (((0,), (1,)), ((), ())), preferred_element_type=F32
    )
    length = inputs.shape[1]
    cosine, sine = rope_tables(length)
    positions = jnp.arange(length)
    masks = (
        (segment_ids[:, :, None] == segment_ids[:, None, :])
        & (positions[:, None] >= positions[None, :])[None]
    ).astype(F32)
    first = is_first.astype(jnp.int32)

    def flags(for_first, for_second):
        return jnp.stack([first, jnp.where(is_first, for_first, for_second)])

    received = jnp.zeros(inputs.shape[1:], BF16)
    saved = []
    produced = []
    arrivals = []
    for turn in range(batches + 1):
        arrivals.append(received)
        hidden, heads, mixed, middle, second = attend_forward(
            flags(min(turn, batches - 1), max(turn - 1, 0)),
            inputs, received, masks, spread, attn_mat, gains_full, cosine, sine,
        )
        gate, up, act, layer_out = mlp_forward(second, middle, gate_up_mat, down_mat)
        saved.append((hidden, heads, mixed, middle, second, gate, up, act))
        produced.append(layer_out)
        if turn < batches:
            received = shifted(layer_out, "section", 1)
    section_outputs = jnp.stack(
        [
            jnp.where(is_first, produced[position], produced[position + 1])
            for position in range(batches)
        ]
    )[None]
    received = jnp.zeros(inputs.shape[1:], BF16)
    places = jnp.sum(
        jnp.where(order[:, None] == jnp.arange(N_DP)[None, :], jnp.arange(N_DP)[:, None], 0), 0
    ).astype(jnp.int32)

    def lefts(member):
        return jnp.concatenate(
            [jnp.where(is_first, saved[b][member], saved[b + 1][member]) for b in range(batches)], 0
        )

    def rights(turns):
        return jnp.concatenate(
            [jnp.where(is_first, turns[b + 1], turns[b]) for b in range(batches)], 0
        )

    returned = []
    downs = []
    gates = []
    ups = []
    projs = []
    attns = []
    gain_sum = 0
    flows = {}
    gate_up_own = []
    attn_own = []
    for turn in range(batches + 1):
        last = turn == batches
        if turn < batches:
            own_grad = cotangent[turn]
        else:
            own_grad = jnp.zeros(inputs.shape[1:], BF16)
        grad_out = jnp.where(is_first, received, own_grad)
        downs.append(grad_out)
        if last:
            blocks = down_sums(lefts(7), rights(downs), places)
            grad_out = after(grad_out, blocks)
            flows["down"] = Flow(
                down_scatter(blocks[N_DP // 2 :], lambda: blocks[: N_DP // 2])
            )
        kept_first, kept_second = saved[max(turn - 1, 0)], saved[min(turn + 1, batches)]
        chosen = flags(max(turn - 1, 0), min(turn, batches - 1))

        def both(member):
            return (kept_first[member], kept_second[member])

        grad_gate, grad_up, grad_middle, gain_two = mlp_backward(
            chosen, grad_out, both(3), both(5), both(6), gate_up_mat, down_mat, spread, gains_full
        )
        gates.append(grad_gate)
        ups.append(grad_up)
        if last:
            terms = (lefts(4), rights(gates), rights(ups))
            other = gate_up_sums(*terms, 1)
            other = step([flows["down"]], other)
            flows["gate_up"] = Flow(
                far_scatter(as_blocks(other), lambda: as_blocks(gate_up_own[0]))
            )
            gate_up_own.append(gate_up_sums(*after(terms, other), 0))
            grad_middle = after(grad_middle, gate_up_own[0])
        grad_proj, grad_attn, grad_in, gain_one = attend_backward(
            chosen, grad_middle, inputs, arrivals[min(turn + 1, batches)], both(1), masks, spread,
            attn_mat, gains_full, cosine, sine,
        )
        if last:
            grad_proj = step([flows["down"], flows["gate_up"]], grad_proj)
        projs.append(grad_proj)
        attns.append(grad_attn)
        gain_sum = gain_sum + jnp.concatenate([gain_one, gain_two], 0)
        returned.append(grad_in)
        if turn < batches:
            received = shifted(grad_in, "section", -1)
    section_input_grads = jnp.stack(
        [
            jnp.where(is_first, returned[position + 1], returned[position])
            for position in range(batches)
        ]
    )[None]
    gain_high = gain_sum.astype(BF16)
    gain_low = (gain_sum - gain_high.astype(F32)).astype(BF16)
    gain_rows = lax.dot_general(
        spread, jnp.stack([gain_high, gain_low]), (((0,), (2,)), ((), ())), preferred_element_type=F32
    )
    first_lane = QKV - (QKV_PAD - LANES)
    gain_rows = jnp.pad(
        gain_rows[:, 0] + gain_rows[:, 1], ((0, 0), (first_lane, LANES - first_lane - 2))
    )
    terms = (lefts(0), lefts(2), rights(projs), rights(attns), gain_rows)
    other = attn_sums(*terms, 1)
    flows["attn"] = Flow(far_scatter(as_blocks(other), lambda: as_blocks(attn_own[0])))
    attn_own.append(attn_sums(*after(terms, other), 0))
    down_flow, gate_up_flow, attn_flow = flows["down"], flows["gate_up"], flows["attn"]
    waiting = attn_own[0]
    while attn_flow.result is None or gate_up_flow.result is None:
        waiting = step([down_flow, gate_up_flow, attn_flow], waiting)
    near_flow = Flow(near_scatter(jnp.concatenate([attn_flow.result, gate_up_flow.result], -1)))
    while near_flow.result is None or down_flow.result is None:
        waiting = step([down_flow, near_flow], waiting)
    down_grad = down_flow.result
    attn_grad = near_flow.result[:, : QKV_PAD + OUT_PAD]
    gate_up_grad = near_flow.result[:, QKV_PAD + OUT_PAD :]
    return (
        section_outputs,
        section_input_grads,
        attn_grad[None, :ROWS, :QKV],
        attn_grad[None, :ROWS, QKV_PAD : QKV_PAD + D],
        gate_up_grad[None, :ROWS],
        down_grad[None],
        attn_grad[None, :ROWS, QKV : QKV + 2],
    )


def solution(mesh):
    in_specs = (
        P(None, "dp", None),
        P(None, "dp"),
        P("section", "dp", None),
        P("section", "dp", None),
        P("section", "dp", None),
        P("section", "dp", None),
        P("section", "dp", None),
        P(None, "dp", None),
    )
    out_specs = (
        P("section", None, "dp", None),
        P("section", None, "dp", None),
        P("section", "dp", None),
        P("section", "dp", None),
        P("section", "dp", None),
        P("section", "dp", None),
        P("section", "dp", None),
    )
    return jax.shard_map(
        per_device, mesh=mesh, in_specs=in_specs, out_specs=out_specs, check_vma=False
    )
```

```python
import jax
import jax.numpy as jnp
from jax import lax
from jax.experimental import pallas as pl
from jax.experimental.pallas import tpu as pltpu
from jax.sharding import PartitionSpec as P

D = 960
H = 15
KV = 5
HD = 64
FF = 2560
QKV = D + 2 * KV * HD
N_DP = 64
ROWS = D // N_DP
PAD = 16
FROWS = FF // N_DP
LANES = 128
QKV_PAD = 1664
OUT_PAD = 1024

EPSILON = 1e-05
ROPE_BASE = 100000.0
BF16 = jnp.bfloat16
F32 = jnp.float32


def place(y, x, z, core):
    return ((y % 4 * 2 + x % 2) * 4 + z % 4) * 2 + core % 2


def route(kind, step):
    pairs = []
    for source in range(N_DP):
        y, x, z, core = source // 16, source // 8 % 2, source // 2 % 4, source % 2
        if kind == "core":
            target = place(y, x, z, core + 1)
        elif kind == "x":
            target = place(y, x + 1, z, core)
        elif (kind == "wide") == (core == 0):
            target = place(y, x, z + step, core)
        else:
            target = place(y + step, x, z, core)
        pairs.append((source, target))
    return pairs


def send(block, kind, step=1):
    return lax.ppermute(block, "dp", route(kind, step))


def total(*terms):
    result = terms[0].astype(F32)
    for term in terms[1:]:
        result = result + term.astype(F32)
    return result


def near_scatter(blocks):
    blocks = yield from ring_scatter((blocks,), "narrow")
    (got,) = yield ((blocks[1], "x"),)
    return total(blocks[0], got)


def ring_scatter(terms, kind):
    terms = [term.reshape((4, term.shape[0] // 4) + term.shape[1:]) for term in terms]
    half = terms[0].shape[1] // 2

    def own(step, part):
        return [term[step, part] for term in terms]

    near, far = slice(0, half), slice(half, None)
    left, right = yield (
        (total(*own(3, near)).astype(BF16), kind, 1),
        (total(*own(3, far)).astype(BF16), kind, -1),
    )
    onward = jnp.concatenate([total(*own(1, near), left), total(*own(1, far))], 0).astype(BF16)
    back = jnp.concatenate([total(*own(2, near)), total(*own(2, far), right)], 0).astype(BF16)
    left, right = yield ((onward, kind, 1), (back, kind, -1))
    return total(*[term[0] for term in terms], left, right).astype(BF16)


def far_scatter(for_other, for_own):
    (got,) = yield ((for_other, "core"),)
    return (yield from ring_scatter((for_own(), got), "wide"))


def full_scatter(for_other, for_own):
    blocks = yield from far_scatter(for_other, for_own)
    return (yield from near_scatter(blocks))


class Flow:
    def __init__(self, stages):
        self.stages = stages
        self.result = None
        self.wanted = next(stages)
        self.launch(tuple(request[0] for request in self.wanted))

    def launch(self, blocks):
        self.pending = tuple(
            send(block, *request[1:]) for block, request in zip(blocks, self.wanted)
        )

    def advance(self, arrived):
        try:
            self.wanted = self.stages.send(arrived)
        except StopIteration as end:
            self.wanted = ()
            self.result = end.value


def step(flows, value):
    flows = [flow for flow in flows if flow.result is None]
    arrived, value = lax.optimization_barrier((tuple(flow.pending for flow in flows), value))
    for flow, got in zip(flows, arrived):
        flow.advance(got)
    blocks = tuple(tuple(request[0] for request in flow.wanted) for flow in flows)
    blocks, value = lax.optimization_barrier((blocks, value))
    for flow, ready in zip(flows, blocks):
        flow.launch(ready)
    return value


def ring_gather(block, kind):
    half = block.shape[0] // 2
    from_left = send(block, kind, 1)
    from_right = send(block, kind, -1)
    far_left = send(from_left[:half], kind, 1)
    far_right = send(from_right[half:], kind, -1)
    sides = jnp.concatenate([from_right, from_left], 0)
    return [block, sides, jnp.concatenate([far_left, far_right], 0)]


def gather_near(shard):
    block = jnp.stack([shard, send(shard, "x")], 0)
    return jnp.concatenate(ring_gather(block, "narrow"), 0)


def gather_far(block):
    half = block.shape[0] // 2
    left, right, others = yield ((block, "wide", 1), (block, "wide", -1), (block, "core"))
    sides = jnp.concatenate([right, left], 0)
    left, right, sides_there = yield (
        (left[:half], "wide", 1),
        (right[half:], "wide", -1),
        (sides, "core"),
    )
    far = jnp.concatenate([left, right], 0)
    (far_there,) = yield ((far, "core"),)
    return jnp.concatenate([block, sides, far, others, sides_there, far_there], 0)


def after(value, earlier):
    return lax.optimization_barrier((value, earlier))[0]


def block_order():
    index = lax.axis_index("dp")
    y, x, z, core = index // 16, index // 8 % 2, index // 2 % 4, index % 2
    position = jnp.arange(N_DP)
    core_step, wide, narrow, x_step = position // 32, position // 8 % 4, position // 2 % 4, position % 2
    wide, narrow = wide ^ (wide // 2), narrow ^ (narrow // 2)
    core_there = (core + core_step) % 2
    z_step = jnp.where(core_there == 0, wide, narrow)
    y_step = jnp.where(core_there == 0, narrow, wide)
    return (((y + y_step) % 4 * 2 + (x + x_step) % 2) * 4 + (z + z_step) % 4) * 2 + core_there


def placement(order):
    column = jnp.arange(N_DP * PAD)
    inner = column % PAD
    row = jnp.where(inner < ROWS, jnp.repeat(order, PAD) * ROWS + inner, -1)
    return (jnp.arange(D)[:, None] == row[None, :]).astype(BF16)


def reorder_kernel(scatter, order_ref, blocks_ref, out_ref):
    def one(step, carry):
        there = order_ref[step]
        if scatter:
            out_ref[there] = blocks_ref[step]
        else:
            out_ref[step] = blocks_ref[there]
        return carry

    lax.fori_loop(0, N_DP, one, 0)


def reorder(blocks, order, scatter):
    return pl.pallas_call(
        lambda *refs: reorder_kernel(scatter, *refs),
        out_shape=jax.ShapeDtypeStruct(blocks.shape, blocks.dtype),
        in_specs=[
            pl.BlockSpec(memory_space=pltpu.SMEM),
            pl.BlockSpec(memory_space=pltpu.VMEM),
        ],
        out_specs=pl.BlockSpec(memory_space=pltpu.VMEM),
        compiler_params=pltpu.CompilerParams(vmem_limit_bytes=24 * 1024 * 1024),
    )(order, blocks)


def across(left, right):
    return lax.dot_general(left, right, (((0,), (0,)), ((), ())), preferred_element_type=F32)


VMEM_BYTES = 16 * 1024 * 1024


def down_kernel(place_ref, left_ref, right_ref, own_ref, other_ref):
    step = pl.program_id(0)
    rows = across(left_ref[...], right_ref[...]).astype(BF16)
    count = rows.shape[0] // FROWS
    for block in range(count):
        place_here = place_ref[step * count + block]
        part = rows[block * FROWS : (block + 1) * FROWS]

        @pl.when(place_here < N_DP // 2)
        def keep():
            own_ref[place_here] = part

        @pl.when(place_here >= N_DP // 2)
        def give():
            other_ref[place_here - N_DP // 2] = part


def down_sums(left, right, places):
    tokens = left.shape[0]
    width = 640
    return pl.pallas_call(
        down_kernel,
        grid=(FF // width,),
        out_shape=[jax.ShapeDtypeStruct((N_DP // 2, FROWS, D), BF16)] * 2,
        in_specs=[
            pl.BlockSpec(memory_space=pltpu.SMEM),
            pl.BlockSpec((tokens, width), lambda i: (0, i)),
            pl.BlockSpec((tokens, D), lambda i: (0, 0)),
        ],
        out_specs=[pl.BlockSpec((N_DP // 2, FROWS, D), lambda i: (0, 0, 0))] * 2,
        compiler_params=pltpu.CompilerParams(vmem_limit_bytes=VMEM_BYTES),
        cost_estimate=pl.CostEstimate(
            flops=2 * tokens * FF * D, bytes_accessed=2 * FF * D, transcendentals=0
        ),
    )(places, left, right)


def gate_up_kernel(left_ref, gate_ref, up_ref, out_ref):
    left = left_ref[...]
    out_ref[:, :FF] = across(left, gate_ref[...]).astype(BF16)
    out_ref[:, FF:] = across(left, up_ref[...]).astype(BF16)


def gate_up_sums(left, gate, up, first):
    tokens = left.shape[0]
    columns = 2 * FF
    width = 128
    count = N_DP * PAD // 2 // width
    return pl.pallas_call(
        gate_up_kernel,
        grid=(count,),
        out_shape=jax.ShapeDtypeStruct((N_DP * PAD // 2, columns), BF16),
        in_specs=[
            pl.BlockSpec((tokens, width), lambda i: (0, i + first * count)),
            pl.BlockSpec((tokens, FF), lambda i: (0, 0)),
            pl.BlockSpec((tokens, FF), lambda i: (0, 0)),
        ],
        out_specs=pl.BlockSpec((width, columns), lambda i: (i, 0)),
        compiler_params=pltpu.CompilerParams(vmem_limit_bytes=VMEM_BYTES),
        cost_estimate=pl.CostEstimate(
            flops=tokens * N_DP * PAD * columns, bytes_accessed=N_DP * PAD * columns, transcendentals=0
        ),
    )(left, gate, up)


def attn_kernel(left_ref, mixed_ref, proj_ref, attn_ref, gain_ref, out_ref):
    qkv = across(left_ref[...], proj_ref[...])
    edge = QKV_PAD - LANES
    out_ref[:, :edge] = qkv[:, :edge].astype(BF16)
    out_ref[:, edge:QKV_PAD] = (qkv[:, edge:] + gain_ref[...]).astype(BF16)
    out_ref[:, QKV_PAD:] = across(mixed_ref[...], attn_ref[...]).astype(BF16)


def attn_sums(left, mixed, proj, attn, gain, first):
    tokens = left.shape[0]
    width = 128
    count = N_DP * PAD // 2 // width
    columns = QKV_PAD + OUT_PAD
    return pl.pallas_call(
        attn_kernel,
        grid=(count,),
        out_shape=jax.ShapeDtypeStruct((N_DP * PAD // 2, columns), BF16),
        in_specs=[
            pl.BlockSpec((tokens, width), lambda i: (0, i + first * count)),
            pl.BlockSpec((tokens, width), lambda i: (0, i + first * count)),
            pl.BlockSpec((tokens, QKV_PAD), lambda i: (0, 0)),
            pl.BlockSpec((tokens, OUT_PAD), lambda i: (0, 0)),
            pl.BlockSpec((width, LANES), lambda i: (i + first * count, 0)),
        ],
        out_specs=pl.BlockSpec((width, columns), lambda i: (i, 0)),
        compiler_params=pltpu.CompilerParams(vmem_limit_bytes=VMEM_BYTES),
        cost_estimate=pl.CostEstimate(
            flops=tokens * N_DP * PAD * columns, bytes_accessed=N_DP * PAD * columns, transcendentals=0
        ),
    )(left, mixed, proj, attn, gain)


def dot(left, right):
    return jnp.dot(left, right, preferred_element_type=F32)


def dot_t(left, right):
    return lax.dot_general(left, right, (((1,), (1,)), ((), ())), preferred_element_type=F32)


def shifted(block, axis, distance):
    devices = range(lax.axis_size(axis))
    pairs = [(i - distance, i) for i in devices if i - distance in devices]
    return lax.ppermute(block, axis, pairs)


def rope_tables(length):
    position = jnp.arange(length, dtype=F32)[:, None]
    frequency = ROPE_BASE ** (-jnp.arange(0, HD, 2, dtype=F32) / HD)
    angle = position * frequency[None, :]
    cosine, sine = jnp.cos(angle), jnp.sin(angle)
    return (jnp.tile(cosine, (1, LANES // (HD // 2))), jnp.tile(jnp.concatenate([-sine, sine], 1), (1, LANES // HD)))


SCALE = HD**-0.5
TURNED = D + KV * HD
PARTS = 5
PART = FF // PARTS


def params():
    return pltpu.CompilerParams(vmem_limit_bytes=VMEM_BYTES)


def whole(*shape):
    return pl.BlockSpec(shape, lambda *_: (0,) * len(shape), pipeline_mode=pl.Buffered(1))


def scaled(value, gain):
    return value * lax.rsqrt(jnp.mean(value * value, axis=-1, keepdims=True) + EPSILON) * gain


def scaled_backward(value, gain, grad):
    inverse = lax.rsqrt(jnp.mean(value * value, axis=-1, keepdims=True) + EPSILON)
    normed = value * inverse
    inner = grad * gain
    gain_sum = jnp.sum(grad * normed, axis=0, keepdims=True)
    through = inverse * (inner - normed * jnp.mean(inner * normed, axis=-1, keepdims=True))
    return (through, gain_sum)


def turn_heads(value, cosine, sine):
    first = lax.broadcasted_iota(jnp.int32, cosine.shape, 1) % HD < HD // 2
    tiles = []
    for start in range(0, TURNED, LANES):
        tile = value[:, start : start + LANES]
        other = jnp.where(first, pltpu.roll(tile, LANES - HD // 2, 1), pltpu.roll(tile, HD // 2, 1))
        tiles.append(tile * cosine + other * sine)
    return tiles


def head_columns(value, index):
    return value[:, index * HD : index * HD + HD]


def group_rows(value, group):
    return jnp.concatenate(
        [head_columns(value, group * (H // KV) + j) for j in range(H // KV)], 0
    ).astype(BF16)


def probabilities(queries, keys, mask):
    scores = jnp.where(mask > 0, dot_t(queries, keys) * SCALE, -1000000000.0)
    terms = jnp.exp(scores - jnp.max(scores, axis=-1, keepdims=True))
    return terms / jnp.sum(terms, axis=-1, keepdims=True)


def attend_forward_kernel(
    flag_ref, own_ref, got_ref, mask_ref, spread_ref, mat_ref, gains_ref, cosine_ref, sine_ref,
    hidden_ref, heads_ref, mixed_ref, middle_ref, second_ref,
):
    first = flag_ref[0] == 1
    stream = jnp.where(first, own_ref[0].astype(F32), got_ref[...].astype(F32))
    spread = spread_ref[...]
    gains = gains_ref[...]
    hidden = dot(scaled(stream, gains[0:1]).astype(BF16), spread).astype(BF16)
    hidden_ref[...] = hidden
    projected = dot(hidden, mat_ref[:, :QKV_PAD])
    tiles = turn_heads(projected, cosine_ref[...], sine_ref[...])
    for index, tile in enumerate(tiles):
        heads_ref[:, index * LANES : index * LANES + LANES] = tile.astype(BF16)
    heads_ref[:, TURNED:] = projected[:, TURNED:].astype(BF16)
    turned = jnp.concatenate(tiles, 1)
    mask = jnp.concatenate([mask_ref[0]] * (H // KV), 0)
    length = stream.shape[0]
    outs = []
    for group in range(KV):
        queries = group_rows(turned, group)
        keys = head_columns(turned, H + group).astype(BF16)
        values = head_columns(projected, H + KV + group).astype(BF16)
        mixed = dot(probabilities(queries, keys, mask).astype(BF16), values)
        outs += [mixed[j * length : j * length + length] for j in range(H // KV)]
    mixed = dot(jnp.concatenate(outs, 1).astype(BF16), spread).astype(BF16)
    mixed_ref[...] = mixed
    middle = stream + dot(mixed, mat_ref[:, QKV_PAD:])[:, :D]
    middle_ref[...] = middle
    second_ref[...] = dot(scaled(middle, gains[1:2]).astype(BF16), spread).astype(BF16)


def attend_forward(flags, inputs, got, masks, spread, mat, gains, cosine, sine):
    length = got.shape[0]
    wide = N_DP * PAD
    return pl.pallas_call(
        attend_forward_kernel,
        grid_spec=pltpu.PrefetchScalarGridSpec(
            num_scalar_prefetch=1,
            grid=(1,),
            in_specs=[
                pl.BlockSpec((1, length, D), lambda i, flag: (flag[1], 0, 0)),
                whole(length, D),
                pl.BlockSpec((1, length, length), lambda i, flag: (flag[1], 0, 0)),
                whole(D, wide),
                whole(wide, QKV_PAD + OUT_PAD),
                whole(2, D),
                whole(length, LANES),
                whole(length, LANES),
            ],
            out_specs=[
                whole(length, wide),
                whole(length, QKV_PAD),
                whole(length, wide),
                whole(length, D),
                whole(length, wide),
            ],
        ),
        out_shape=[
            jax.ShapeDtypeStruct((length, wide), BF16),
            jax.ShapeDtypeStruct((length, QKV_PAD), BF16),
            jax.ShapeDtypeStruct((length, wide), BF16),
            jax.ShapeDtypeStruct((length, D), F32),
            jax.ShapeDtypeStruct((length, wide), BF16),
        ],
        compiler_params=params(),
        cost_estimate=pl.CostEstimate(
            flops=2 * length * wide * 5700, bytes_accessed=8000000, transcendentals=H * length * length
        ),
    )(flags, inputs, got, masks, spread, mat, gains, cosine, sine)


def mlp_forward_kernel(
    second_ref, middle_ref, gate_mat_ref, up_mat_ref, down_ref, gate_ref, up_ref, act_ref, out_ref, sum_ref
):
    part = pl.program_id(0)
    second = second_ref[...]
    gate = dot(second, gate_mat_ref[...])
    up = dot(second, up_mat_ref[...])
    gate_ref[...] = gate
    up_ref[...] = up
    act = (gate / (1.0 + jnp.exp(-gate)) * up).astype(BF16)
    act_ref[...] = act
    before = jnp.where(part == 0, middle_ref[...], sum_ref[...])
    after_part = before + dot(act, down_ref[...])
    sum_ref[...] = after_part
    out_ref[...] = after_part.astype(BF16)


def mlp_forward(second, middle, gate_up_mat, down_mat):
    length, wide = second.shape
    column = lambda i: (0, i)
    return pl.pallas_call(
        mlp_forward_kernel,
        grid=(PARTS,),
        in_specs=[
            whole(length, wide),
            whole(length, D),
            pl.BlockSpec((wide, PART), column),
            pl.BlockSpec((wide, PART), lambda i: (0, i + PARTS)),
            pl.BlockSpec((PART, D), lambda i: (i, 0)),
        ],
        out_specs=[
            pl.BlockSpec((length, PART), column),
            pl.BlockSpec((length, PART), column),
            pl.BlockSpec((length, PART), column),
            whole(length, D),
        ],
        out_shape=[
            jax.ShapeDtypeStruct((length, FF), F32),
            jax.ShapeDtypeStruct((length, FF), F32),
            jax.ShapeDtypeStruct((length, FF), BF16),
            jax.ShapeDtypeStruct((length, D), BF16),
        ],
        scratch_shapes=[pltpu.VMEM((length, D), F32)],
        compiler_params=params(),
        cost_estimate=pl.CostEstimate(
            flops=2 * length * wide * 7680, bytes_accessed=20000000, transcendentals=length * FF
        ),
    )(second, middle, gate_up_mat, gate_up_mat, down_mat)


def mlp_backward_kernel(
    flag_ref, grad_ref, middle_a_ref, middle_b_ref, gate_a_ref, gate_b_ref, up_a_ref, up_b_ref,
    gate_mat_ref, up_mat_ref, down_ref, spread_ref, gains_ref,
    grad_gate_ref, grad_up_ref, grad_middle_ref, gain_ref, sum_ref,
):
    part = pl.program_id(0)
    first = flag_ref[0] == 1
    gate = jnp.where(first, gate_a_ref[...], gate_b_ref[...])
    up = jnp.where(first, up_a_ref[...], up_b_ref[...])
    grad_act = dot_t(grad_ref[...], down_ref[...])
    sig = 1.0 / (1.0 + jnp.exp(-gate))
    grad_gate = (grad_act * up * sig * (1.0 + gate * (1.0 - sig))).astype(BF16)
    grad_up = (grad_act * gate * sig).astype(BF16)
    grad_gate_ref[...] = grad_gate
    grad_up_ref[...] = grad_up
    more = dot_t(grad_gate, gate_mat_ref[...]) + dot_t(grad_up, up_mat_ref[...])

    @pl.when(part == 0)
    def begin():
        sum_ref[...] = more

    @pl.when(part > 0)
    def go_on():
        sum_ref[...] += more

    @pl.when(part == PARTS - 1)
    def end():
        grad_two = dot_t(sum_ref[...].astype(BF16), spread_ref[...])
        middle = jnp.where(first, middle_a_ref[...], middle_b_ref[...])
        through, gain = scaled_backward(middle, gains_ref[1:2], grad_two)
        grad_middle_ref[...] = grad_ref[...].astype(F32) + through
        gain_ref[...] = gain


def mlp_backward(flags, grad, middles, gates, ups, gate_up_mat, down_mat, spread, gains):
    length = grad.shape[0]
    wide = N_DP * PAD
    column = lambda i, flag: (0, i)
    chosen = pl.BlockSpec((length, PART), lambda i, flag: (0, i * flag[0]))
    other = pl.BlockSpec((length, PART), lambda i, flag: (0, i * (1 - flag[0])))
    return pl.pallas_call(
        mlp_backward_kernel,
        grid_spec=pltpu.PrefetchScalarGridSpec(
            num_scalar_prefetch=1,
            grid=(PARTS,),
            in_specs=[
                whole(length, D),
                whole(length, D),
                whole(length, D),
                chosen,
                other,
                chosen,
                other,
                pl.BlockSpec((wide, PART), column),
                pl.BlockSpec((wide, PART), lambda i, flag: (0, i + PARTS)),
                pl.BlockSpec((PART, D), lambda i, flag: (i, 0)),
                whole(D, wide),
                whole(2, D),
            ],
            out_specs=[
                pl.BlockSpec((length, PART), column),
                pl.BlockSpec((length, PART), column),
                whole(length, D),
                whole(1, D),
            ],
            scratch_shapes=[pltpu.VMEM((length, wide), F32)],
        ),
        out_shape=[
            jax.ShapeDtypeStruct((length, FF), BF16),
            jax.ShapeDtypeStruct((length, FF), BF16),
            jax.ShapeDtypeStruct((length, D), F32),
            jax.ShapeDtypeStruct((1, D), F32),
        ],
        compiler_params=params(),
        cost_estimate=pl.CostEstimate(
            flops=2 * length * wide * 7680, bytes_accessed=22000000, transcendentals=length * FF
        ),
    )(flags, grad, *middles, *gates, *ups, gate_up_mat, gate_up_mat, down_mat, spread, gains)


def gate_grads_kernel(
    flag_ref, grad_ref, gate_a_ref, gate_b_ref, up_a_ref, up_b_ref, down_ref, grad_gate_ref, grad_up_ref
):
    first = flag_ref[0] == 1
    gate = jnp.where(first, gate_a_ref[...], gate_b_ref[...])
    up = jnp.where(first, up_a_ref[...], up_b_ref[...])
    grad_act = dot_t(grad_ref[...], down_ref[...])
    sig = 1.0 / (1.0 + jnp.exp(-gate))
    grad_gate_ref[...] = (grad_act * up * sig * (1.0 + gate * (1.0 - sig))).astype(BF16)
    grad_up_ref[...] = (grad_act * gate * sig).astype(BF16)


def gate_grads(flags, grad, gates, ups, down_mat):
    length = grad.shape[0]
    column = lambda i, flag: (0, i)
    chosen = pl.BlockSpec((length, PART), lambda i, flag: (0, i * flag[0]))
    other = pl.BlockSpec((length, PART), lambda i, flag: (0, i * (1 - flag[0])))
    return pl.pallas_call(
        gate_grads_kernel,
        grid_spec=pltpu.PrefetchScalarGridSpec(
            num_scalar_prefetch=1,
            grid=(PARTS,),
            in_specs=[
                whole(length, D),
                chosen,
                other,
                chosen,
                other,
                pl.BlockSpec((PART, D), lambda i, flag: (i, 0)),
            ],
            out_specs=[pl.BlockSpec((length, PART), column)] * 2,
        ),
        out_shape=[jax.ShapeDtypeStruct((length, FF), BF16)] * 2,
        compiler_params=params(),
        cost_estimate=pl.CostEstimate(
            flops=2 * length * D * FF, bytes_accessed=9000000, transcendentals=length * FF
        ),
    )(flags, grad, *gates, *ups, down_mat)


def middle_grad_kernel(
    flag_ref, grad_ref, middle_a_ref, middle_b_ref, grad_gate_ref, grad_up_ref,
    gate_mat_ref, up_mat_ref, spread_ref, gains_ref, grad_middle_ref, gain_ref, sum_ref,
):
    part = pl.program_id(0)
    more = dot_t(grad_gate_ref[...], gate_mat_ref[...]) + dot_t(grad_up_ref[...], up_mat_ref[...])

    @pl.when(part == 0)
    def begin():
        sum_ref[...] = more

    @pl.when(part > 0)
    def go_on():
        sum_ref[...] += more

    @pl.when(part == PARTS - 1)
    def end():
        grad_two = dot_t(sum_ref[...].astype(BF16), spread_ref[...])
        middle = jnp.where(flag_ref[0] == 1, middle_a_ref[...], middle_b_ref[...])
        through, gain = scaled_backward(middle, gains_ref[1:2], grad_two)
        grad_middle_ref[...] = grad_ref[...].astype(F32) + through
        gain_ref[...] = gain


def middle_grad(flags, grad, middles, grad_gate, grad_up, gate_up_mat, spread, gains):
    length = grad.shape[0]
    wide = N_DP * PAD
    column = lambda i, flag: (0, i)
    return pl.pallas_call(
        middle_grad_kernel,
        grid_spec=pltpu.PrefetchScalarGridSpec(
            num_scalar_prefetch=1,
            grid=(PARTS,),
            in_specs=[
                whole(length, D),
                whole(length, D),
                whole(length, D),
                pl.BlockSpec((length, PART), column),
                pl.BlockSpec((length, PART), column),
                pl.BlockSpec((wide, PART), column),
                pl.BlockSpec((wide, PART), lambda i, flag: (0, i + PARTS)),
                whole(D, wide),
                whole(2, D),
            ],
            out_specs=[whole(length, D), whole(1, D)],
            scratch_shapes=[pltpu.VMEM((length, wide), F32)],
        ),
        out_shape=[
            jax.ShapeDtypeStruct((length, D), F32),
            jax.ShapeDtypeStruct((1, D), F32),
        ],
        compiler_params=params(),
        cost_estimate=pl.CostEstimate(
            flops=2 * length * wide * 5120, bytes_accessed=14000000, transcendentals=0
        ),
    )(flags, grad, *middles, grad_gate, grad_up, gate_up_mat, gate_up_mat, spread, gains)


def attend_backward_kernel(
    flag_ref, grad_ref, own_ref, got_ref, heads_a_ref, heads_b_ref, mask_ref, spread_ref, mat_ref,
    gains_ref, cosine_ref, sine_ref, grad_proj_ref, grad_attn_ref, grad_in_ref, gain_ref,
):
    first = flag_ref[0] == 1
    spread = spread_ref[...]
    grad_middle = grad_ref[...]
    grad_attn = grad_middle.astype(BF16)
    length = grad_middle.shape[0]
    grad_attn_ref[:, :D] = grad_attn
    grad_attn_ref[:, D:] = jnp.zeros((length, OUT_PAD - D), BF16)
    grad_mixed = dot_t(grad_attn, mat_ref[:, QKV_PAD : QKV_PAD + D]).astype(BF16)
    grad_mixed = dot_t(grad_mixed, spread)
    heads = jnp.where(first, heads_a_ref[...].astype(F32), heads_b_ref[...].astype(F32))
    mask = jnp.concatenate([mask_ref[0]] * (H // KV), 0)
    grad_queries, grad_keys, grad_values = [], [], []
    for group in range(KV):
        queries = group_rows(heads, group)
        keys = head_columns(heads, H + group).astype(BF16)
        values = head_columns(heads, H + KV + group).astype(BF16)
        mixed = group_rows(grad_mixed, group)
        probs = probabilities(queries, keys, mask)
        grad_probs = dot_t(mixed, values)
        grad_scores = probs * (grad_probs - jnp.sum(grad_probs * probs, axis=-1, keepdims=True))
        grad_scores = grad_scores.astype(BF16)
        queries_part = dot(grad_scores, keys) * SCALE
        grad_queries += [queries_part[j * length : j * length + length] for j in range(H // KV)]
        grad_keys.append(across(grad_scores, queries) * SCALE)
        grad_values.append(across(probs.astype(BF16), mixed))
    turned = jnp.concatenate(grad_queries + grad_keys, 1).astype(BF16).astype(F32)
    tiles = turn_heads(turned, cosine_ref[...], -sine_ref[...])
    blank = jnp.zeros((length, QKV_PAD - QKV), F32)
    grad_proj = jnp.concatenate(tiles + grad_values + [blank], 1).astype(BF16)
    grad_proj_ref[...] = grad_proj
    grad_one = dot_t(grad_proj, mat_ref[:, :QKV_PAD]).astype(BF16)
    grad_one = dot_t(grad_one, spread)
    stream = jnp.where(first, own_ref[0].astype(F32), got_ref[...].astype(F32))
    through, gain = scaled_backward(stream, gains_ref[0:1], grad_one)
    grad_in_ref[...] = (grad_middle + through).astype(BF16)
    gain_ref[...] = gain


def attend_backward(flags, grad, inputs, got, heads, masks, spread, mat, gains, cosine, sine):
    length = grad.shape[0]
    wide = N_DP * PAD
    return pl.pallas_call(
        attend_backward_kernel,
        grid_spec=pltpu.PrefetchScalarGridSpec(
            num_scalar_prefetch=1,
            grid=(1,),
            in_specs=[
                whole(length, D),
                pl.BlockSpec((1, length, D), lambda i, flag: (flag[1], 0, 0)),
                whole(length, D),
                whole(length, QKV_PAD),
                whole(length, QKV_PAD),
                pl.BlockSpec((1, length, length), lambda i, flag: (flag[1], 0, 0)),
                whole(D, wide),
                whole(wide, QKV_PAD + OUT_PAD),
                whole(2, D),
                whole(length, LANES),
                whole(length, LANES),
            ],
            out_specs=[
                whole(length, QKV_PAD),
                whole(length, OUT_PAD),
                whole(length, D),
                whole(1, D),
            ],
        ),
        out_shape=[
            jax.ShapeDtypeStruct((length, QKV_PAD), BF16),
            jax.ShapeDtypeStruct((length, OUT_PAD), BF16),
            jax.ShapeDtypeStruct((length, D), BF16),
            jax.ShapeDtypeStruct((1, D), F32),
        ],
        compiler_params=params(),
        cost_estimate=pl.CostEstimate(
            flops=2 * length * wide * 6700, bytes_accessed=9000000, transcendentals=H * length * length
        ),
    )(flags, grad, inputs, got, *heads, masks, spread, mat, gains, cosine, sine)


def as_blocks(rows):
    return rows.reshape(N_DP // 2, -1, rows.shape[-1])


def per_device(
    inputs, segment_ids, qkv_weight, out_weight, gate_up_weight, down_weight, norm_gains, cotangent
):
    batches = inputs.shape[0]
    is_first = lax.axis_index("section") == 0
    order = block_order()
    spread = placement(order)
    attn_shard = jnp.concatenate(
        [
            qkv_weight[0],
            norm_gains[0],
            jnp.zeros((ROWS, QKV_PAD - QKV - 2), BF16),
            out_weight[0],
            jnp.zeros((ROWS, OUT_PAD - D), BF16),
        ],
        1,
    )
    widths = (QKV_PAD + OUT_PAD, 2 * FF)
    down_shard = jnp.pad(down_weight[0], ((0, 0), (0, OUT_PAD - D))).reshape(PAD, -1)
    rows = jnp.concatenate(
        [
            jnp.pad(attn_shard, ((0, 1), (0, 0))),
            jnp.pad(gate_up_weight[0], ((0, 1), (0, 0))),
            down_shard,
        ],
        1,
    )
    near = gather_near(rows)
    near_attn = near[:, :, : widths[0]]
    near_gate_up = near[:, :, widths[0] : widths[0] + widths[1]]
    near_down = near[:, :, widths[0] + widths[1] :].reshape(8, FROWS, OUT_PAD)[:, :, :D]
    gate_up_flow = Flow(gather_far(near_gate_up))
    attn_flow = Flow(gather_far(after(near_attn, near_gate_up)))
    spread = step([attn_flow], spread)
    spread, near_down = step([gate_up_flow], (spread, near_down))
    down_flow = Flow(gather_far(near_down))
    for group in ([attn_flow], [gate_up_flow], [attn_flow], [down_flow], [gate_up_flow], [down_flow]):
        spread = step(group, spread)
    spread = step([down_flow], spread)
    attn_mat, gate_up_mat, down_mat = attn_flow.result, gate_up_flow.result, down_flow.result
    attn_mat = attn_mat.reshape(N_DP * PAD, -1)
    gate_up_mat = gate_up_mat.reshape(N_DP * PAD, -1)
    down_mat = reorder(down_mat, order, True).reshape(FF, D)
    gains_full = lax.dot_general(
        attn_mat[:, QKV : QKV + 2], spread, (((0,), (1,)), ((), ())), preferred_element_type=F32
    )
    length = inputs.shape[1]
    cosine, sine = rope_tables(length)
    positions = jnp.arange(length)
    masks = (
        (segment_ids[:, :, None] == segment_ids[:, None, :])
        & (positions[:, None] >= positions[None, :])[None]
    ).astype(F32)
    first = is_first.astype(jnp.int32)

    def flags(for_first, for_second):
        return jnp.stack([first, jnp.where(is_first, for_first, for_second)])

    received = jnp.zeros(inputs.shape[1:], BF16)
    saved = []
    produced = []
    arrivals = []
    for turn in range(batches + 1):
        arrivals.append(received)
        hidden, heads, mixed, middle, second = attend_forward(
            flags(min(turn, batches - 1), max(turn - 1, 0)),
            inputs, received, masks, spread, attn_mat, gains_full, cosine, sine,
        )
        gate, up, act, layer_out = mlp_forward(second, middle, gate_up_mat, down_mat)
        saved.append((hidden, heads, mixed, middle, second, gate, up, act))
        produced.append(layer_out)
        if turn < batches:
            received = shifted(layer_out, "section", 1)
    section_outputs = jnp.stack(
        [
            jnp.where(is_first, produced[position], produced[position + 1])
            for position in range(batches)
        ]
    )[None]
    received = jnp.zeros(inputs.shape[1:], BF16)
    places = jnp.sum(
        jnp.where(order[:, None] == jnp.arange(N_DP)[None, :], jnp.arange(N_DP)[:, None], 0), 0
    ).astype(jnp.int32)

    def lefts(member):
        return jnp.concatenate(
            [jnp.where(is_first, saved[b][member], saved[b + 1][member]) for b in range(batches)], 0
        )

    def rights(turns):
        return jnp.concatenate(
            [jnp.where(is_first, turns[b + 1], turns[b]) for b in range(batches)], 0
        )

    returned = []
    downs = []
    gates = []
    ups = []
    projs = []
    attns = []
    gain_sum = 0
    flows = {}
    gate_up_own = []
    attn_own = []
    for turn in range(batches + 1):
        last = turn == batches
        if turn < batches:
            own_grad = cotangent[turn]
        else:
            own_grad = jnp.zeros(inputs.shape[1:], BF16)
        grad_out = jnp.where(is_first, received, own_grad)
        downs.append(grad_out)
        if last:
            blocks = down_sums(lefts(7), rights(downs), places)
            grad_out = after(grad_out, blocks)
            down_own, down_other = blocks
            flows["down"] = Flow(full_scatter(down_other, lambda: down_own))
        kept_first, kept_second = saved[max(turn - 1, 0)], saved[min(turn + 1, batches)]
        chosen = flags(max(turn - 1, 0), min(turn, batches - 1))

        def both(member):
            return (kept_first[member], kept_second[member])

        if not last:
            grad_gate, grad_up, grad_middle, gain_two = mlp_backward(
                chosen, grad_out, both(3), both(5), both(6), gate_up_mat, down_mat, spread, gains_full
            )
            gates.append(grad_gate)
            ups.append(grad_up)
        else:
            grad_gate, grad_up = gate_grads(chosen, grad_out, both(5), both(6), down_mat)
            gates.append(grad_gate)
            ups.append(grad_up)
            terms = (lefts(4), rights(gates), rights(ups))
            other = gate_up_sums(*terms, 1)
            other = step([flows["down"]], other)
            flows["gate_up"] = Flow(
                full_scatter(as_blocks(other), lambda: as_blocks(gate_up_own[0]))
            )
            gate_up_own.append(gate_up_sums(*after(terms, other), 0))
            grad_gate, grad_up = after((grad_gate, grad_up), gate_up_own[0])
            grad_middle, gain_two = middle_grad(
                chosen, grad_out, both(3), grad_gate, grad_up, gate_up_mat, spread, gains_full
            )
            grad_middle = step([flows["down"], flows["gate_up"]], grad_middle)
        grad_proj, grad_attn, grad_in, gain_one = attend_backward(
            chosen, grad_middle, inputs, arrivals[min(turn + 1, batches)], both(1), masks, spread,
            attn_mat, gains_full, cosine, sine,
        )
        projs.append(grad_proj)
        attns.append(grad_attn)
        gain_sum = gain_sum + jnp.concatenate([gain_one, gain_two], 0)
        returned.append(grad_in)
        if turn < batches:
            received = shifted(grad_in, "section", -1)
    section_input_grads = jnp.stack(
        [
            jnp.where(is_first, returned[position + 1], returned[position])
            for position in range(batches)
        ]
    )[None]
    gain_high = gain_sum.astype(BF16)
    gain_low = (gain_sum - gain_high.astype(F32)).astype(BF16)
    gain_rows = lax.dot_general(
        spread, jnp.stack([gain_high, gain_low]), (((0,), (2,)), ((), ())), preferred_element_type=F32
    )
    first_lane = QKV - (QKV_PAD - LANES)
    gain_rows = jnp.pad(
        gain_rows[:, 0] + gain_rows[:, 1], ((0, 0), (first_lane, LANES - first_lane - 2))
    )
    terms = (lefts(0), lefts(2), rights(projs), rights(attns), gain_rows)
    other = attn_sums(*terms, 1)
    flows["attn"] = Flow(full_scatter(as_blocks(other), lambda: as_blocks(attn_own[0])))
    attn_own.append(attn_sums(*after(terms, other), 0))
    down_flow, gate_up_flow, attn_flow = flows["down"], flows["gate_up"], flows["attn"]
    waiting = after(section_outputs, attn_own[0])
    for group in (
        [gate_up_flow],
        [attn_flow],
        [down_flow],
        [down_flow],
        [attn_flow],
        [gate_up_flow],
        [down_flow],
        [attn_flow],
        [gate_up_flow, down_flow],
        [attn_flow],
        [gate_up_flow],
        [attn_flow],
        [gate_up_flow, attn_flow],
    ):
        waiting = step(group, waiting)
    section_outputs = waiting
    down_grad, gate_up_grad, attn_grad = down_flow.result, gate_up_flow.result, attn_flow.result
    return (
        section_outputs,
        section_input_grads,
        attn_grad[None, :ROWS, :QKV],
        attn_grad[None, :ROWS, QKV_PAD : QKV_PAD + D],
        gate_up_grad[None, :ROWS],
        down_grad[None],
        attn_grad[None, :ROWS, QKV : QKV + 2],
    )


def solution(mesh):
    in_specs = (
        P(None, "dp", None),
        P(None, "dp"),
        P("section", "dp", None),
        P("section", "dp", None),
        P("section", "dp", None),
        P("section", "dp", None),
        P("section", "dp", None),
        P(None, "dp", None),
    )
    out_specs = (
        P("section", None, "dp", None),
        P("section", None, "dp", None),
        P("section", "dp", None),
        P("section", "dp", None),
        P("section", "dp", None),
        P("section", "dp", None),
        P("section", "dp", None),
    )
    return jax.shard_map(
        per_device, mesh=mesh, in_specs=in_specs, out_specs=out_specs, check_vma=False
    )
```

```python
import jax
import jax.numpy as jnp
from jax import lax
from jax.experimental import pallas as pl
from jax.experimental.pallas import tpu as pltpu
from jax.sharding import PartitionSpec as P

D = 960
H = 15
KV = 5
HD = 64
FF = 2560
QKV = D + 2 * KV * HD
N_DP = 64
ROWS = D // N_DP
PAD = 16
FROWS = FF // N_DP
LANES = 128
QKV_PAD = 1664
OUT_PAD = 1024

EPSILON = 1e-05
ROPE_BASE = 100000.0
BF16 = jnp.bfloat16
F32 = jnp.float32


def place(y, x, z, core):
    return ((y % 4 * 2 + x % 2) * 4 + z % 4) * 2 + core % 2


def route(kind, step):
    pairs = []
    for source in range(N_DP):
        y, x, z, core = source // 16, source // 8 % 2, source // 2 % 4, source % 2
        if kind == "core":
            target = place(y, x, z, core + 1)
        elif kind == "x":
            target = place(y, x + 1, z, core)
        elif (kind == "wide") == (core == 0):
            target = place(y, x, z + step, core)
        else:
            target = place(y + step, x, z, core)
        pairs.append((source, target))
    return pairs


def send(block, kind, step=1):
    return lax.ppermute(block, "dp", route(kind, step))


def total(*terms):
    result = terms[0].astype(F32)
    for term in terms[1:]:
        result = result + term.astype(F32)
    return result


def near_scatter(blocks):
    blocks = yield from ring_scatter((blocks,), "narrow")
    (got,) = yield ((blocks[1], "x"),)
    return total(blocks[0], got)


def ring_scatter(terms, kind):
    terms = [term.reshape((4, term.shape[0] // 4) + term.shape[1:]) for term in terms]
    half = terms[0].shape[1] // 2

    def own(step, part):
        return [term[step, part] for term in terms]

    near, far = slice(0, half), slice(half, None)
    left, right = yield (
        (total(*own(3, near)).astype(BF16), kind, 1),
        (total(*own(3, far)).astype(BF16), kind, -1),
    )
    onward = jnp.concatenate([total(*own(1, near), left), total(*own(1, far))], 0).astype(BF16)
    back = jnp.concatenate([total(*own(2, near)), total(*own(2, far), right)], 0).astype(BF16)
    left, right = yield ((onward, kind, 1), (back, kind, -1))
    return total(*[term[0] for term in terms], left, right).astype(BF16)


def far_scatter(for_other, for_own):
    (got,) = yield ((for_other, "core"),)
    return (yield from ring_scatter((for_own(), got), "wide"))


def full_scatter(for_other, for_own):
    blocks = yield from far_scatter(for_other, for_own)
    return (yield from near_scatter(blocks))


class Flow:
    def __init__(self, stages):
        self.stages = stages
        self.result = None
        self.wanted = next(stages)
        self.launch(tuple(request[0] for request in self.wanted))

    def launch(self, blocks):
        self.pending = tuple(
            send(block, *request[1:]) for block, request in zip(blocks, self.wanted)
        )

    def advance(self, arrived):
        try:
            self.wanted = self.stages.send(arrived)
        except StopIteration as end:
            self.wanted = ()
            self.result = end.value


def step(flows, value):
    flows = [flow for flow in flows if flow.result is None]
    arrived, value = lax.optimization_barrier((tuple(flow.pending for flow in flows), value))
    for flow, got in zip(flows, arrived):
        flow.advance(got)
    blocks = tuple(tuple(request[0] for request in flow.wanted) for flow in flows)
    blocks, value = lax.optimization_barrier((blocks, value))
    for flow, ready in zip(flows, blocks):
        flow.launch(ready)
    return value


def ring_gather(block, kind):
    half = block.shape[0] // 2
    from_left = send(block, kind, 1)
    from_right = send(block, kind, -1)
    far_left = send(from_left[:half], kind, 1)
    far_right = send(from_right[half:], kind, -1)
    sides = jnp.concatenate([from_right, from_left], 0)
    return [block, sides, jnp.concatenate([far_left, far_right], 0)]


def gather_near(shard):
    block = jnp.stack([shard, send(shard, "x")], 0)
    return jnp.concatenate(ring_gather(block, "narrow"), 0)


def gather_far(block):
    half = block.shape[0] // 2
    others = send(block, "core")
    left, right = yield ((block, "wide", 1), (block, "wide", -1))
    sides = [right, left]
    sides_there = send(jnp.concatenate(sides, 0), "core")
    far = yield ((left[:half], "wide", 1), (right[half:], "wide", -1))
    far_there = send(jnp.concatenate(far, 0), "core")
    return [block, *sides, *far, others, sides_there, far_there]


def assemble_kernel(*refs):
    pieces, out_ref, sems = refs[:-2], refs[-2], refs[-1]
    copies = []
    start = 0
    for index, piece in enumerate(pieces):
        rows = piece.shape[0]
        copies.append(pltpu.make_async_copy(piece, out_ref.at[start : start + rows], sems.at[index]))
        start += rows
    for copy in copies:
        copy.start()
    for copy in copies:
        copy.wait()


def assemble(pieces):
    pieces = [piece.reshape(-1, piece.shape[-1]) for piece in pieces]
    columns = pieces[0].shape[1]
    return pl.pallas_call(
        assemble_kernel,
        in_specs=[pl.BlockSpec(memory_space=pl.ANY)] * len(pieces),
        out_specs=pl.BlockSpec(memory_space=pltpu.VMEM),
        out_shape=pltpu.VMEM((N_DP * PAD, columns), BF16),
        scratch_shapes=[pltpu.SemaphoreType.DMA((len(pieces),))],
        compiler_params=pltpu.CompilerParams(vmem_limit_bytes=VMEM_BYTES),
    )(*pieces)


def after(value, earlier):
    return lax.optimization_barrier((value, earlier))[0]


def block_order():
    index = lax.axis_index("dp")
    y, x, z, core = index // 16, index // 8 % 2, index // 2 % 4, index % 2
    position = jnp.arange(N_DP)
    core_step, wide, narrow, x_step = position // 32, position // 8 % 4, position // 2 % 4, position % 2
    wide, narrow = wide ^ (wide // 2), narrow ^ (narrow // 2)
    core_there = (core + core_step) % 2
    z_step = jnp.where(core_there == 0, wide, narrow)
    y_step = jnp.where(core_there == 0, narrow, wide)
    return (((y + y_step) % 4 * 2 + (x + x_step) % 2) * 4 + (z + z_step) % 4) * 2 + core_there


def placement(order):
    column = jnp.arange(N_DP * PAD)
    inner = column % PAD
    row = jnp.where(inner < ROWS, jnp.repeat(order, PAD) * ROWS + inner, -1)
    return (jnp.arange(D)[:, None] == row[None, :]).astype(BF16)


def reorder_kernel(scatter, order_ref, blocks_ref, out_ref):
    def one(step, carry):
        there = order_ref[step]
        if scatter:
            out_ref[there] = blocks_ref[step]
        else:
            out_ref[step] = blocks_ref[there]
        return carry

    lax.fori_loop(0, N_DP, one, 0)


def reorder(blocks, order, scatter):
    return pl.pallas_call(
        lambda *refs: reorder_kernel(scatter, *refs),
        out_shape=jax.ShapeDtypeStruct(blocks.shape, blocks.dtype),
        in_specs=[
            pl.BlockSpec(memory_space=pltpu.SMEM),
            pl.BlockSpec(memory_space=pltpu.VMEM),
        ],
        out_specs=pl.BlockSpec(memory_space=pltpu.VMEM),
        compiler_params=pltpu.CompilerParams(vmem_limit_bytes=24 * 1024 * 1024),
    )(order, blocks)


def across(left, right):
    return lax.dot_general(left, right, (((0,), (0,)), ((), ())), preferred_element_type=F32)


VMEM_BYTES = 16 * 1024 * 1024


def down_kernel(place_ref, left_ref, right_ref, own_ref, other_ref):
    step = pl.program_id(0)
    rows = across(left_ref[...], right_ref[...]).astype(BF16)
    count = rows.shape[0] // FROWS
    for block in range(count):
        place_here = place_ref[step * count + block]
        part = rows[block * FROWS : (block + 1) * FROWS]

        @pl.when(place_here < N_DP // 2)
        def keep():
            own_ref[place_here] = part

        @pl.when(place_here >= N_DP // 2)
        def give():
            other_ref[place_here - N_DP // 2] = part


def down_sums(left, right, places):
    tokens = left.shape[0]
    width = 640
    return pl.pallas_call(
        down_kernel,
        grid=(FF // width,),
        out_shape=[jax.ShapeDtypeStruct((N_DP // 2, FROWS, D), BF16)] * 2,
        in_specs=[
            pl.BlockSpec(memory_space=pltpu.SMEM),
            pl.BlockSpec((tokens, width), lambda i: (0, i)),
            pl.BlockSpec((tokens, D), lambda i: (0, 0)),
        ],
        out_specs=[pl.BlockSpec((N_DP // 2, FROWS, D), lambda i: (0, 0, 0))] * 2,
        compiler_params=pltpu.CompilerParams(vmem_limit_bytes=VMEM_BYTES),
        cost_estimate=pl.CostEstimate(
            flops=2 * tokens * FF * D, bytes_accessed=2 * FF * D, transcendentals=0
        ),
    )(places, left, right)


def gate_up_kernel(left_ref, gate_ref, up_ref, out_ref):
    left = left_ref[...]
    out_ref[:, :FF] = across(left, gate_ref[...]).astype(BF16)
    out_ref[:, FF:] = across(left, up_ref[...]).astype(BF16)


def gate_up_sums(left, gate, up, first):
    tokens = left.shape[0]
    columns = 2 * FF
    width = 128
    count = N_DP * PAD // 2 // width
    return pl.pallas_call(
        gate_up_kernel,
        grid=(count,),
        out_shape=jax.ShapeDtypeStruct((N_DP * PAD // 2, columns), BF16),
        in_specs=[
            pl.BlockSpec((tokens, width), lambda i: (0, i + first * count)),
            pl.BlockSpec((tokens, FF), lambda i: (0, 0)),
            pl.BlockSpec((tokens, FF), lambda i: (0, 0)),
        ],
        out_specs=pl.BlockSpec((width, columns), lambda i: (i, 0)),
        compiler_params=pltpu.CompilerParams(vmem_limit_bytes=VMEM_BYTES),
        cost_estimate=pl.CostEstimate(
            flops=tokens * N_DP * PAD * columns, bytes_accessed=N_DP * PAD * columns, transcendentals=0
        ),
    )(left, gate, up)


def attn_kernel(left_ref, mixed_ref, proj_ref, attn_ref, gain_ref, out_ref):
    qkv = across(left_ref[...], proj_ref[...])
    edge = QKV_PAD - LANES
    out_ref[:, :edge] = qkv[:, :edge].astype(BF16)
    out_ref[:, edge:QKV_PAD] = (qkv[:, edge:] + gain_ref[...]).astype(BF16)
    out_ref[:, QKV_PAD:] = across(mixed_ref[...], attn_ref[...]).astype(BF16)


def attn_sums(left, mixed, proj, attn, gain, first):
    tokens = left.shape[0]
    width = 128
    count = N_DP * PAD // 2 // width
    columns = QKV_PAD + OUT_PAD
    return pl.pallas_call(
        attn_kernel,
        grid=(count,),
        out_shape=jax.ShapeDtypeStruct((N_DP * PAD // 2, columns), BF16),
        in_specs=[
            pl.BlockSpec((tokens, width), lambda i: (0, i + first * count)),
            pl.BlockSpec((tokens, width), lambda i: (0, i + first * count)),
            pl.BlockSpec((tokens, QKV_PAD), lambda i: (0, 0)),
            pl.BlockSpec((tokens, OUT_PAD), lambda i: (0, 0)),
            pl.BlockSpec((width, LANES), lambda i: (i + first * count, 0)),
        ],
        out_specs=pl.BlockSpec((width, columns), lambda i: (i, 0)),
        compiler_params=pltpu.CompilerParams(vmem_limit_bytes=VMEM_BYTES),
        cost_estimate=pl.CostEstimate(
            flops=tokens * N_DP * PAD * columns, bytes_accessed=N_DP * PAD * columns, transcendentals=0
        ),
    )(left, mixed, proj, attn, gain)


def dot(left, right):
    return jnp.dot(left, right, preferred_element_type=F32)


def dot_t(left, right):
    return lax.dot_general(left, right, (((1,), (1,)), ((), ())), preferred_element_type=F32)


def shifted(block, axis, distance):
    devices = range(lax.axis_size(axis))
    pairs = [(i - distance, i) for i in devices if i - distance in devices]
    return lax.ppermute(block, axis, pairs)


def rope_tables(length):
    position = jnp.arange(length, dtype=F32)[:, None]
    frequency = ROPE_BASE ** (-jnp.arange(0, HD, 2, dtype=F32) / HD)
    angle = position * frequency[None, :]
    cosine, sine = jnp.cos(angle), jnp.sin(angle)
    return (jnp.tile(cosine, (1, LANES // (HD // 2))), jnp.tile(jnp.concatenate([-sine, sine], 1), (1, LANES // HD)))


SCALE = HD**-0.5
TURNED = D + KV * HD
PARTS = 5
PART = FF // PARTS
KEPT = jnp.bfloat16


def params():
    return pltpu.CompilerParams(vmem_limit_bytes=VMEM_BYTES)


def local_call(kernel, outs, cost, *operands):
    flops, moved, transcendentals = cost
    specs = [pl.BlockSpec(memory_space=pltpu.VMEM)] * (len(operands) - 1)
    return pl.pallas_call(
        kernel,
        in_specs=[pl.BlockSpec(memory_space=pltpu.SMEM)] + specs,
        out_specs=[pl.BlockSpec(memory_space=pltpu.VMEM)] * len(outs),
        out_shape=[jax.ShapeDtypeStruct(shape, dtype) for shape, dtype in outs],
        compiler_params=params(),
        cost_estimate=pl.CostEstimate(
            flops=flops, bytes_accessed=moved, transcendentals=transcendentals
        ),
    )(*operands)


def scaled(value, gain):
    return value * lax.rsqrt(jnp.mean(value * value, axis=-1, keepdims=True) + EPSILON) * gain


def scaled_backward(value, gain, grad):
    inverse = lax.rsqrt(jnp.mean(value * value, axis=-1, keepdims=True) + EPSILON)
    normed = value * inverse
    inner = grad * gain
    gain_sum = jnp.sum(grad * normed, axis=0, keepdims=True)
    through = inverse * (inner - normed * jnp.mean(inner * normed, axis=-1, keepdims=True))
    return (through, gain_sum)


def turn_heads(value, cosine, sine):
    first = lax.broadcasted_iota(jnp.int32, cosine.shape, 1) % HD < HD // 2
    tiles = []
    for start in range(0, TURNED, LANES):
        tile = value[:, start : start + LANES]
        other = jnp.where(first, pltpu.roll(tile, LANES - HD // 2, 1), pltpu.roll(tile, HD // 2, 1))
        tiles.append(tile * cosine + other * sine)
    return tiles


def head_columns(value, index):
    return value[:, index * HD : index * HD + HD]


def group_rows(value, group):
    return jnp.concatenate(
        [head_columns(value, group * (H // KV) + j) for j in range(H // KV)], 0
    ).astype(BF16)


def probabilities(queries, keys, mask):
    scores = jnp.where(mask > 0, dot_t(queries, keys) * SCALE, -1000000000.0)
    terms = jnp.exp(scores - jnp.max(scores, axis=-1, keepdims=True))
    return terms / jnp.sum(terms, axis=-1, keepdims=True)


def attend_forward_kernel(
    flag_ref, own_ref, got_ref, mask_ref, spread_ref, mat_ref, gains_ref, cosine_ref, sine_ref,
    hidden_ref, heads_ref, mixed_ref, middle_ref, second_ref,
):
    first = flag_ref[0] == 1
    stream = jnp.where(first, own_ref[flag_ref[1]].astype(F32), got_ref[...].astype(F32))
    spread = spread_ref[...]
    gains = gains_ref[...]
    hidden = dot(scaled(stream, gains[0:1]).astype(BF16), spread).astype(BF16)
    hidden_ref[...] = hidden
    projected = dot(hidden, mat_ref[:, :QKV_PAD])
    tiles = turn_heads(projected, cosine_ref[...], sine_ref[...])
    for index, tile in enumerate(tiles):
        heads_ref[:, index * LANES : index * LANES + LANES] = tile.astype(BF16)
    heads_ref[:, TURNED:] = projected[:, TURNED:].astype(BF16)
    turned = jnp.concatenate(tiles, 1)
    mask = jnp.concatenate([mask_ref[flag_ref[1]]] * (H // KV), 0)
    length = stream.shape[0]
    outs = []
    for group in range(KV):
        queries = group_rows(turned, group)
        keys = head_columns(turned, H + group).astype(BF16)
        values = head_columns(projected, H + KV + group).astype(BF16)
        mixed = dot(probabilities(queries, keys, mask).astype(BF16), values)
        outs += [mixed[j * length : j * length + length] for j in range(H // KV)]
    mixed = dot(jnp.concatenate(outs, 1).astype(BF16), spread).astype(BF16)
    mixed_ref[...] = mixed
    middle = stream + dot(mixed, mat_ref[:, QKV_PAD:])[:, :D]
    middle_ref[...] = middle
    second_ref[...] = dot(scaled(middle, gains[1:2]).astype(BF16), spread).astype(BF16)


def attend_forward(flags, inputs, got, masks, spread, mat, gains, cosine, sine):
    length = got.shape[0]
    wide = N_DP * PAD
    outs = [
        ((length, wide), BF16),
        ((length, QKV_PAD), BF16),
        ((length, wide), BF16),
        ((length, D), F32),
        ((length, wide), BF16),
    ]
    cost = (2 * length * wide * 5700, 8000000, H * length * length)
    return local_call(
        attend_forward_kernel, outs, cost, flags, inputs, got, masks, spread, mat, gains, cosine, sine
    )


def mlp_forward_kernel(
    flag_ref, second_ref, middle_ref, mat_ref, down_ref, gate_ref, up_ref, act_ref, out_ref
):
    second = second_ref[...]
    out = middle_ref[...]
    for start in range(0, FF, PART):
        here = slice(start, start + PART)
        gate = dot(second, mat_ref[:, here])
        up = dot(second, mat_ref[:, FF + start : FF + start + PART])
        gate_ref[:, here] = gate.astype(KEPT)
        up_ref[:, here] = up.astype(KEPT)
        act = (gate / (1.0 + jnp.exp(-gate)) * up).astype(BF16)
        act_ref[:, here] = act
        out = out + dot(act, down_ref[here, :])
    out_ref[...] = out.astype(BF16)


def mlp_forward(flags, second, middle, gate_up_mat, down_mat):
    length, wide = second.shape
    outs = [((length, FF), KEPT), ((length, FF), KEPT), ((length, FF), BF16), ((length, D), BF16)]
    cost = (2 * length * wide * 7680, 20000000, length * FF)
    return local_call(
        mlp_forward_kernel, outs, cost, flags, second, middle, gate_up_mat, down_mat
    )


def gate_grads_part(first, grad, gates, ups, down, here):
    gate = jnp.where(first, gates[0][:, here].astype(F32), gates[1][:, here].astype(F32))
    up = jnp.where(first, ups[0][:, here].astype(F32), ups[1][:, here].astype(F32))
    grad_act = dot_t(grad, down[here, :])
    sig = 1.0 / (1.0 + jnp.exp(-gate))
    grad_gate = (grad_act * up * sig * (1.0 + gate * (1.0 - sig))).astype(BF16)
    return (grad_gate, (grad_act * gate * sig).astype(BF16))


def middle_part(first, grad, middles, total_two, spread, gains):
    grad_two = dot_t(total_two.astype(BF16), spread)
    middle = jnp.where(first, middles[0][...], middles[1][...])
    through, gain = scaled_backward(middle, gains[1:2], grad_two)
    return (grad.astype(F32) + through, gain)


def mlp_backward_kernel(
    flag_ref, grad_ref, middle_a_ref, middle_b_ref, gate_a_ref, gate_b_ref, up_a_ref, up_b_ref,
    mat_ref, down_ref, spread_ref, gains_ref,
    grad_gate_ref, grad_up_ref, grad_middle_ref, gain_ref,
):
    first = flag_ref[0] == 1
    grad = grad_ref[...]
    total_two = 0
    for start in range(0, FF, PART):
        here = slice(start, start + PART)
        grad_gate, grad_up = gate_grads_part(
            first, grad, (gate_a_ref, gate_b_ref), (up_a_ref, up_b_ref), down_ref, here
        )
        grad_gate_ref[:, here] = grad_gate
        grad_up_ref[:, here] = grad_up
        total_two += dot_t(grad_gate, mat_ref[:, here])
        total_two += dot_t(grad_up, mat_ref[:, FF + start : FF + start + PART])
    grad_middle_ref[...], gain_ref[...] = middle_part(
        first, grad, (middle_a_ref, middle_b_ref), total_two, spread_ref[...], gains_ref[...]
    )


def mlp_backward(flags, grad, middles, gates, ups, gate_up_mat, down_mat, spread, gains):
    length = grad.shape[0]
    outs = [((length, FF), BF16), ((length, FF), BF16), ((length, D), F32), ((1, D), F32)]
    cost = (2 * length * N_DP * PAD * 7680, 22000000, length * FF)
    return local_call(
        mlp_backward_kernel, outs, cost,
        flags, grad, *middles, *gates, *ups, gate_up_mat, down_mat, spread, gains,
    )


def gate_grads_kernel(
    flag_ref, grad_ref, gate_a_ref, gate_b_ref, up_a_ref, up_b_ref, down_ref, grad_gate_ref, grad_up_ref
):
    first = flag_ref[0] == 1
    for start in range(0, FF, PART):
        here = slice(start, start + PART)
        grad_gate_ref[:, here], grad_up_ref[:, here] = gate_grads_part(
            first, grad_ref[...], (gate_a_ref, gate_b_ref), (up_a_ref, up_b_ref), down_ref, here
        )


def gate_grads(flags, grad, gates, ups, down_mat):
    length = grad.shape[0]
    outs = [((length, FF), BF16), ((length, FF), BF16)]
    cost = (2 * length * D * FF, 9000000, length * FF)
    return local_call(gate_grads_kernel, outs, cost, flags, grad, *gates, *ups, down_mat)


def middle_grad_kernel(
    flag_ref, grad_ref, middle_a_ref, middle_b_ref, grad_gate_ref, grad_up_ref,
    mat_ref, spread_ref, gains_ref, grad_middle_ref, gain_ref,
):
    total_two = dot_t(grad_gate_ref[...], mat_ref[:, :FF]) + dot_t(grad_up_ref[...], mat_ref[:, FF:])
    grad_middle_ref[...], gain_ref[...] = middle_part(
        flag_ref[0] == 1, grad_ref[...], (middle_a_ref, middle_b_ref), total_two, spread_ref[...],
        gains_ref[...],
    )


def middle_grad(flags, grad, middles, grad_gate, grad_up, gate_up_mat, spread, gains):
    length = grad.shape[0]
    outs = [((length, D), F32), ((1, D), F32)]
    cost = (2 * length * N_DP * PAD * 5120, 14000000, 0)
    return local_call(
        middle_grad_kernel, outs, cost,
        flags, grad, *middles, grad_gate, grad_up, gate_up_mat, spread, gains,
    )


def attend_backward_kernel(
    flag_ref, grad_ref, own_ref, got_ref, heads_a_ref, heads_b_ref, mask_ref, spread_ref, mat_ref,
    gains_ref, cosine_ref, sine_ref, grad_proj_ref, grad_attn_ref, grad_in_ref, gain_ref,
):
    first = flag_ref[0] == 1
    spread = spread_ref[...]
    grad_middle = grad_ref[...]
    grad_attn = grad_middle.astype(BF16)
    length = grad_middle.shape[0]
    grad_attn_ref[:, :D] = grad_attn
    grad_attn_ref[:, D:] = jnp.zeros((length, OUT_PAD - D), BF16)
    grad_mixed = dot_t(grad_attn, mat_ref[:, QKV_PAD : QKV_PAD + D]).astype(BF16)
    grad_mixed = dot_t(grad_mixed, spread)
    heads = jnp.where(first, heads_a_ref[...].astype(F32), heads_b_ref[...].astype(F32))
    mask = jnp.concatenate([mask_ref[flag_ref[1]]] * (H // KV), 0)
    grad_queries, grad_keys, grad_values = [], [], []
    for group in range(KV):
        queries = group_rows(heads, group)
        keys = head_columns(heads, H + group).astype(BF16)
        values = head_columns(heads, H + KV + group).astype(BF16)
        mixed = group_rows(grad_mixed, group)
        probs = probabilities(queries, keys, mask)
        grad_probs = dot_t(mixed, values)
        grad_scores = probs * (grad_probs - jnp.sum(grad_probs * probs, axis=-1, keepdims=True))
        grad_scores = grad_scores.astype(BF16)
        queries_part = dot(grad_scores, keys) * SCALE
        grad_queries += [queries_part[j * length : j * length + length] for j in range(H // KV)]
        grad_keys.append(across(grad_scores, queries) * SCALE)
        grad_values.append(across(probs.astype(BF16), mixed))
    turned = jnp.concatenate(grad_queries + grad_keys, 1).astype(BF16).astype(F32)
    tiles = turn_heads(turned, cosine_ref[...], -sine_ref[...])
    blank = jnp.zeros((length, QKV_PAD - QKV), F32)
    grad_proj = jnp.concatenate(tiles + grad_values + [blank], 1).astype(BF16)
    grad_proj_ref[...] = grad_proj
    grad_one = dot_t(grad_proj, mat_ref[:, :QKV_PAD]).astype(BF16)
    grad_one = dot_t(grad_one, spread)
    stream = jnp.where(first, own_ref[flag_ref[1]].astype(F32), got_ref[...].astype(F32))
    through, gain = scaled_backward(stream, gains_ref[0:1], grad_one)
    grad_in_ref[...] = (grad_middle + through).astype(BF16)
    gain_ref[...] = gain


def attend_backward(flags, grad, inputs, got, heads, masks, spread, mat, gains, cosine, sine):
    length = grad.shape[0]
    wide = N_DP * PAD
    outs = [
        ((length, QKV_PAD), BF16),
        ((length, OUT_PAD), BF16),
        ((length, D), BF16),
        ((1, D), F32),
    ]
    cost = (2 * length * wide * 6700, 9000000, H * length * length)
    return local_call(
        attend_backward_kernel, outs, cost,
        flags, grad, inputs, got, *heads, masks, spread, mat, gains, cosine, sine,
    )

def as_blocks(rows):
    return rows.reshape(N_DP // 2, -1, rows.shape[-1])


def per_device(
    inputs, segment_ids, qkv_weight, out_weight, gate_up_weight, down_weight, norm_gains, cotangent
):
    batches = inputs.shape[0]
    is_first = lax.axis_index("section") == 0
    order = block_order()
    spread = placement(order)
    attn_shard = jnp.concatenate(
        [
            qkv_weight[0],
            norm_gains[0],
            jnp.zeros((ROWS, QKV_PAD - QKV - 2), BF16),
            out_weight[0],
            jnp.zeros((ROWS, OUT_PAD - D), BF16),
        ],
        1,
    )
    widths = (QKV_PAD + OUT_PAD, 2 * FF)
    down_shard = jnp.pad(down_weight[0], ((0, 0), (0, OUT_PAD - D))).reshape(PAD, -1)
    rows = jnp.concatenate(
        [
            jnp.pad(attn_shard, ((0, 1), (0, 0))),
            jnp.pad(gate_up_weight[0], ((0, 1), (0, 0))),
            down_shard,
        ],
        1,
    )
    near = gather_near(rows)
    near_attn = near[:, :, : widths[0]]
    near_gate_up = near[:, :, widths[0] : widths[0] + widths[1]]
    near_down = near[:, :, widths[0] + widths[1] :].reshape(8, FROWS, OUT_PAD)[:, :, :D]
    gate_up_flow = Flow(gather_far(near_gate_up))
    attn_flow = Flow(gather_far(after(near_attn, near_gate_up)))
    spread = step([attn_flow], spread)
    spread, near_down = step([gate_up_flow], (spread, near_down))
    down_flow = Flow(gather_far(near_down))
    for group in ([attn_flow], [gate_up_flow], [down_flow], [down_flow]):
        spread = step(group, spread)
    attn_mat, gate_up_mat, down_mat = attn_flow.result, gate_up_flow.result, down_flow.result
    gain_rows = jnp.concatenate([piece[:, :, QKV : QKV + 2] for piece in attn_mat], 0)
    gain_rows = gain_rows.reshape(N_DP * PAD, 2)
    attn_mat = assemble(attn_mat)
    gate_up_mat = assemble(gate_up_mat)
    down_mat = reorder(jnp.concatenate(down_mat, 0), order, True).reshape(FF, D)
    gains_full = lax.dot_general(
        gain_rows, spread, (((0,), (1,)), ((), ())), preferred_element_type=F32
    )
    length = inputs.shape[1]
    cosine, sine = rope_tables(length)
    positions = jnp.arange(length)
    masks = (
        (segment_ids[:, :, None] == segment_ids[:, None, :])
        & (positions[:, None] >= positions[None, :])[None]
    ).astype(F32)
    first = is_first.astype(jnp.int32)

    def flags(for_first, for_second):
        return jnp.stack([first, jnp.where(is_first, for_first, for_second)])

    received = jnp.zeros(inputs.shape[1:], BF16)
    saved = []
    produced = []
    arrivals = []
    for turn in range(batches + 1):
        arrivals.append(received)
        hidden, heads, mixed, middle, second = attend_forward(
            flags(min(turn, batches - 1), max(turn - 1, 0)),
            inputs, received, masks, spread, attn_mat, gains_full, cosine, sine,
        )
        gate, up, act, layer_out = mlp_forward(
            flags(0, 0), second, middle, gate_up_mat, down_mat
        )
        saved.append((hidden, heads, mixed, middle, second, gate, up, act))
        produced.append(layer_out)
        if turn < batches:
            received = shifted(layer_out, "section", 1)
    section_outputs = jnp.stack(
        [
            jnp.where(is_first, produced[position], produced[position + 1])
            for position in range(batches)
        ]
    )[None]
    received = jnp.zeros(inputs.shape[1:], BF16)
    places = jnp.sum(
        jnp.where(order[:, None] == jnp.arange(N_DP)[None, :], jnp.arange(N_DP)[:, None], 0), 0
    ).astype(jnp.int32)

    def lefts(member):
        return jnp.concatenate(
            [jnp.where(is_first, saved[b][member], saved[b + 1][member]) for b in range(batches)], 0
        )

    def rights(turns):
        return jnp.concatenate(
            [jnp.where(is_first, turns[b + 1], turns[b]) for b in range(batches)], 0
        )

    returned = []
    downs = []
    gates = []
    ups = []
    projs = []
    attns = []
    gain_sum = 0
    flows = {}
    gate_up_own = []
    attn_own = []
    for turn in range(batches + 1):
        last = turn == batches
        if turn < batches:
            own_grad = cotangent[turn]
        else:
            own_grad = jnp.zeros(inputs.shape[1:], BF16)
        grad_out = jnp.where(is_first, received, own_grad)
        downs.append(grad_out)
        if last:
            blocks = down_sums(lefts(7), rights(downs), places)
            grad_out = after(grad_out, blocks)
            down_own, down_other = blocks
            flows["down"] = Flow(full_scatter(down_other, lambda: down_own))
        kept_first, kept_second = saved[max(turn - 1, 0)], saved[min(turn + 1, batches)]
        chosen = flags(max(turn - 1, 0), min(turn, batches - 1))

        def both(member):
            return (kept_first[member], kept_second[member])

        if not last:
            grad_gate, grad_up, grad_middle, gain_two = mlp_backward(
                chosen, grad_out, both(3), both(5), both(6), gate_up_mat, down_mat, spread, gains_full
            )
            gates.append(grad_gate)
            ups.append(grad_up)
        else:
            grad_gate, grad_up = gate_grads(chosen, grad_out, both(5), both(6), down_mat)
            gates.append(grad_gate)
            ups.append(grad_up)
            terms = (lefts(4), rights(gates), rights(ups))
            other = gate_up_sums(*terms, 1)
            other = step([flows["down"]], other)
            flows["gate_up"] = Flow(
                full_scatter(as_blocks(other), lambda: as_blocks(gate_up_own[0]))
            )
            gate_up_own.append(gate_up_sums(*after(terms, other), 0))
            grad_gate, grad_up = after((grad_gate, grad_up), gate_up_own[0])
            grad_middle, gain_two = middle_grad(
                chosen, grad_out, both(3), grad_gate, grad_up, gate_up_mat, spread, gains_full
            )
            grad_middle = step([flows["down"], flows["gate_up"]], grad_middle)
        grad_proj, grad_attn, grad_in, gain_one = attend_backward(
            chosen, grad_middle, inputs, arrivals[min(turn + 1, batches)], both(1), masks, spread,
            attn_mat, gains_full, cosine, sine,
        )
        if last:
            grad_proj = step([flows["gate_up"], flows["down"]], grad_proj)
        projs.append(grad_proj)
        attns.append(grad_attn)
        gain_sum = gain_sum + jnp.concatenate([gain_one, gain_two], 0)
        returned.append(grad_in)
        if turn < batches:
            received = shifted(grad_in, "section", -1)
    section_input_grads = jnp.stack(
        [
            jnp.where(is_first, returned[position + 1], returned[position])
            for position in range(batches)
        ]
    )[None]
    gain_high = gain_sum.astype(BF16)
    gain_low = (gain_sum - gain_high.astype(F32)).astype(BF16)
    gain_rows = lax.dot_general(
        spread, jnp.stack([gain_high, gain_low]), (((0,), (2,)), ((), ())), preferred_element_type=F32
    )
    first_lane = QKV - (QKV_PAD - LANES)
    gain_rows = jnp.pad(
        gain_rows[:, 0] + gain_rows[:, 1], ((0, 0), (first_lane, LANES - first_lane - 2))
    )
    terms = (lefts(0), lefts(2), rights(projs), rights(attns), gain_rows)
    other = attn_sums(*terms, 1)
    flows["attn"] = Flow(full_scatter(as_blocks(other), lambda: as_blocks(attn_own[0])))
    attn_own.append(attn_sums(*after(terms, other), 0))
    down_flow, gate_up_flow, attn_flow = flows["down"], flows["gate_up"], flows["attn"]
    waiting = after(section_outputs, attn_own[0])
    for group in (
        [attn_flow],
        [down_flow],
        [gate_up_flow],
        [attn_flow],
        [down_flow],
        [gate_up_flow],
        [attn_flow],
        [down_flow],
        [gate_up_flow],
        [attn_flow],
        [down_flow, gate_up_flow],
        [attn_flow],
        [attn_flow],
    ):
        waiting = step(group, waiting)
    section_outputs = waiting
    while min(flow.result is not None for flow in (down_flow, gate_up_flow, attn_flow)) == 0:
        waiting = step([down_flow, gate_up_flow, attn_flow], waiting)
    section_outputs = waiting
    down_grad, gate_up_grad, attn_grad = down_flow.result, gate_up_flow.result, attn_flow.result
    return (
        section_outputs,
        section_input_grads,
        attn_grad[None, :ROWS, :QKV],
        attn_grad[None, :ROWS, QKV_PAD : QKV_PAD + D],
        gate_up_grad[None, :ROWS],
        down_grad[None],
        attn_grad[None, :ROWS, QKV : QKV + 2],
    )


def solution(mesh):
    in_specs = (
        P(None, "dp", None),
        P(None, "dp"),
        P("section", "dp", None),
        P("section", "dp", None),
        P("section", "dp", None),
        P("section", "dp", None),
        P("section", "dp", None),
        P(None, "dp", None),
    )
    out_specs = (
        P("section", None, "dp", None),
        P("section", None, "dp", None),
        P("section", "dp", None),
        P("section", "dp", None),
        P("section", "dp", None),
        P("section", "dp", None),
        P("section", "dp", None),
    )
    return jax.shard_map(
        per_device, mesh=mesh, in_specs=in_specs, out_specs=out_specs, check_vma=False
    )
```

```python
import jax
import jax.numpy as jnp
from jax import lax
from jax.experimental import pallas as pl
from jax.experimental.pallas import tpu as pltpu
from jax.sharding import PartitionSpec as P

D = 960
H = 15
KV = 5
HD = 64
FF = 2560
QKV = D + 2 * KV * HD
N_DP = 64
ROWS = D // N_DP
PAD = 16
FROWS = FF // N_DP
LANES = 128
QKV_PAD = 1664
OUT_PAD = 1024

EPSILON = 1e-05
ROPE_BASE = 100000.0
BF16 = jnp.bfloat16
F32 = jnp.float32


def place(y, x, z, core):
    return ((y % 4 * 2 + x % 2) * 4 + z % 4) * 2 + core % 2


def route(kind, step):
    pairs = []
    for source in range(N_DP):
        y, x, z, core = source // 16, source // 8 % 2, source // 2 % 4, source % 2
        if kind == "core":
            target = place(y, x, z, core + 1)
        elif kind == "x":
            target = place(y, x + 1, z, core)
        elif (kind == "wide") == (core == 0):
            target = place(y, x, z + step, core)
        else:
            target = place(y + step, x, z, core)
        pairs.append((source, target))
    return pairs


def send(block, kind, step=1):
    return lax.ppermute(block, "dp", route(kind, step))


def total(*terms):
    result = terms[0].astype(F32)
    for term in terms[1:]:
        result = result + term.astype(F32)
    return result


def near_scatter(blocks):
    blocks = yield from ring_scatter((blocks,), "narrow")
    (got,) = yield ((blocks[1], "x"),)
    return total(blocks[0], got)


def ring_scatter(terms, kind):
    terms = [term.reshape((4, term.shape[0] // 4) + term.shape[1:]) for term in terms]
    half = terms[0].shape[1] // 2

    def own(step, part):
        return [term[step, part] for term in terms]

    near, far = slice(0, half), slice(half, None)
    left, right = yield (
        (total(*own(3, near)).astype(BF16), kind, 1),
        (total(*own(3, far)).astype(BF16), kind, -1),
    )
    onward = jnp.concatenate([total(*own(1, near), left), total(*own(1, far))], 0).astype(BF16)
    back = jnp.concatenate([total(*own(2, near)), total(*own(2, far), right)], 0).astype(BF16)
    left, right = yield ((onward, kind, 1), (back, kind, -1))
    return total(*[term[0] for term in terms], left, right).astype(BF16)


def far_scatter(for_other, for_own):
    (got,) = yield ((for_other, "core"),)
    return (yield from ring_scatter((for_own(), got), "wide"))


def full_scatter(for_other, for_own):
    blocks = yield from far_scatter(for_other, for_own)
    return (yield from near_scatter(blocks))


class Flow:
    def __init__(self, stages):
        self.stages = stages
        self.result = None
        self.wanted = next(stages)
        self.launch(tuple(request[0] for request in self.wanted))

    def launch(self, blocks):
        self.pending = tuple(
            send(block, *request[1:]) for block, request in zip(blocks, self.wanted)
        )

    def advance(self, arrived):
        try:
            self.wanted = self.stages.send(arrived)
        except StopIteration as end:
            self.wanted = ()
            self.result = end.value


def step(flows, value):
    flows = [flow for flow in flows if flow.result is None]
    arrived, value = lax.optimization_barrier((tuple(flow.pending for flow in flows), value))
    for flow, got in zip(flows, arrived):
        flow.advance(got)
    blocks = tuple(tuple(request[0] for request in flow.wanted) for flow in flows)
    blocks, value = lax.optimization_barrier((blocks, value))
    for flow, ready in zip(flows, blocks):
        flow.launch(ready)
    return value


def ring_gather(block, kind):
    half = block.shape[0] // 2
    from_left = send(block, kind, 1)
    from_right = send(block, kind, -1)
    far_left = send(from_left[:half], kind, 1)
    far_right = send(from_right[half:], kind, -1)
    sides = jnp.concatenate([from_right, from_left], 0)
    return [block, sides, jnp.concatenate([far_left, far_right], 0)]


def gather_near(shard):
    block = jnp.stack([shard, send(shard, "x")], 0)
    return jnp.concatenate(ring_gather(block, "narrow"), 0)


def gather_far(block):
    half = block.shape[0] // 2
    others = send(block, "core")
    left, right = yield ((block, "wide", 1), (block, "wide", -1))
    sides = [right, left]
    sides_there = send(jnp.concatenate(sides, 0), "core")
    far = yield ((left[:half], "wide", 1), (right[half:], "wide", -1))
    far_there = send(jnp.concatenate(far, 0), "core")
    return [block, *sides, *far, others, sides_there, far_there]


def assemble_kernel(*refs):
    pieces, out_ref, sems = refs[:-2], refs[-2], refs[-1]
    copies = []
    start = 0
    for index, piece in enumerate(pieces):
        rows = piece.shape[0]
        copies.append(pltpu.make_async_copy(piece, out_ref.at[start : start + rows], sems.at[index]))
        start += rows
    for copy in copies:
        copy.start()
    for copy in copies:
        copy.wait()


def assemble(pieces):
    pieces = [piece.reshape(-1, piece.shape[-1]) for piece in pieces]
    columns = pieces[0].shape[1]
    return pl.pallas_call(
        assemble_kernel,
        in_specs=[pl.BlockSpec(memory_space=pl.ANY)] * len(pieces),
        out_specs=pl.BlockSpec(memory_space=pltpu.VMEM),
        out_shape=pltpu.VMEM((N_DP * PAD, columns), BF16),
        scratch_shapes=[pltpu.SemaphoreType.DMA((len(pieces),))],
        compiler_params=pltpu.CompilerParams(vmem_limit_bytes=VMEM_BYTES),
    )(*pieces)


def after(value, earlier):
    return lax.optimization_barrier((value, earlier))[0]


def block_order():
    index = lax.axis_index("dp")
    y, x, z, core = index // 16, index // 8 % 2, index // 2 % 4, index % 2
    position = jnp.arange(N_DP)
    core_step, wide, narrow, x_step = position // 32, position // 8 % 4, position // 2 % 4, position % 2
    wide, narrow = wide ^ (wide // 2), narrow ^ (narrow // 2)
    core_there = (core + core_step) % 2
    z_step = jnp.where(core_there == 0, wide, narrow)
    y_step = jnp.where(core_there == 0, narrow, wide)
    return (((y + y_step) % 4 * 2 + (x + x_step) % 2) * 4 + (z + z_step) % 4) * 2 + core_there


def placement(order):
    column = jnp.arange(N_DP * PAD)
    inner = column % PAD
    row = jnp.where(inner < ROWS, jnp.repeat(order, PAD) * ROWS + inner, -1)
    return (jnp.arange(D)[:, None] == row[None, :]).astype(BF16)


def reorder_kernel(scatter, order_ref, blocks_ref, out_ref):
    def one(step, carry):
        there = order_ref[step]
        if scatter:
            out_ref[there] = blocks_ref[step]
        else:
            out_ref[step] = blocks_ref[there]
        return carry

    lax.fori_loop(0, N_DP, one, 0)


def reorder(blocks, order, scatter):
    return pl.pallas_call(
        lambda *refs: reorder_kernel(scatter, *refs),
        out_shape=jax.ShapeDtypeStruct(blocks.shape, blocks.dtype),
        in_specs=[
            pl.BlockSpec(memory_space=pltpu.SMEM),
            pl.BlockSpec(memory_space=pltpu.VMEM),
        ],
        out_specs=pl.BlockSpec(memory_space=pltpu.VMEM),
        compiler_params=pltpu.CompilerParams(vmem_limit_bytes=24 * 1024 * 1024),
    )(order, blocks)


def across(left, right):
    return lax.dot_general(left, right, (((0,), (0,)), ((), ())), preferred_element_type=F32)


VMEM_BYTES = 16 * 1024 * 1024


def down_kernel(place_ref, left_ref, right_ref, own_ref, other_ref):
    step = pl.program_id(0)
    rows = across(left_ref[...], right_ref[...]).astype(BF16)
    count = rows.shape[0] // FROWS
    for block in range(count):
        place_here = place_ref[step * count + block]
        part = rows[block * FROWS : (block + 1) * FROWS]

        @pl.when(place_here < N_DP // 2)
        def keep():
            own_ref[place_here] = part

        @pl.when(place_here >= N_DP // 2)
        def give():
            other_ref[place_here - N_DP // 2] = part


def down_sums(left, right, places):
    tokens = left.shape[0]
    width = 640
    return pl.pallas_call(
        down_kernel,
        grid=(FF // width,),
        out_shape=[jax.ShapeDtypeStruct((N_DP // 2, FROWS, D), BF16)] * 2,
        in_specs=[
            pl.BlockSpec(memory_space=pltpu.SMEM),
            pl.BlockSpec((tokens, width), lambda i: (0, i)),
            pl.BlockSpec((tokens, D), lambda i: (0, 0)),
        ],
        out_specs=[pl.BlockSpec((N_DP // 2, FROWS, D), lambda i: (0, 0, 0))] * 2,
        compiler_params=pltpu.CompilerParams(vmem_limit_bytes=VMEM_BYTES),
        cost_estimate=pl.CostEstimate(
            flops=2 * tokens * FF * D, bytes_accessed=2 * FF * D, transcendentals=0
        ),
    )(places, left, right)


def gate_up_kernel(left_ref, gate_ref, up_ref, out_ref):
    left = left_ref[...]
    out_ref[:, :FF] = across(left, gate_ref[...]).astype(BF16)
    out_ref[:, FF:] = across(left, up_ref[...]).astype(BF16)


def gate_up_sums(left, gate, up, first):
    tokens = left.shape[0]
    columns = 2 * FF
    width = 128
    count = N_DP * PAD // 2 // width
    return pl.pallas_call(
        gate_up_kernel,
        grid=(count,),
        out_shape=jax.ShapeDtypeStruct((N_DP * PAD // 2, columns), BF16),
        in_specs=[
            pl.BlockSpec((tokens, width), lambda i: (0, i + first * count)),
            pl.BlockSpec((tokens, FF), lambda i: (0, 0)),
            pl.BlockSpec((tokens, FF), lambda i: (0, 0)),
        ],
        out_specs=pl.BlockSpec((width, columns), lambda i: (i, 0)),
        compiler_params=pltpu.CompilerParams(vmem_limit_bytes=VMEM_BYTES),
        cost_estimate=pl.CostEstimate(
            flops=tokens * N_DP * PAD * columns, bytes_accessed=N_DP * PAD * columns, transcendentals=0
        ),
    )(left, gate, up)


def attn_kernel(left_ref, mixed_ref, proj_ref, attn_ref, gain_ref, out_ref):
    qkv = across(left_ref[...], proj_ref[...])
    edge = QKV_PAD - LANES
    out_ref[:, :edge] = qkv[:, :edge].astype(BF16)
    out_ref[:, edge:QKV_PAD] = (qkv[:, edge:] + gain_ref[...]).astype(BF16)
    out_ref[:, QKV_PAD:] = across(mixed_ref[...], attn_ref[...]).astype(BF16)


def attn_sums(left, mixed, proj, attn, gain, first):
    tokens = left.shape[0]
    width = 128
    count = N_DP * PAD // 2 // width
    columns = QKV_PAD + OUT_PAD
    return pl.pallas_call(
        attn_kernel,
        grid=(count,),
        out_shape=jax.ShapeDtypeStruct((N_DP * PAD // 2, columns), BF16),
        in_specs=[
            pl.BlockSpec((tokens, width), lambda i: (0, i + first * count)),
            pl.BlockSpec((tokens, width), lambda i: (0, i + first * count)),
            pl.BlockSpec((tokens, QKV_PAD), lambda i: (0, 0)),
            pl.BlockSpec((tokens, OUT_PAD), lambda i: (0, 0)),
            pl.BlockSpec((width, LANES), lambda i: (i + first * count, 0)),
        ],
        out_specs=pl.BlockSpec((width, columns), lambda i: (i, 0)),
        compiler_params=pltpu.CompilerParams(vmem_limit_bytes=VMEM_BYTES),
        cost_estimate=pl.CostEstimate(
            flops=tokens * N_DP * PAD * columns, bytes_accessed=N_DP * PAD * columns, transcendentals=0
        ),
    )(left, mixed, proj, attn, gain)


def dot(left, right):
    return jnp.dot(left, right, preferred_element_type=F32)


def dot_t(left, right):
    return lax.dot_general(left, right, (((1,), (1,)), ((), ())), preferred_element_type=F32)


def shifted(block, axis, distance):
    devices = range(lax.axis_size(axis))
    pairs = [(i - distance, i) for i in devices if i - distance in devices]
    return lax.ppermute(block, axis, pairs)


def rope_tables(length):
    position = jnp.arange(length, dtype=F32)[:, None]
    frequency = ROPE_BASE ** (-jnp.arange(0, HD, 2, dtype=F32) / HD)
    angle = position * frequency[None, :]
    cosine, sine = jnp.cos(angle), jnp.sin(angle)
    return (jnp.tile(cosine, (1, LANES // (HD // 2))), jnp.tile(jnp.concatenate([-sine, sine], 1), (1, LANES // HD)))


SCALE = HD**-0.5
TURNED = D + KV * HD
PARTS = 5
PART = FF // PARTS
KEPT = jnp.bfloat16


def params():
    return pltpu.CompilerParams(vmem_limit_bytes=VMEM_BYTES)


def local_call(kernel, outs, cost, *operands):
    flops, moved, transcendentals = cost
    specs = [pl.BlockSpec(memory_space=pltpu.VMEM)] * (len(operands) - 1)
    return pl.pallas_call(
        kernel,
        in_specs=[pl.BlockSpec(memory_space=pltpu.SMEM)] + specs,
        out_specs=[pl.BlockSpec(memory_space=pltpu.VMEM)] * len(outs),
        out_shape=[jax.ShapeDtypeStruct(shape, dtype) for shape, dtype in outs],
        compiler_params=params(),
        cost_estimate=pl.CostEstimate(
            flops=flops, bytes_accessed=moved, transcendentals=transcendentals
        ),
    )(*operands)


def scaled(value, gain):
    return value * lax.rsqrt(jnp.mean(value * value, axis=-1, keepdims=True) + EPSILON) * gain


def scaled_backward(value, gain, grad):
    inverse = lax.rsqrt(jnp.mean(value * value, axis=-1, keepdims=True) + EPSILON)
    normed = value * inverse
    inner = grad * gain
    gain_sum = jnp.sum(grad * normed, axis=0, keepdims=True)
    through = inverse * (inner - normed * jnp.mean(inner * normed, axis=-1, keepdims=True))
    return (through, gain_sum)


def turn_heads(value, cosine, sine):
    first = lax.broadcasted_iota(jnp.int32, cosine.shape, 1) % HD < HD // 2
    tiles = []
    for start in range(0, TURNED, LANES):
        tile = value[:, start : start + LANES]
        other = jnp.where(first, pltpu.roll(tile, LANES - HD // 2, 1), pltpu.roll(tile, HD // 2, 1))
        tiles.append(tile * cosine + other * sine)
    return tiles


def head_columns(value, index):
    return value[:, index * HD : index * HD + HD]


def group_rows(value, group):
    return jnp.concatenate(
        [head_columns(value, group * (H // KV) + j) for j in range(H // KV)], 0
    ).astype(BF16)


def probabilities(queries, keys, mask):
    scores = jnp.where(mask > 0, dot_t(queries, keys) * SCALE, -1000000000.0)
    terms = jnp.exp(scores - jnp.max(scores, axis=-1, keepdims=True))
    return terms / jnp.sum(terms, axis=-1, keepdims=True)


def attend_forward_kernel(
    flag_ref, own_ref, got_ref, mask_ref, spread_ref, mat_ref, gains_ref, cosine_ref, sine_ref,
    hidden_ref, heads_ref, mixed_ref, middle_ref, second_ref,
):
    first = flag_ref[0] == 1
    stream = jnp.where(first, own_ref[flag_ref[1]].astype(F32), got_ref[...].astype(F32))
    spread = spread_ref[...]
    gains = gains_ref[...]
    hidden = dot(scaled(stream, gains[0:1]).astype(BF16), spread).astype(BF16)
    hidden_ref[...] = hidden
    projected = dot(hidden, mat_ref[:, :QKV_PAD])
    tiles = turn_heads(projected, cosine_ref[...], sine_ref[...])
    for index, tile in enumerate(tiles):
        heads_ref[:, index * LANES : index * LANES + LANES] = tile.astype(BF16)
    heads_ref[:, TURNED:] = projected[:, TURNED:].astype(BF16)
    turned = jnp.concatenate(tiles, 1)
    mask = jnp.concatenate([mask_ref[flag_ref[1]]] * (H // KV), 0)
    length = stream.shape[0]
    outs = []
    for group in range(KV):
        queries = group_rows(turned, group)
        keys = head_columns(turned, H + group).astype(BF16)
        values = head_columns(projected, H + KV + group).astype(BF16)
        mixed = dot(probabilities(queries, keys, mask).astype(BF16), values)
        outs += [mixed[j * length : j * length + length] for j in range(H // KV)]
    mixed = dot(jnp.concatenate(outs, 1).astype(BF16), spread).astype(BF16)
    mixed_ref[...] = mixed
    middle = stream + dot(mixed, mat_ref[:, QKV_PAD:])[:, :D]
    middle_ref[...] = middle
    second_ref[...] = dot(scaled(middle, gains[1:2]).astype(BF16), spread).astype(BF16)


def attend_forward(flags, inputs, got, masks, spread, mat, gains, cosine, sine):
    length = got.shape[0]
    wide = N_DP * PAD
    outs = [
        ((length, wide), BF16),
        ((length, QKV_PAD), BF16),
        ((length, wide), BF16),
        ((length, D), F32),
        ((length, wide), BF16),
    ]
    cost = (2 * length * wide * 5700, 8000000, H * length * length)
    return local_call(
        attend_forward_kernel, outs, cost, flags, inputs, got, masks, spread, mat, gains, cosine, sine
    )


def mlp_forward_kernel(
    flag_ref, second_ref, middle_ref, mat_ref, down_ref, gate_ref, up_ref, act_ref, out_ref
):
    second = second_ref[...]
    out = middle_ref[...]
    for start in range(0, FF, PART):
        here = slice(start, start + PART)
        gate = dot(second, mat_ref[:, here])
        up = dot(second, mat_ref[:, FF + start : FF + start + PART])
        gate_ref[:, here] = gate.astype(KEPT)
        up_ref[:, here] = up.astype(KEPT)
        act = (gate / (1.0 + jnp.exp(-gate)) * up).astype(BF16)
        act_ref[:, here] = act
        out = out + dot(act, down_ref[here, :])
    out_ref[...] = out.astype(BF16)


def mlp_forward(flags, second, middle, gate_up_mat, down_mat):
    length, wide = second.shape
    outs = [((length, FF), KEPT), ((length, FF), KEPT), ((length, FF), BF16), ((length, D), BF16)]
    cost = (2 * length * wide * 7680, 20000000, length * FF)
    return local_call(
        mlp_forward_kernel, outs, cost, flags, second, middle, gate_up_mat, down_mat
    )


def gate_grads_part(first, grad, gates, ups, down, here):
    gate = jnp.where(first, gates[0][:, here].astype(F32), gates[1][:, here].astype(F32))
    up = jnp.where(first, ups[0][:, here].astype(F32), ups[1][:, here].astype(F32))
    grad_act = dot_t(grad, down[here, :])
    sig = 1.0 / (1.0 + jnp.exp(-gate))
    grad_gate = (grad_act * up * sig * (1.0 + gate * (1.0 - sig))).astype(BF16)
    return (grad_gate, (grad_act * gate * sig).astype(BF16))


def middle_part(first, grad, middles, total_two, spread, gains):
    grad_two = dot_t(total_two.astype(BF16), spread)
    middle = jnp.where(first, middles[0][...], middles[1][...])
    through, gain = scaled_backward(middle, gains[1:2], grad_two)
    return (grad.astype(F32) + through, gain)


def mlp_backward_kernel(
    flag_ref, grad_ref, middle_a_ref, middle_b_ref, gate_a_ref, gate_b_ref, up_a_ref, up_b_ref,
    mat_ref, down_ref, spread_ref, gains_ref,
    grad_gate_ref, grad_up_ref, grad_middle_ref, gain_ref,
):
    first = flag_ref[0] == 1
    grad = grad_ref[...]
    total_two = 0
    for start in range(0, FF, PART):
        here = slice(start, start + PART)
        grad_gate, grad_up = gate_grads_part(
            first, grad, (gate_a_ref, gate_b_ref), (up_a_ref, up_b_ref), down_ref, here
        )
        grad_gate_ref[:, here] = grad_gate
        grad_up_ref[:, here] = grad_up
        total_two += dot_t(grad_gate, mat_ref[:, here])
        total_two += dot_t(grad_up, mat_ref[:, FF + start : FF + start + PART])
    grad_middle_ref[...], gain_ref[...] = middle_part(
        first, grad, (middle_a_ref, middle_b_ref), total_two, spread_ref[...], gains_ref[...]
    )


def mlp_backward(flags, grad, middles, gates, ups, gate_up_mat, down_mat, spread, gains):
    length = grad.shape[0]
    outs = [((length, FF), BF16), ((length, FF), BF16), ((length, D), F32), ((1, D), F32)]
    cost = (2 * length * N_DP * PAD * 7680, 22000000, length * FF)
    return local_call(
        mlp_backward_kernel, outs, cost,
        flags, grad, *middles, *gates, *ups, gate_up_mat, down_mat, spread, gains,
    )


def gate_grads_kernel(
    flag_ref, grad_ref, gate_a_ref, gate_b_ref, up_a_ref, up_b_ref, down_ref, grad_gate_ref, grad_up_ref
):
    first = flag_ref[0] == 1
    for start in range(0, FF, PART):
        here = slice(start, start + PART)
        grad_gate_ref[:, here], grad_up_ref[:, here] = gate_grads_part(
            first, grad_ref[...], (gate_a_ref, gate_b_ref), (up_a_ref, up_b_ref), down_ref, here
        )


def gate_grads(flags, grad, gates, ups, down_mat):
    length = grad.shape[0]
    outs = [((length, FF), BF16), ((length, FF), BF16)]
    cost = (2 * length * D * FF, 9000000, length * FF)
    return local_call(gate_grads_kernel, outs, cost, flags, grad, *gates, *ups, down_mat)


def middle_grad_kernel(
    flag_ref, grad_ref, middle_a_ref, middle_b_ref, grad_gate_ref, grad_up_ref,
    mat_ref, spread_ref, gains_ref, grad_middle_ref, gain_ref,
):
    total_two = dot_t(grad_gate_ref[...], mat_ref[:, :FF]) + dot_t(grad_up_ref[...], mat_ref[:, FF:])
    grad_middle_ref[...], gain_ref[...] = middle_part(
        flag_ref[0] == 1, grad_ref[...], (middle_a_ref, middle_b_ref), total_two, spread_ref[...],
        gains_ref[...],
    )


def middle_grad(flags, grad, middles, grad_gate, grad_up, gate_up_mat, spread, gains):
    length = grad.shape[0]
    outs = [((length, D), F32), ((1, D), F32)]
    cost = (2 * length * N_DP * PAD * 5120, 14000000, 0)
    return local_call(
        middle_grad_kernel, outs, cost,
        flags, grad, *middles, grad_gate, grad_up, gate_up_mat, spread, gains,
    )


def attend_backward_kernel(
    flag_ref, grad_ref, own_ref, got_ref, heads_a_ref, heads_b_ref, mask_ref, spread_ref, mat_ref,
    gains_ref, cosine_ref, sine_ref, grad_proj_ref, grad_attn_ref, grad_in_ref, gain_ref,
):
    first = flag_ref[0] == 1
    spread = spread_ref[...]
    grad_middle = grad_ref[...]
    grad_attn = grad_middle.astype(BF16)
    length = grad_middle.shape[0]
    grad_attn_ref[:, :D] = grad_attn
    grad_attn_ref[:, D:] = jnp.zeros((length, OUT_PAD - D), BF16)
    grad_mixed = dot_t(grad_attn, mat_ref[:, QKV_PAD : QKV_PAD + D]).astype(BF16)
    grad_mixed = dot_t(grad_mixed, spread)
    heads = jnp.where(first, heads_a_ref[...].astype(F32), heads_b_ref[...].astype(F32))
    mask = jnp.concatenate([mask_ref[flag_ref[1]]] * (H // KV), 0)
    grad_queries, grad_keys, grad_values = [], [], []
    for group in range(KV):
        queries = group_rows(heads, group)
        keys = head_columns(heads, H + group).astype(BF16)
        values = head_columns(heads, H + KV + group).astype(BF16)
        mixed = group_rows(grad_mixed, group)
        probs = probabilities(queries, keys, mask)
        grad_probs = dot_t(mixed, values)
        grad_scores = probs * (grad_probs - jnp.sum(grad_probs * probs, axis=-1, keepdims=True))
        grad_scores = grad_scores.astype(BF16)
        queries_part = dot(grad_scores, keys) * SCALE
        grad_queries += [queries_part[j * length : j * length + length] for j in range(H // KV)]
        grad_keys.append(across(grad_scores, queries) * SCALE)
        grad_values.append(across(probs.astype(BF16), mixed))
    turned = jnp.concatenate(grad_queries + grad_keys, 1).astype(BF16).astype(F32)
    tiles = turn_heads(turned, cosine_ref[...], -sine_ref[...])
    blank = jnp.zeros((length, QKV_PAD - QKV), F32)
    grad_proj = jnp.concatenate(tiles + grad_values + [blank], 1).astype(BF16)
    grad_proj_ref[...] = grad_proj
    grad_one = dot_t(grad_proj, mat_ref[:, :QKV_PAD]).astype(BF16)
    grad_one = dot_t(grad_one, spread)
    stream = jnp.where(first, own_ref[flag_ref[1]].astype(F32), got_ref[...].astype(F32))
    through, gain = scaled_backward(stream, gains_ref[0:1], grad_one)
    grad_in_ref[...] = (grad_middle + through).astype(BF16)
    gain_ref[...] = gain


def attend_backward(flags, grad, inputs, got, heads, masks, spread, mat, gains, cosine, sine):
    length = grad.shape[0]
    wide = N_DP * PAD
    outs = [
        ((length, QKV_PAD), BF16),
        ((length, OUT_PAD), BF16),
        ((length, D), BF16),
        ((1, D), F32),
    ]
    cost = (2 * length * wide * 6700, 9000000, H * length * length)
    return local_call(
        attend_backward_kernel, outs, cost,
        flags, grad, inputs, got, *heads, masks, spread, mat, gains, cosine, sine,
    )

def as_blocks(rows):
    return rows.reshape(N_DP // 2, -1, rows.shape[-1])


def per_device(
    inputs, segment_ids, qkv_weight, out_weight, gate_up_weight, down_weight, norm_gains, cotangent
):
    batches = inputs.shape[0]
    is_first = lax.axis_index("section") == 0
    order = block_order()
    spread = placement(order)
    attn_shard = jnp.concatenate(
        [
            qkv_weight[0],
            norm_gains[0],
            jnp.zeros((ROWS, QKV_PAD - QKV - 2), BF16),
            out_weight[0],
            jnp.zeros((ROWS, OUT_PAD - D), BF16),
        ],
        1,
    )
    widths = (QKV_PAD + OUT_PAD, 2 * FF)
    down_shard = jnp.pad(down_weight[0], ((0, 0), (0, OUT_PAD - D))).reshape(PAD, -1)
    rows = jnp.concatenate(
        [
            jnp.pad(attn_shard, ((0, 1), (0, 0))),
            jnp.pad(gate_up_weight[0], ((0, 1), (0, 0))),
            down_shard,
        ],
        1,
    )
    near = gather_near(rows)
    near_attn = near[:, :, : widths[0]]
    near_gate_up = near[:, :, widths[0] : widths[0] + widths[1]]
    near_down = near[:, :, widths[0] + widths[1] :].reshape(8, FROWS, OUT_PAD)[:, :, :D]
    gate_up_flow = Flow(gather_far(near_gate_up))
    attn_flow = Flow(gather_far(after(near_attn, near_gate_up)))
    spread = step([attn_flow], spread)
    spread, near_down = step([gate_up_flow], (spread, near_down))
    down_flow = Flow(gather_far(near_down))
    for group in ([attn_flow], [gate_up_flow], [down_flow], [down_flow]):
        spread = step(group, spread)
    attn_mat, gate_up_mat, down_mat = attn_flow.result, gate_up_flow.result, down_flow.result
    gain_rows = jnp.concatenate([piece[:, :, QKV : QKV + 2] for piece in attn_mat], 0)
    gain_rows = gain_rows.reshape(N_DP * PAD, 2)
    attn_mat = assemble(attn_mat)
    gate_up_mat = assemble(gate_up_mat)
    down_mat = reorder(jnp.concatenate(down_mat, 0), order, True).reshape(FF, D)
    gains_full = lax.dot_general(
        gain_rows, spread, (((0,), (1,)), ((), ())), preferred_element_type=F32
    )
    length = inputs.shape[1]
    cosine, sine = rope_tables(length)
    positions = jnp.arange(length)
    masks = (
        (segment_ids[:, :, None] == segment_ids[:, None, :])
        & (positions[:, None] >= positions[None, :])[None]
    ).astype(F32)
    first = is_first.astype(jnp.int32)

    def flags(for_first, for_second):
        return jnp.stack([first, jnp.where(is_first, for_first, for_second)])

    received = jnp.zeros(inputs.shape[1:], BF16)
    saved = []
    produced = []
    arrivals = []
    for turn in range(batches + 1):
        arrivals.append(received)
        hidden, heads, mixed, middle, second = attend_forward(
            flags(min(turn, batches - 1), max(turn - 1, 0)),
            inputs, received, masks, spread, attn_mat, gains_full, cosine, sine,
        )
        gate, up, act, layer_out = mlp_forward(
            flags(0, 0), second, middle, gate_up_mat, down_mat
        )
        saved.append((hidden, heads, mixed, middle, second, gate, up, act))
        produced.append(layer_out)
        if turn < batches:
            received = shifted(layer_out, "section", 1)
    section_outputs = jnp.stack(
        [
            jnp.where(is_first, produced[position], produced[position + 1])
            for position in range(batches)
        ]
    )[None]
    received = jnp.zeros(inputs.shape[1:], BF16)
    places = jnp.sum(
        jnp.where(order[:, None] == jnp.arange(N_DP)[None, :], jnp.arange(N_DP)[:, None], 0), 0
    ).astype(jnp.int32)

    def lefts(member):
        return jnp.concatenate(
            [jnp.where(is_first, saved[b][member], saved[b + 1][member]) for b in range(batches)], 0
        )

    def rights(turns):
        return jnp.concatenate(
            [jnp.where(is_first, turns[b + 1], turns[b]) for b in range(batches)], 0
        )

    returned = []
    downs = []
    gates = []
    ups = []
    projs = []
    attns = []
    gain_sum = 0
    flows = {}
    gate_up_own = []
    attn_own = []
    for turn in range(batches + 1):
        last = turn == batches
        if turn < batches:
            own_grad = cotangent[turn]
        else:
            own_grad = jnp.zeros(inputs.shape[1:], BF16)
        grad_out = jnp.where(is_first, received, own_grad)
        downs.append(grad_out)
        kept_first, kept_second = saved[max(turn - 1, 0)], saved[min(turn + 1, batches)]
        chosen = flags(max(turn - 1, 0), min(turn, batches - 1))

        def both(member):
            return (kept_first[member], kept_second[member])

        if not last:
            grad_gate, grad_up, grad_middle, gain_two = mlp_backward(
                chosen, grad_out, both(3), both(5), both(6), gate_up_mat, down_mat, spread, gains_full
            )
            gates.append(grad_gate)
            ups.append(grad_up)
        else:
            grad_gate, grad_up = gate_grads(chosen, grad_out, both(5), both(6), down_mat)
            gates.append(grad_gate)
            ups.append(grad_up)
            terms = (lefts(4), rights(gates), rights(ups))
            other = gate_up_sums(*terms, 1)
            flows["gate_up"] = Flow(
                full_scatter(as_blocks(other), lambda: as_blocks(gate_up_own[0]))
            )
            down_own, down_other = down_sums(lefts(7), after(rights(downs), other), places)
            flows["down"] = Flow(full_scatter(down_other, lambda: down_own))
            gate_up_own.append(gate_up_sums(*after(terms, down_other), 0))
            grad_gate, grad_up = after((grad_gate, grad_up), gate_up_own[0])
            grad_middle, gain_two = middle_grad(
                chosen, grad_out, both(3), grad_gate, grad_up, gate_up_mat, spread, gains_full
            )
        grad_proj, grad_attn, grad_in, gain_one = attend_backward(
            chosen, grad_middle, inputs, arrivals[min(turn + 1, batches)], both(1), masks, spread,
            attn_mat, gains_full, cosine, sine,
        )
        if last:
            grad_proj = step([flows["gate_up"], flows["down"]], grad_proj)
        projs.append(grad_proj)
        attns.append(grad_attn)
        gain_sum = gain_sum + jnp.concatenate([gain_one, gain_two], 0)
        returned.append(grad_in)
        if turn < batches:
            received = shifted(grad_in, "section", -1)
    section_input_grads = jnp.stack(
        [
            jnp.where(is_first, returned[position + 1], returned[position])
            for position in range(batches)
        ]
    )[None]
    gain_high = gain_sum.astype(BF16)
    gain_low = (gain_sum - gain_high.astype(F32)).astype(BF16)
    gain_rows = lax.dot_general(
        spread, jnp.stack([gain_high, gain_low]), (((0,), (2,)), ((), ())), preferred_element_type=F32
    )
    first_lane = QKV - (QKV_PAD - LANES)
    gain_rows = jnp.pad(
        gain_rows[:, 0] + gain_rows[:, 1], ((0, 0), (first_lane, LANES - first_lane - 2))
    )
    terms = (lefts(0), lefts(2), rights(projs), rights(attns), gain_rows)
    other = attn_sums(*terms, 1)
    flows["attn"] = Flow(full_scatter(as_blocks(other), lambda: as_blocks(attn_own[0])))
    attn_own.append(attn_sums(*after(terms, other), 0))
    down_flow, gate_up_flow, attn_flow = flows["down"], flows["gate_up"], flows["attn"]
    waiting = after(section_outputs, attn_own[0])
    for group in (
        [gate_up_flow],
        [attn_flow],
        [down_flow],
        [attn_flow],
        [gate_up_flow],
        [attn_flow],
        [gate_up_flow, down_flow],
        [attn_flow],
        [gate_up_flow, down_flow],
        [attn_flow],
        [down_flow],
    ):
        waiting = step(group, waiting)
    section_outputs = waiting
    while min(flow.result is not None for flow in (down_flow, gate_up_flow, attn_flow)) == 0:
        waiting = step([down_flow, gate_up_flow, attn_flow], waiting)
    section_outputs = waiting
    down_grad, gate_up_grad, attn_grad = down_flow.result, gate_up_flow.result, attn_flow.result
    return (
        section_outputs,
        section_input_grads,
        attn_grad[None, :ROWS, :QKV],
        attn_grad[None, :ROWS, QKV_PAD : QKV_PAD + D],
        gate_up_grad[None, :ROWS],
        down_grad[None],
        attn_grad[None, :ROWS, QKV : QKV + 2],
    )


def solution(mesh):
    in_specs = (
        P(None, "dp", None),
        P(None, "dp"),
        P("section", "dp", None),
        P("section", "dp", None),
        P("section", "dp", None),
        P("section", "dp", None),
        P("section", "dp", None),
        P(None, "dp", None),
    )
    out_specs = (
        P("section", None, "dp", None),
        P("section", None, "dp", None),
        P("section", "dp", None),
        P("section", "dp", None),
        P("section", "dp", None),
        P("section", "dp", None),
        P("section", "dp", None),
    )
    return jax.shard_map(
        per_device, mesh=mesh, in_specs=in_specs, out_specs=out_specs, check_vma=False
    )
```

```python
import jax
import jax.numpy as jnp
from jax import lax
from jax.experimental import pallas as pl
from jax.experimental.pallas import tpu as pltpu
from jax.sharding import PartitionSpec as P

D = 960
H = 15
KV = 5
HD = 64
FF = 2560
QKV = D + 2 * KV * HD
N_DP = 64
ROWS = D // N_DP
PAD = 16
FROWS = FF // N_DP
LANES = 128
QKV_PAD = 1664
OUT_PAD = 1024

EPSILON = 1e-05
ROPE_BASE = 100000.0
BF16 = jnp.bfloat16
F32 = jnp.float32


def place(y, x, z, core):
    return ((y % 4 * 2 + x % 2) * 4 + z % 4) * 2 + core % 2


def route(kind, step):
    pairs = []
    for source in range(N_DP):
        y, x, z, core = source // 16, source // 8 % 2, source // 2 % 4, source % 2
        if kind == "core":
            target = place(y, x, z, core + 1)
        elif kind == "x":
            target = place(y, x + 1, z, core)
        elif (kind == "wide") == (core == 0):
            target = place(y, x, z + step, core)
        else:
            target = place(y + step, x, z, core)
        pairs.append((source, target))
    return pairs


def send(block, kind, step=1):
    return lax.ppermute(block, "dp", route(kind, step))


def total(*terms):
    result = terms[0].astype(F32)
    for term in terms[1:]:
        result = result + term.astype(F32)
    return result


def near_scatter(blocks):
    blocks = yield from ring_scatter((blocks,), "narrow")
    (got,) = yield ((blocks[1], "x"),)
    return total(blocks[0], got)


def ring_scatter(terms, kind):
    terms = [term.reshape((4, term.shape[0] // 4) + term.shape[1:]) for term in terms]
    half = terms[0].shape[1] // 2

    def own(step, part):
        return [term[step, part] for term in terms]

    near, far = slice(0, half), slice(half, None)
    left, right = yield (
        (total(*own(3, near)).astype(BF16), kind, 1),
        (total(*own(3, far)).astype(BF16), kind, -1),
    )
    onward = jnp.concatenate([total(*own(1, near), left), total(*own(1, far))], 0).astype(BF16)
    back = jnp.concatenate([total(*own(2, near)), total(*own(2, far), right)], 0).astype(BF16)
    left, right = yield ((onward, kind, 1), (back, kind, -1))
    return total(*[term[0] for term in terms], left, right).astype(BF16)


def far_scatter(for_other, for_own):
    (got,) = yield ((for_other, "core"),)
    return (yield from ring_scatter((for_own(), got), "wide"))


def full_scatter(for_other, for_own):
    blocks = yield from far_scatter(for_other, for_own)
    return (yield from near_scatter(blocks))


class Flow:
    def __init__(self, stages):
        self.stages = stages
        self.result = None
        self.wanted = next(stages)
        self.launch(tuple(request[0] for request in self.wanted))

    def launch(self, blocks):
        self.pending = tuple(
            send(block, *request[1:]) for block, request in zip(blocks, self.wanted)
        )

    def advance(self, arrived):
        try:
            self.wanted = self.stages.send(arrived)
        except StopIteration as end:
            self.wanted = ()
            self.result = end.value


def step(flows, value):
    flows = [flow for flow in flows if flow.result is None]
    arrived, value = lax.optimization_barrier((tuple(flow.pending for flow in flows), value))
    for flow, got in zip(flows, arrived):
        flow.advance(got)
    blocks = tuple(tuple(request[0] for request in flow.wanted) for flow in flows)
    blocks, value = lax.optimization_barrier((blocks, value))
    for flow, ready in zip(flows, blocks):
        flow.launch(ready)
    return value


def ring_gather(block, kind):
    half = block.shape[0] // 2
    from_left = send(block, kind, 1)
    from_right = send(block, kind, -1)
    far_left = send(from_left[:half], kind, 1)
    far_right = send(from_right[half:], kind, -1)
    sides = jnp.concatenate([from_right, from_left], 0)
    return [block, sides, jnp.concatenate([far_left, far_right], 0)]


def gather_near(shard):
    block = jnp.stack([shard, send(shard, "x")], 0)
    return jnp.concatenate(ring_gather(block, "narrow"), 0)


def gather_far(block):
    half = block.shape[0] // 2
    others = send(block, "core")
    left, right = yield ((block, "wide", 1), (block, "wide", -1))
    sides = [right, left]
    sides_there = send(jnp.concatenate(sides, 0), "core")
    far = yield ((left[:half], "wide", 1), (right[half:], "wide", -1))
    far_there = send(jnp.concatenate(far, 0), "core")
    return [block, *sides, *far, others, sides_there, far_there]


def assemble_kernel(*refs):
    pieces, out_ref, sems = refs[:-2], refs[-2], refs[-1]
    copies = []
    start = 0
    for index, piece in enumerate(pieces):
        rows = piece.shape[0]
        copies.append(pltpu.make_async_copy(piece, out_ref.at[start : start + rows], sems.at[index]))
        start += rows
    for copy in copies:
        copy.start()
    for copy in copies:
        copy.wait()


def assemble(pieces):
    pieces = [piece.reshape(-1, piece.shape[-1]) for piece in pieces]
    columns = pieces[0].shape[1]
    return pl.pallas_call(
        assemble_kernel,
        in_specs=[pl.BlockSpec(memory_space=pl.ANY)] * len(pieces),
        out_specs=pl.BlockSpec(memory_space=pltpu.VMEM),
        out_shape=pltpu.VMEM((N_DP * PAD, columns), BF16),
        scratch_shapes=[pltpu.SemaphoreType.DMA((len(pieces),))],
        compiler_params=pltpu.CompilerParams(vmem_limit_bytes=VMEM_BYTES),
    )(*pieces)


def after(value, earlier):
    return lax.optimization_barrier((value, earlier))[0]


def block_order():
    index = lax.axis_index("dp")
    y, x, z, core = index // 16, index // 8 % 2, index // 2 % 4, index % 2
    position = jnp.arange(N_DP)
    core_step, wide, narrow, x_step = position // 32, position // 8 % 4, position // 2 % 4, position % 2
    wide, narrow = wide ^ (wide // 2), narrow ^ (narrow // 2)
    core_there = (core + core_step) % 2
    z_step = jnp.where(core_there == 0, wide, narrow)
    y_step = jnp.where(core_there == 0, narrow, wide)
    return (((y + y_step) % 4 * 2 + (x + x_step) % 2) * 4 + (z + z_step) % 4) * 2 + core_there


def placement(order):
    column = jnp.arange(N_DP * PAD)
    inner = column % PAD
    row = jnp.where(inner < ROWS, jnp.repeat(order, PAD) * ROWS + inner, -1)
    return (jnp.arange(D)[:, None] == row[None, :]).astype(BF16)


def reorder_kernel(scatter, order_ref, blocks_ref, out_ref):
    def one(step, carry):
        there = order_ref[step]
        if scatter:
            out_ref[there] = blocks_ref[step]
        else:
            out_ref[step] = blocks_ref[there]
        return carry

    lax.fori_loop(0, N_DP, one, 0)


def reorder(blocks, order, scatter):
    return pl.pallas_call(
        lambda *refs: reorder_kernel(scatter, *refs),
        out_shape=jax.ShapeDtypeStruct(blocks.shape, blocks.dtype),
        in_specs=[
            pl.BlockSpec(memory_space=pltpu.SMEM),
            pl.BlockSpec(memory_space=pltpu.VMEM),
        ],
        out_specs=pl.BlockSpec(memory_space=pltpu.VMEM),
        compiler_params=pltpu.CompilerParams(vmem_limit_bytes=24 * 1024 * 1024),
    )(order, blocks)


def across(left, right):
    return lax.dot_general(left, right, (((0,), (0,)), ((), ())), preferred_element_type=F32)


VMEM_BYTES = 16 * 1024 * 1024


def down_kernel(place_ref, left_ref, right_ref, own_ref, other_ref):
    step = pl.program_id(0)
    rows = across(left_ref[...], right_ref[...]).astype(BF16)
    count = rows.shape[0] // FROWS
    for block in range(count):
        place_here = place_ref[step * count + block]
        part = rows[block * FROWS : (block + 1) * FROWS]

        @pl.when(place_here < N_DP // 2)
        def keep():
            own_ref[place_here] = part

        @pl.when(place_here >= N_DP // 2)
        def give():
            other_ref[place_here - N_DP // 2] = part


def down_sums(left, right, places):
    tokens = left.shape[0]
    width = 640
    return pl.pallas_call(
        down_kernel,
        grid=(FF // width,),
        out_shape=[jax.ShapeDtypeStruct((N_DP // 2, FROWS, D), BF16)] * 2,
        in_specs=[
            pl.BlockSpec(memory_space=pltpu.SMEM),
            pl.BlockSpec((tokens, width), lambda i: (0, i)),
            pl.BlockSpec((tokens, D), lambda i: (0, 0)),
        ],
        out_specs=[pl.BlockSpec((N_DP // 2, FROWS, D), lambda i: (0, 0, 0))] * 2,
        compiler_params=pltpu.CompilerParams(vmem_limit_bytes=VMEM_BYTES),
        cost_estimate=pl.CostEstimate(
            flops=2 * tokens * FF * D, bytes_accessed=2 * FF * D, transcendentals=0
        ),
    )(places, left, right)


def gate_up_kernel(left_ref, gate_ref, up_ref, out_ref):
    left = left_ref[...]
    out_ref[:, :FF] = across(left, gate_ref[...]).astype(BF16)
    out_ref[:, FF:] = across(left, up_ref[...]).astype(BF16)


def gate_up_sums(left, gate, up, first):
    tokens = left.shape[0]
    columns = 2 * FF
    width = 128
    count = N_DP * PAD // 2 // width
    return pl.pallas_call(
        gate_up_kernel,
        grid=(count,),
        out_shape=jax.ShapeDtypeStruct((N_DP * PAD // 2, columns), BF16),
        in_specs=[
            pl.BlockSpec((tokens, width), lambda i: (0, i + first * count)),
            pl.BlockSpec((tokens, FF), lambda i: (0, 0)),
            pl.BlockSpec((tokens, FF), lambda i: (0, 0)),
        ],
        out_specs=pl.BlockSpec((width, columns), lambda i: (i, 0)),
        compiler_params=pltpu.CompilerParams(vmem_limit_bytes=VMEM_BYTES),
        cost_estimate=pl.CostEstimate(
            flops=tokens * N_DP * PAD * columns, bytes_accessed=N_DP * PAD * columns, transcendentals=0
        ),
    )(left, gate, up)


def attn_kernel(left_ref, mixed_ref, proj_ref, attn_ref, gain_ref, out_ref):
    qkv = across(left_ref[...], proj_ref[...])
    edge = QKV_PAD - LANES
    out_ref[:, :edge] = qkv[:, :edge].astype(BF16)
    out_ref[:, edge:QKV_PAD] = (qkv[:, edge:] + gain_ref[...]).astype(BF16)
    out_ref[:, QKV_PAD:] = across(mixed_ref[...], attn_ref[...]).astype(BF16)


def attn_sums(left, mixed, proj, attn, gain, first):
    tokens = left.shape[0]
    width = 128
    count = N_DP * PAD // 2 // width
    columns = QKV_PAD + OUT_PAD
    return pl.pallas_call(
        attn_kernel,
        grid=(count,),
        out_shape=jax.ShapeDtypeStruct((N_DP * PAD // 2, columns), BF16),
        in_specs=[
            pl.BlockSpec((tokens, width), lambda i: (0, i + first * count)),
            pl.BlockSpec((tokens, width), lambda i: (0, i + first * count)),
            pl.BlockSpec((tokens, QKV_PAD), lambda i: (0, 0)),
            pl.BlockSpec((tokens, OUT_PAD), lambda i: (0, 0)),
            pl.BlockSpec((width, LANES), lambda i: (i + first * count, 0)),
        ],
        out_specs=pl.BlockSpec((width, columns), lambda i: (i, 0)),
        compiler_params=pltpu.CompilerParams(vmem_limit_bytes=VMEM_BYTES),
        cost_estimate=pl.CostEstimate(
            flops=tokens * N_DP * PAD * columns, bytes_accessed=N_DP * PAD * columns, transcendentals=0
        ),
    )(left, mixed, proj, attn, gain)


def dot(left, right):
    return jnp.dot(left, right, preferred_element_type=F32)


def dot_t(left, right):
    return lax.dot_general(left, right, (((1,), (1,)), ((), ())), preferred_element_type=F32)


def shifted(block, axis, distance):
    devices = range(lax.axis_size(axis))
    pairs = [(i - distance, i) for i in devices if i - distance in devices]
    return lax.ppermute(block, axis, pairs)


def rope_tables(length):
    position = jnp.arange(length, dtype=F32)[:, None]
    frequency = ROPE_BASE ** (-jnp.arange(0, HD, 2, dtype=F32) / HD)
    angle = position * frequency[None, :]
    cosine, sine = jnp.cos(angle), jnp.sin(angle)
    return (jnp.tile(cosine, (1, LANES // (HD // 2))), jnp.tile(jnp.concatenate([-sine, sine], 1), (1, LANES // HD)))


SCALE = HD**-0.5
TURNED = D + KV * HD
PARTS = 5
PART = FF // PARTS
KEPT = jnp.bfloat16


def params():
    return pltpu.CompilerParams(vmem_limit_bytes=VMEM_BYTES)


def local_call(kernel, outs, cost, *operands):
    flops, moved, transcendentals = cost
    specs = [pl.BlockSpec(memory_space=pltpu.VMEM)] * (len(operands) - 1)
    return pl.pallas_call(
        kernel,
        in_specs=[pl.BlockSpec(memory_space=pltpu.SMEM)] + specs,
        out_specs=[pl.BlockSpec(memory_space=pltpu.VMEM)] * len(outs),
        out_shape=[jax.ShapeDtypeStruct(shape, dtype) for shape, dtype in outs],
        compiler_params=params(),
        cost_estimate=pl.CostEstimate(
            flops=flops, bytes_accessed=moved, transcendentals=transcendentals
        ),
    )(*operands)


def scaled(value, gain):
    return value * lax.rsqrt(jnp.mean(value * value, axis=-1, keepdims=True) + EPSILON) * gain


def scaled_backward(value, gain, grad):
    inverse = lax.rsqrt(jnp.mean(value * value, axis=-1, keepdims=True) + EPSILON)
    normed = value * inverse
    inner = grad * gain
    gain_sum = jnp.sum(grad * normed, axis=0, keepdims=True)
    through = inverse * (inner - normed * jnp.mean(inner * normed, axis=-1, keepdims=True))
    return (through, gain_sum)


def turn_heads(value, cosine, sine):
    first = lax.broadcasted_iota(jnp.int32, cosine.shape, 1) % HD < HD // 2
    tiles = []
    for start in range(0, TURNED, LANES):
        tile = value[:, start : start + LANES]
        other = jnp.where(first, pltpu.roll(tile, LANES - HD // 2, 1), pltpu.roll(tile, HD // 2, 1))
        tiles.append(tile * cosine + other * sine)
    return tiles


def head_columns(value, index):
    return value[:, index * HD : index * HD + HD]


def group_rows(value, group):
    return jnp.concatenate(
        [head_columns(value, group * (H // KV) + j) for j in range(H // KV)], 0
    ).astype(BF16)


def probabilities(queries, keys, mask):
    scores = jnp.where(mask > 0, dot_t(queries, keys) * SCALE, -1000000000.0)
    terms = jnp.exp(scores - jnp.max(scores, axis=-1, keepdims=True))
    return terms / jnp.sum(terms, axis=-1, keepdims=True)


def attend_forward_kernel(
    flag_ref, own_ref, got_ref, mask_ref, spread_ref, mat_ref, gains_ref, cosine_ref, sine_ref,
    hidden_ref, heads_ref, mixed_ref, middle_ref, second_ref,
):
    first = flag_ref[0] == 1
    stream = jnp.where(first, own_ref[flag_ref[1]].astype(F32), got_ref[...].astype(F32))
    spread = spread_ref[...]
    gains = gains_ref[...]
    hidden = dot(scaled(stream, gains[0:1]).astype(BF16), spread).astype(BF16)
    hidden_ref[...] = hidden
    projected = dot(hidden, mat_ref[:, :QKV_PAD])
    tiles = turn_heads(projected, cosine_ref[...], sine_ref[...])
    for index, tile in enumerate(tiles):
        heads_ref[:, index * LANES : index * LANES + LANES] = tile.astype(BF16)
    heads_ref[:, TURNED:] = projected[:, TURNED:].astype(BF16)
    turned = jnp.concatenate(tiles, 1)
    mask = jnp.concatenate([mask_ref[flag_ref[1]]] * (H // KV), 0)
    length = stream.shape[0]
    outs = []
    for group in range(KV):
        queries = group_rows(turned, group)
        keys = head_columns(turned, H + group).astype(BF16)
        values = head_columns(projected, H + KV + group).astype(BF16)
        mixed = dot(probabilities(queries, keys, mask).astype(BF16), values)
        outs += [mixed[j * length : j * length + length] for j in range(H // KV)]
    mixed = dot(jnp.concatenate(outs, 1).astype(BF16), spread).astype(BF16)
    mixed_ref[...] = mixed
    middle = stream + dot(mixed, mat_ref[:, QKV_PAD:])[:, :D]
    middle_ref[...] = middle
    second_ref[...] = dot(scaled(middle, gains[1:2]).astype(BF16), spread).astype(BF16)


def attend_forward(flags, inputs, got, masks, spread, mat, gains, cosine, sine):
    length = got.shape[0]
    wide = N_DP * PAD
    outs = [
        ((length, wide), BF16),
        ((length, QKV_PAD), BF16),
        ((length, wide), BF16),
        ((length, D), F32),
        ((length, wide), BF16),
    ]
    cost = (2 * length * wide * 5700, 8000000, H * length * length)
    return local_call(
        attend_forward_kernel, outs, cost, flags, inputs, got, masks, spread, mat, gains, cosine, sine
    )


def mlp_forward_kernel(
    flag_ref, second_ref, middle_ref, mat_ref, down_ref, gate_ref, up_ref, act_ref, out_ref
):
    second = second_ref[...]
    out = middle_ref[...]
    for start in range(0, FF, PART):
        here = slice(start, start + PART)
        gate = dot(second, mat_ref[:, here])
        up = dot(second, mat_ref[:, FF + start : FF + start + PART])
        gate_ref[:, here] = gate.astype(KEPT)
        up_ref[:, here] = up.astype(KEPT)
        act = (gate / (1.0 + jnp.exp(-gate)) * up).astype(BF16)
        act_ref[:, here] = act
        out = out + dot(act, down_ref[here, :])
    out_ref[...] = out.astype(BF16)


def mlp_forward(flags, second, middle, gate_up_mat, down_mat):
    length, wide = second.shape
    outs = [((length, FF), KEPT), ((length, FF), KEPT), ((length, FF), BF16), ((length, D), BF16)]
    cost = (2 * length * wide * 7680, 20000000, length * FF)
    return local_call(
        mlp_forward_kernel, outs, cost, flags, second, middle, gate_up_mat, down_mat
    )


def gate_grads_part(first, grad, gates, ups, down, here):
    gate = jnp.where(first, gates[0][:, here].astype(F32), gates[1][:, here].astype(F32))
    up = jnp.where(first, ups[0][:, here].astype(F32), ups[1][:, here].astype(F32))
    grad_act = dot_t(grad, down[here, :])
    sig = 1.0 / (1.0 + jnp.exp(-gate))
    grad_gate = (grad_act * up * sig * (1.0 + gate * (1.0 - sig))).astype(BF16)
    return (grad_gate, (grad_act * gate * sig).astype(BF16))


def middle_part(first, grad, middles, total_two, spread, gains):
    grad_two = dot_t(total_two.astype(BF16), spread)
    middle = jnp.where(first, middles[0][...], middles[1][...])
    through, gain = scaled_backward(middle, gains[1:2], grad_two)
    return (grad.astype(F32) + through, gain)


def mlp_backward_kernel(
    flag_ref, grad_ref, middle_a_ref, middle_b_ref, gate_a_ref, gate_b_ref, up_a_ref, up_b_ref,
    mat_ref, down_ref, spread_ref, gains_ref,
    grad_gate_ref, grad_up_ref, grad_middle_ref, gain_ref,
):
    first = flag_ref[0] == 1
    grad = grad_ref[...]
    total_two = 0
    for start in range(0, FF, PART):
        here = slice(start, start + PART)
        grad_gate, grad_up = gate_grads_part(
            first, grad, (gate_a_ref, gate_b_ref), (up_a_ref, up_b_ref), down_ref, here
        )
        grad_gate_ref[:, here] = grad_gate
        grad_up_ref[:, here] = grad_up
        total_two += dot_t(grad_gate, mat_ref[:, here])
        total_two += dot_t(grad_up, mat_ref[:, FF + start : FF + start + PART])
    grad_middle_ref[...], gain_ref[...] = middle_part(
        first, grad, (middle_a_ref, middle_b_ref), total_two, spread_ref[...], gains_ref[...]
    )


def mlp_backward(flags, grad, middles, gates, ups, gate_up_mat, down_mat, spread, gains):
    length = grad.shape[0]
    outs = [((length, FF), BF16), ((length, FF), BF16), ((length, D), F32), ((1, D), F32)]
    cost = (2 * length * N_DP * PAD * 7680, 22000000, length * FF)
    return local_call(
        mlp_backward_kernel, outs, cost,
        flags, grad, *middles, *gates, *ups, gate_up_mat, down_mat, spread, gains,
    )


def gate_grads_kernel(
    flag_ref, grad_ref, gate_a_ref, gate_b_ref, up_a_ref, up_b_ref, down_ref, grad_gate_ref, grad_up_ref
):
    first = flag_ref[0] == 1
    for start in range(0, FF, PART):
        here = slice(start, start + PART)
        grad_gate_ref[:, here], grad_up_ref[:, here] = gate_grads_part(
            first, grad_ref[...], (gate_a_ref, gate_b_ref), (up_a_ref, up_b_ref), down_ref, here
        )


def gate_grads(flags, grad, gates, ups, down_mat):
    length = grad.shape[0]
    outs = [((length, FF), BF16), ((length, FF), BF16)]
    cost = (2 * length * D * FF, 9000000, length * FF)
    return local_call(gate_grads_kernel, outs, cost, flags, grad, *gates, *ups, down_mat)


def middle_grad_kernel(
    flag_ref, grad_ref, middle_a_ref, middle_b_ref, grad_gate_ref, grad_up_ref,
    mat_ref, spread_ref, gains_ref, grad_middle_ref, gain_ref,
):
    total_two = dot_t(grad_gate_ref[...], mat_ref[:, :FF]) + dot_t(grad_up_ref[...], mat_ref[:, FF:])
    grad_middle_ref[...], gain_ref[...] = middle_part(
        flag_ref[0] == 1, grad_ref[...], (middle_a_ref, middle_b_ref), total_two, spread_ref[...],
        gains_ref[...],
    )


def middle_grad(flags, grad, middles, grad_gate, grad_up, gate_up_mat, spread, gains):
    length = grad.shape[0]
    outs = [((length, D), F32), ((1, D), F32)]
    cost = (2 * length * N_DP * PAD * 5120, 14000000, 0)
    return local_call(
        middle_grad_kernel, outs, cost,
        flags, grad, *middles, grad_gate, grad_up, gate_up_mat, spread, gains,
    )


def attend_backward_kernel(
    flag_ref, grad_ref, own_ref, got_ref, heads_a_ref, heads_b_ref, mask_ref, spread_ref, mat_ref,
    gains_ref, cosine_ref, sine_ref, grad_proj_ref, grad_attn_ref, grad_in_ref, gain_ref,
):
    first = flag_ref[0] == 1
    spread = spread_ref[...]
    grad_middle = grad_ref[...]
    grad_attn = grad_middle.astype(BF16)
    length = grad_middle.shape[0]
    grad_attn_ref[:, :D] = grad_attn
    grad_attn_ref[:, D:] = jnp.zeros((length, OUT_PAD - D), BF16)
    grad_mixed = dot_t(grad_attn, mat_ref[:, QKV_PAD : QKV_PAD + D]).astype(BF16)
    grad_mixed = dot_t(grad_mixed, spread)
    heads = jnp.where(first, heads_a_ref[...].astype(F32), heads_b_ref[...].astype(F32))
    mask = jnp.concatenate([mask_ref[flag_ref[1]]] * (H // KV), 0)
    grad_queries, grad_keys, grad_values = [], [], []
    for group in range(KV):
        queries = group_rows(heads, group)
        keys = head_columns(heads, H + group).astype(BF16)
        values = head_columns(heads, H + KV + group).astype(BF16)
        mixed = group_rows(grad_mixed, group)
        probs = probabilities(queries, keys, mask)
        grad_probs = dot_t(mixed, values)
        grad_scores = probs * (grad_probs - jnp.sum(grad_probs * probs, axis=-1, keepdims=True))
        grad_scores = grad_scores.astype(BF16)
        queries_part = dot(grad_scores, keys) * SCALE
        grad_queries += [queries_part[j * length : j * length + length] for j in range(H // KV)]
        grad_keys.append(across(grad_scores, queries) * SCALE)
        grad_values.append(across(probs.astype(BF16), mixed))
    turned = jnp.concatenate(grad_queries + grad_keys, 1).astype(BF16).astype(F32)
    tiles = turn_heads(turned, cosine_ref[...], -sine_ref[...])
    blank = jnp.zeros((length, QKV_PAD - QKV), F32)
    grad_proj = jnp.concatenate(tiles + grad_values + [blank], 1).astype(BF16)
    grad_proj_ref[...] = grad_proj
    grad_one = dot_t(grad_proj, mat_ref[:, :QKV_PAD]).astype(BF16)
    grad_one = dot_t(grad_one, spread)
    stream = jnp.where(first, own_ref[flag_ref[1]].astype(F32), got_ref[...].astype(F32))
    through, gain = scaled_backward(stream, gains_ref[0:1], grad_one)
    grad_in_ref[...] = (grad_middle + through).astype(BF16)
    gain_ref[...] = gain


def attend_backward(flags, grad, inputs, got, heads, masks, spread, mat, gains, cosine, sine):
    length = grad.shape[0]
    wide = N_DP * PAD
    outs = [
        ((length, QKV_PAD), BF16),
        ((length, OUT_PAD), BF16),
        ((length, D), BF16),
        ((1, D), F32),
    ]
    cost = (2 * length * wide * 6700, 9000000, H * length * length)
    return local_call(
        attend_backward_kernel, outs, cost,
        flags, grad, inputs, got, *heads, masks, spread, mat, gains, cosine, sine,
    )

def as_blocks(rows):
    return rows.reshape(N_DP // 2, -1, rows.shape[-1])


def per_device(
    inputs, segment_ids, qkv_weight, out_weight, gate_up_weight, down_weight, norm_gains, cotangent
):
    batches = inputs.shape[0]
    is_first = lax.axis_index("section") == 0
    order = block_order()
    spread = placement(order)
    attn_shard = jnp.concatenate(
        [
            qkv_weight[0],
            norm_gains[0],
            jnp.zeros((ROWS, QKV_PAD - QKV - 2), BF16),
            out_weight[0],
            jnp.zeros((ROWS, OUT_PAD - D), BF16),
        ],
        1,
    )
    widths = (QKV_PAD + OUT_PAD, 2 * FF)
    down_shard = jnp.pad(down_weight[0], ((0, 0), (0, OUT_PAD - D))).reshape(PAD, -1)
    rows = jnp.concatenate(
        [
            jnp.pad(attn_shard, ((0, 1), (0, 0))),
            jnp.pad(gate_up_weight[0], ((0, 1), (0, 0))),
            down_shard,
        ],
        1,
    )
    near = gather_near(rows)
    near_attn = near[:, :, : widths[0]]
    near_gate_up = near[:, :, widths[0] : widths[0] + widths[1]]
    near_down = near[:, :, widths[0] + widths[1] :].reshape(8, FROWS, OUT_PAD)[:, :, :D]
    gate_up_flow = Flow(gather_far(near_gate_up))
    attn_flow = Flow(gather_far(after(near_attn, near_gate_up)))
    spread = step([attn_flow], spread)
    spread, near_down = step([gate_up_flow], (spread, near_down))
    down_flow = Flow(gather_far(near_down))
    for group in ([attn_flow], [gate_up_flow], [down_flow], [down_flow]):
        spread = step(group, spread)
    attn_mat, gate_up_mat, down_mat = attn_flow.result, gate_up_flow.result, down_flow.result
    gain_rows = jnp.concatenate([piece[:, :, QKV : QKV + 2] for piece in attn_mat], 0)
    gain_rows = gain_rows.reshape(N_DP * PAD, 2)
    attn_mat = assemble(attn_mat)
    gate_up_mat = assemble(gate_up_mat)
    down_mat = reorder(jnp.concatenate(down_mat, 0), order, True).reshape(FF, D)
    gains_full = lax.dot_general(
        gain_rows, spread, (((0,), (1,)), ((), ())), preferred_element_type=F32
    )
    length = inputs.shape[1]
    cosine, sine = rope_tables(length)
    positions = jnp.arange(length)
    masks = (
        (segment_ids[:, :, None] == segment_ids[:, None, :])
        & (positions[:, None] >= positions[None, :])[None]
    ).astype(F32)
    first = is_first.astype(jnp.int32)

    def flags(for_first, for_second):
        return jnp.stack([first, jnp.where(is_first, for_first, for_second)])

    received = jnp.zeros(inputs.shape[1:], BF16)
    saved = []
    produced = []
    arrivals = []
    for turn in range(batches + 1):
        arrivals.append(received)
        hidden, heads, mixed, middle, second = attend_forward(
            flags(min(turn, batches - 1), max(turn - 1, 0)),
            inputs, received, masks, spread, attn_mat, gains_full, cosine, sine,
        )
        gate, up, act, layer_out = mlp_forward(
            flags(0, 0), second, middle, gate_up_mat, down_mat
        )
        saved.append((hidden, heads, mixed, middle, second, gate, up, act))
        produced.append(layer_out)
        if turn < batches:
            received = shifted(layer_out, "section", 1)
    section_outputs = jnp.stack(
        [
            jnp.where(is_first, produced[position], produced[position + 1])
            for position in range(batches)
        ]
    )[None]
    received = jnp.zeros(inputs.shape[1:], BF16)
    places = jnp.sum(
        jnp.where(order[:, None] == jnp.arange(N_DP)[None, :], jnp.arange(N_DP)[:, None], 0), 0
    ).astype(jnp.int32)

    def lefts(member):
        return jnp.concatenate(
            [jnp.where(is_first, saved[b][member], saved[b + 1][member]) for b in range(batches)], 0
        )

    def rights(turns):
        return jnp.concatenate(
            [jnp.where(is_first, turns[b + 1], turns[b]) for b in range(batches)], 0
        )

    returned = []
    downs = []
    gates = []
    ups = []
    projs = []
    attns = []
    gain_sum = 0
    flows = {}
    gate_up_own = []
    attn_own = []
    for turn in range(batches + 1):
        last = turn == batches
        if turn < batches:
            own_grad = cotangent[turn]
        else:
            own_grad = jnp.zeros(inputs.shape[1:], BF16)
        grad_out = jnp.where(is_first, received, own_grad)
        downs.append(grad_out)
        kept_first, kept_second = saved[max(turn - 1, 0)], saved[min(turn + 1, batches)]
        chosen = flags(max(turn - 1, 0), min(turn, batches - 1))

        def both(member):
            return (kept_first[member], kept_second[member])

        if not last:
            grad_gate, grad_up, grad_middle, gain_two = mlp_backward(
                chosen, grad_out, both(3), both(5), both(6), gate_up_mat, down_mat, spread, gains_full
            )
            gates.append(grad_gate)
            ups.append(grad_up)
        else:
            grad_gate, grad_up = gate_grads(chosen, grad_out, both(5), both(6), down_mat)
            gates.append(grad_gate)
            ups.append(grad_up)
            terms = (lefts(4), rights(gates), rights(ups))
            other = gate_up_sums(*terms, 1)
            flows["gate_up"] = Flow(
                full_scatter(as_blocks(other), lambda: as_blocks(gate_up_own[0]))
            )
            down_own, down_other = down_sums(lefts(7), after(rights(downs), other), places)
            flows["down"] = Flow(full_scatter(down_other, lambda: down_own))
            gate_up_own.append(gate_up_sums(*after(terms, down_other), 0))
            grad_gate, grad_up = after((grad_gate, grad_up), gate_up_own[0])
            grad_middle, gain_two = middle_grad(
                chosen, grad_out, both(3), grad_gate, grad_up, gate_up_mat, spread, gains_full
            )
        grad_proj, grad_attn, grad_in, gain_one = attend_backward(
            chosen, grad_middle, inputs, arrivals[min(turn + 1, batches)], both(1), masks, spread,
            attn_mat, gains_full, cosine, sine,
        )
        if last:
            grad_proj = step([flows["gate_up"], flows["down"]], grad_proj)
        projs.append(grad_proj)
        attns.append(grad_attn)
        gain_sum = gain_sum + jnp.concatenate([gain_one, gain_two], 0)
        returned.append(grad_in)
        if turn < batches:
            received = shifted(grad_in, "section", -1)
    section_input_grads = jnp.stack(
        [
            jnp.where(is_first, returned[position + 1], returned[position])
            for position in range(batches)
        ]
    )[None]
    gain_high = gain_sum.astype(BF16)
    gain_low = (gain_sum - gain_high.astype(F32)).astype(BF16)
    gain_rows = lax.dot_general(
        spread, jnp.stack([gain_high, gain_low]), (((0,), (2,)), ((), ())), preferred_element_type=F32
    )
    first_lane = QKV - (QKV_PAD - LANES)
    gain_rows = jnp.pad(
        gain_rows[:, 0] + gain_rows[:, 1], ((0, 0), (first_lane, LANES - first_lane - 2))
    )
    terms = (lefts(0), lefts(2), rights(projs), rights(attns), gain_rows)
    other = attn_sums(*terms, 1)
    flows["attn"] = Flow(full_scatter(as_blocks(other), lambda: as_blocks(attn_own[0])))
    attn_own.append(attn_sums(*after(terms, other), 0))
    down_flow, gate_up_flow, attn_flow = flows["down"], flows["gate_up"], flows["attn"]
    waiting = after(section_outputs, attn_own[0])
    for group in (
        [gate_up_flow],
        [down_flow],
        [attn_flow],
        [down_flow],
        [attn_flow],
        [down_flow],
        [gate_up_flow],
        [down_flow],
        [attn_flow],
        [gate_up_flow],
        [attn_flow],
        [gate_up_flow],
        [attn_flow],
    ):
        waiting = step(group, waiting)
    section_outputs = waiting
    while min(flow.result is not None for flow in (down_flow, gate_up_flow, attn_flow)) == 0:
        waiting = step([down_flow, gate_up_flow, attn_flow], waiting)
    section_outputs = waiting
    down_grad, gate_up_grad, attn_grad = down_flow.result, gate_up_flow.result, attn_flow.result
    return (
        section_outputs,
        section_input_grads,
        attn_grad[None, :ROWS, :QKV],
        attn_grad[None, :ROWS, QKV_PAD : QKV_PAD + D],
        gate_up_grad[None, :ROWS],
        down_grad[None],
        attn_grad[None, :ROWS, QKV : QKV + 2],
    )


def solution(mesh):
    in_specs = (
        P(None, "dp", None),
        P(None, "dp"),
        P("section", "dp", None),
        P("section", "dp", None),
        P("section", "dp", None),
        P("section", "dp", None),
        P("section", "dp", None),
        P(None, "dp", None),
    )
    out_specs = (
        P("section", None, "dp", None),
        P("section", None, "dp", None),
        P("section", "dp", None),
        P("section", "dp", None),
        P("section", "dp", None),
        P("section", "dp", None),
        P("section", "dp", None),
    )
    return jax.shard_map(
        per_device, mesh=mesh, in_specs=in_specs, out_specs=out_specs, check_vma=False
    )
```
